128 devices in a mesh: dp: 16 (over z, x), row: 2 (over core), col: 4 (over y).
Axes of the slice: x: 4, y: 4, z: 4, core: 2. Of those that a mesh axis runs over, the one named last changes fastest.
Arguments:
- layer_input: bfloat16 [16384, 1536], P(('dp', 'col'), 'row'), may hold values from -6 to 6
- prefix: int32 [16], P('dp'), may hold values from 102 to 512
- gain_one: bfloat16 [1536], P('row'), may hold values from 0.5 to 1.5
- w_query: bfloat16 [1536, 1536], P('row', 'col'), may hold values from -0.15625 to 0.15625
- b_query: bfloat16 [1536], P('col'), may hold values from -1 to 1
- w_keyval: bfloat16 [1536, 512], P('row'), may hold values from -0.15625 to 0.15625
- b_keyval: bfloat16 [512], replicated, may hold values from -1 to 1
- w_out: bfloat16 [1536, 1536], P('col', 'row'), may hold values from -0.625 to 0.625
- gain_two: bfloat16 [1536], P('row'), may hold values from 0.5 to 1.5
- w_gate: bfloat16 [1536, 8960], P('row', 'col'), may hold values from -0.15625 to 0.15625
- w_up: bfloat16 [1536, 8960], P('row', 'col'), may hold values from -0.15625 to 0.15625
- w_down: bfloat16 [8960, 1536], P('col', 'row'), may hold values from -0.0625 to 0.0625
- cotangent: bfloat16 [16384, 1536], P(('dp', 'col'), 'row'), may hold values from -6 to 6
Outputs:
- output: bfloat16 [16384, 1536], P(('dp', 'col'), 'row')
- grad_input: float32 [16384, 1536], P(('dp', 'col'), 'row')
- grad_gain_one: float32 [1536], P('row')
- grad_w_query: float32 [1536, 1536], P('row', 'col')
- grad_b_query: float32 [1536], P('col')
- grad_w_keyval: float32 [1536, 512], P('row')
- grad_b_keyval: float32 [512], replicated
- grad_w_out: float32 [1536, 1536], P('col', 'row')
- grad_gain_two: float32 [1536], P('row')
- grad_w_gate: float32 [1536, 8960], P('row', 'col')
- grad_w_up: float32 [1536, 8960], P('row', 'col')
- grad_w_down: float32 [8960, 1536], P('col', 'row')
The draws below stay inside these ranges and needn't reach their ends.
Inputs may be any that keep to these rules, and one draw needn't show every extreme that they name: `prefix`: each sequence's count of leading tokens that attend in both directions.
All inputs are finite; a program needn't handle non-finite values.
Results may differ from the reference program's by a relative error of at most 0.02.
Values may be sent and summed in bfloat16 or wider, within the bound.
No kernel may reach another device: no remote copies, remote signals or barrier semaphores. Data moves between devices by JAX's collectives and lax.ppermute only.
A program may use at most 192 MiB of HBM per device.

```python
import jax
import jax.numpy as jnp
from jax import lax

D = 1536
FF = 8960
QH = 12
KVH = 2
HD = 128
SEQ_LEN = 1024
NSEQ = 16
TOKENS = 16384


def set_ends(values, own_key, least, largest):
    longest = values.shape.index(max(values.shape))
    spots = []
    for shift in (0, 1):
        where = [jax.random.randint(jax.random.fold_in(own_key, axis), (), 0, length) for axis, length in enumerate(values.shape)]
        where[longest] = (where[longest] + shift) % values.shape[longest]
        spots.append(tuple(where))
    return values.at[spots[0]].set(least).at[spots[1]].set(largest)


def block_levels(stream_key, shape, cuts, least, high):
    def one(axis_at, shards_of):
        steps = jax.random.uniform(jax.random.fold_in(jax.random.fold_in(stream_key, 6), axis_at), (shards_of,), jnp.float32, least / len(cuts), high / len(cuts))
        return jnp.repeat(jnp.exp(steps), shape[axis_at] // shards_of).reshape((-1,) + (1,) * (len(shape) - axis_at - 1))

    factor_of = one(*cuts[0])
    for cut in cuts[1:]:
        factor_of = factor_of * one(*cut)
    return factor_of


def bell_draw(stream_key, dims, spread, most, shards=(), kind=jnp.bfloat16):
    factor_of = block_levels(stream_key, dims, shards, -0.22, 0.18) if shards else 1.0
    values = jax.random.normal(stream_key, dims, jnp.float32) * spread * factor_of
    return jnp.minimum(jnp.maximum(values, -most), most).astype(kind)


def setup_inputs(seed: int = 0) -> dict:
    seeds = jax.random.split(jax.random.key(seed), 14)
    layer_input = bell_draw(seeds[0], (TOKENS, D), 1.0, 6.0, ((0, 64), (1, 2)))
    prefix = set_ends(jax.random.randint(seeds[1], (NSEQ,), max(1, SEQ_LEN // 10), SEQ_LEN // 2 + 1), jax.random.fold_in(seeds[1], 1), max(1, SEQ_LEN // 10), (SEQ_LEN // 2 + 1) - 1).astype(jnp.int32)
    gain_one = jnp.clip(1.0 + 0.1 * jax.random.normal(seeds[2], (D,), jnp.float32), 0.5, 1.5).astype(jnp.bfloat16)
    w_query = bell_draw(seeds[3], (D, QH * HD), D ** -0.5, 0.15625, ((0, 2), (1, 4)))
    b_query = bell_draw(seeds[4], (QH * HD,), 0.2, 1.0, ((0, 4),))
    w_keyval = bell_draw(seeds[5], (D, 2 * KVH * HD), D ** -0.5, 0.15625, ((0, 2),))
    b_keyval = bell_draw(seeds[6], (2 * KVH * HD,), 0.2, 1.0)
    w_out = bell_draw(seeds[7], (QH * HD, D), (max(1, QH * HD // 16)) ** -0.5, 0.625, ((0, 4), (1, 2)))
    gain_two = jnp.clip(1.0 + 0.1 * jax.random.normal(seeds[8], (D,), jnp.float32), 0.5, 1.5).astype(jnp.bfloat16)
    w_gate = bell_draw(seeds[9], (D, FF), D ** -0.5, 0.15625, ((0, 2), (1, 4)))
    w_up = bell_draw(seeds[10], (D, FF), D ** -0.5, 0.15625, ((0, 2), (1, 4)))
    w_down = bell_draw(seeds[11], (FF, D), FF ** -0.5, 0.0625, ((0, 4), (1, 2)))
    cotangent = bell_draw(seeds[12], (TOKENS, D), 1.0, 6.0, ((0, 64), (1, 2)))
    return dict(layer_input=layer_input, prefix=prefix, gain_one=gain_one, w_query=w_query, b_query=b_query, w_keyval=w_keyval, b_keyval=b_keyval, w_out=w_out, gain_two=gain_two, w_gate=w_gate, w_up=w_up, w_down=w_down, cotangent=cotangent)


@jax.custom_vjp
def low(v):
    return lax.optimization_barrier(v.astype(jnp.bfloat16)).astype(jnp.float32)

@jax.custom_vjp
def low_back(v):
    return v

def low_keep(v):
    return (low(v), None)

def low_pass(kept, grad):
    return (grad,)

def back_keep(v):
    return (v, None)

def back_low(kept, grad):
    return (low(grad),)
low.defvjp(low_keep, low_pass)
low_back.defvjp(back_keep, back_low)
EPS = 1e-06
THETA = 1000000.0
NEG = -1e+30
HIGHEST_PRECISION = lax.Precision.HIGHEST

def matmul(left, right):
    return jnp.dot(left, right, precision=HIGHEST_PRECISION)

def tables(length):
    position = jnp.arange(length, dtype=jnp.float32)
    frequency = THETA ** (-jnp.arange(0, HD // 2, dtype=jnp.float32) * 2.0 / HD)
    angle = position[:, None] * frequency[None, :]
    return (jnp.cos(angle)[:, None], jnp.sin(angle)[:, None])

def rotate(value, cosine, sine):
    middle = value.shape[-1] // 2
    first = value[..., :middle]
    second = value[..., middle:]
    return jnp.concatenate([first * cosine - second * sine, second * cosine + first * sine], axis=-1)

def rms_scale(value, gain):
    return value * lax.rsqrt(lax.optimization_barrier(jnp.mean(value * value, axis=-1, keepdims=True)) + EPS) * gain

def forward(layer_input, gain_one, w_query, b_query, w_keyval, b_keyval, w_out, gain_two, w_gate, w_up, w_down, bound):
    length = layer_input.shape[0]
    cosine, sine = tables(length)
    normed_one = low(rms_scale(layer_input, gain_one))
    query = low_back(matmul(normed_one, w_query)) + b_query
    keyval = low_back(matmul(normed_one, w_keyval)) + b_keyval
    query = low(rotate(query.reshape(length, QH, HD), cosine, sine)).reshape(length, KVH, QH // KVH, HD)
    key = low(rotate(keyval[:, :KVH * HD].reshape(length, KVH, HD), cosine, sine))
    value = low(keyval[:, KVH * HD:].reshape(length, KVH, HD))
    scores = low_back(jnp.einsum('qkgd,pkd->kgqp', query, key, precision=HIGHEST_PRECISION) * HD ** (-0.5))
    position = jnp.arange(length, dtype=jnp.int32)
    visible = (position[None, :] <= position[:, None]) | (position[None, :] < bound)
    weights = jax.nn.softmax(jnp.where(visible, scores, NEG), axis=-1)
    attended = jnp.einsum('kgqp,pkd->qkgd', low(weights), value, precision=HIGHEST_PRECISION).reshape(length, QH * HD)
    attended = low(low_back(attended))
    resid = layer_input + low_back(matmul(attended, w_out))
    normed_two = low(rms_scale(resid, gain_two))
    gate = low_back(matmul(normed_two, w_gate))
    up_part = low_back(matmul(normed_two, w_up))
    mixed = low(jax.nn.silu(gate) * up_part)
    return resid + matmul(mixed, w_down)

def reference(layer_input, prefix, gain_one, w_query, b_query, w_keyval, b_keyval, w_out, gain_two, w_gate, w_up, w_down, cotangent):
    params = tuple((weight.astype(jnp.float32) for weight in (gain_one, w_query, b_query, w_keyval, b_keyval, w_out, gain_two, w_gate, w_up, w_down)))
    inputs = layer_input.astype(jnp.float32).reshape(NSEQ, SEQ_LEN, D)
    cotangents = cotangent.astype(jnp.float32).reshape(NSEQ, SEQ_LEN, D)

    def step(total, item):
        sequence, grad_out, bound = item

        def apply(value, *weights):
            return forward(value, *weights, bound)
        result, pull = jax.vjp(apply, sequence, *params)
        grads = pull(grad_out)
        total = tuple((left + right for left, right in zip(total, grads[1:])))
        return (total, (result, grads[0]))
    zeros = tuple((jnp.zeros_like(weight) for weight in params))
    total, (results, grad_inputs) = lax.scan(step, zeros, (inputs, cotangents, prefix))
    output = results.reshape(NSEQ * SEQ_LEN, D).astype(jnp.bfloat16)
    grad_input = grad_inputs.reshape(NSEQ * SEQ_LEN, D)
    return (output, grad_input, total[0], total[1], total[2], total[3], total[4], total[5], total[6], total[7], total[8], total[9])
```

```python
import jax
import jax.numpy as jnp
from jax import lax
from jax.sharding import PartitionSpec as P

HD = 128
SEQ_LEN = 1024
LANES = 128

EPS = 1e-06
THETA = 1000000.0
NEG = -1e30
BF16 = jnp.bfloat16
F32 = jnp.float32
CONTRACT = (((1,), (1,)), ((), ()))
TOKENS = (((0,), (0,)), ((), ()))


def mm(left, right):
    return jnp.dot(left, right, preferred_element_type=F32)


def mm_nt(left, right):
    return lax.dot_general(left, right, CONTRACT, preferred_element_type=F32)


def mm_tn(left, right):
    return lax.dot_general(left, right, TOKENS, preferred_element_type=F32)


def swap_rows(value):
    return lax.ppermute(value, "row", [(0, 1), (1, 0)])


def from_col(value, offset):
    count = lax.axis_size("col")
    return lax.ppermute(value, "col", [((i + offset) % count, i) for i in range(count)])


def gather_col(value):
    count = lax.axis_size("col")
    order = [j for j in (1, count - 1) if j != 0] + list(range(2, count - 1))
    blocks = {0: value}
    for j in order:
        blocks[j] = from_col(value, j)
    return [blocks[j] for j in range(count)]


def scatter_col(blocks):
    count = lax.axis_size("col")
    order = [1, count - 1] + list(range(2, count - 1))
    got = {j: from_col(blocks[j].astype(BF16), -j) for j in order}
    total = blocks[0].astype(F32)
    for j in range(1, count):
        total = total + got[j].astype(F32)
    return total


def halves(value):
    middle = value.shape[-1] // 2
    return value[..., :middle], value[..., middle:]


def turn(value):
    first, second = halves(value)
    return jnp.concatenate([second, first], axis=-1)


def rotate(value, cosine, sine):
    first, second = halves(value)
    return jnp.concatenate(
        [first * cosine - second * sine, second * cosine + first * sine], axis=-1
    )


def unrotate(grad, cosine, sine):
    first, second = halves(grad)
    return jnp.concatenate(
        [first * cosine + second * sine, second * cosine - first * sine], axis=-1
    )


def roll_blocks(value, shift, axis):
    size = value.shape[axis]
    twice = jnp.concatenate([value, value], axis=axis)
    return lax.dynamic_slice_in_dim(twice, shift, size, axis)


def shift_dp(value, along, offset, side):
    pairs = []
    for z in range(side):
        for x in range(side):
            if along == "z":
                source = ((z + offset) % side) * side + x
            else:
                source = z * side + (x + offset) % side
            pairs.append((source, z * side + x))
    return lax.ppermute(value, "dp", pairs)


def scatter_dp(blocks, along, side):
    total = blocks[0].astype(F32)
    got = [shift_dp(blocks[j], along, -j, side) for j in range(1, side)]
    for part in got:
        total = total + part.astype(F32)
    return total.astype(BF16)


def gather_dp(value, along, side):
    return jnp.stack([value] + [shift_dp(value, along, j, side) for j in range(1, side)])


def body(
    layer_input,
    prefix,
    gain_one,
    w_query,
    b_query,
    w_keyval,
    b_keyval,
    w_out,
    gain_two,
    w_gate,
    w_up,
    w_down,
    cotangent,
):
    cols = lax.axis_size("col")
    groups = lax.axis_size("dp")
    side = int(round(groups**0.5))
    r = lax.axis_index("row")
    c = lax.axis_index("col")
    dp = lax.axis_index("dp")
    rows_in, feat = layer_input.shape
    own = rows_in // 2
    tokens = own * cols
    width = 2 * feat
    qw = w_query.shape[1]
    heads = qw // HD
    kvw = w_keyval.shape[1] // 2
    share = cols // (kvw // HD)
    kv_head = c // share
    scaling = HD ** (-0.5)
    ff = w_gate.shape[1]
    part = -(-ff // (2 * LANES)) * LANES
    keep_at = r * part
    send_at = (1 - r) * part

    def split_in(weight):
        padded = jnp.pad(weight, ((0, 0), (0, 2 * part - ff)))
        kept = lax.dynamic_slice_in_dim(padded, keep_at, part, 1)
        sent = lax.dynamic_slice_in_dim(padded, send_at, part, 1)
        return jnp.concatenate([kept, swap_rows(sent)], axis=0)

    x_blocks = gather_col(layer_input)

    key_start = kv_head * HD
    w_own = jnp.concatenate(
        [
            lax.dynamic_slice_in_dim(w_keyval, key_start, HD, 1),
            lax.dynamic_slice_in_dim(w_keyval, kvw + key_start, HD, 1),
        ],
        axis=1,
    )
    b_own = jnp.concatenate(
        [
            lax.dynamic_slice_in_dim(b_keyval, key_start, HD, 0),
            lax.dynamic_slice_in_dim(b_keyval, kvw + key_start, HD, 0),
        ]
    ).astype(F32)
    w_qkv_own = jnp.concatenate([w_query, w_own], axis=1)
    w_qkv = jnp.concatenate([w_qkv_own, swap_rows(w_qkv_own)], axis=0)
    gains_own = jnp.stack([gain_one, gain_two])
    gains = jnp.concatenate([gains_own, swap_rows(gains_own)], axis=1).astype(F32)
    gain_one_f, gain_two_f = gains[0], gains[1]

    block_first = rows_in * ((c + jnp.arange(cols, dtype=jnp.int32)) % cols)
    inside = jnp.arange(own, dtype=jnp.int32)
    pos_own = ((block_first[:, None] + own * r + inside[None]) % SEQ_LEN).reshape(-1)
    pos_other = ((block_first[:, None] + own * (1 - r) + inside[None]) % SEQ_LEN).reshape(-1)
    frequency = THETA ** (-jnp.arange(0, HD // 2, dtype=F32) * 2.0 / HD)
    angle = pos_own.astype(F32)[:, None] * frequency[None, :]
    cosine, sine = jnp.cos(angle), jnp.sin(angle)
    cos_h, sin_h = cosine[:, None], sine[:, None]

    def split_tokens(blocks):
        stacked = jnp.stack(blocks)
        mine = lax.dynamic_slice_in_dim(stacked, own * r, own, 1)
        theirs = lax.dynamic_slice_in_dim(stacked, own * (1 - r), own, 1)
        return mine.reshape(tokens, feat), theirs.reshape(tokens, feat)

    x_mine, x_theirs = split_tokens(x_blocks)
    x_full = jnp.concatenate([x_mine, swap_rows(x_theirs)], axis=1).astype(F32)
    inverse_one = lax.rsqrt(jnp.mean(x_full * x_full, axis=1, keepdims=True) + EPS)
    normed_one = (x_full * inverse_one * gain_one_f).astype(BF16)

    qkv = mm(normed_one, w_qkv)
    query = (qkv[:, :qw] + b_query.astype(F32)).reshape(tokens, heads, HD)
    query_in = rotate(query, cos_h, sin_h).astype(BF16)
    keyval = qkv[:, qw:] + b_own
    kv_mine = jnp.concatenate(
        [rotate(keyval[:, :HD], cosine, sine), keyval[:, HD:]], axis=1
    ).astype(BF16)
    kv_all = jnp.concatenate([kv_mine, swap_rows(kv_mine)], axis=0)
    keys, values = kv_all[:, :HD], kv_all[:, HD:]
    key_pos = jnp.concatenate([pos_own, pos_other])
    visible = (key_pos[None, :] <= pos_own[:, None]) | (key_pos[None, :] < prefix[0])
    scores = jnp.einsum("qhd,kd->hqk", query_in, keys, preferred_element_type=F32) * scaling
    scores = jnp.where(visible[None], scores, NEG)
    highest = jnp.max(scores, axis=2, keepdims=True)
    exponent = jnp.exp(scores - highest)
    weights = exponent / jnp.sum(exponent, axis=2, keepdims=True)
    weights_low = weights.astype(BF16)
    attended = (
        jnp.einsum("hqk,kd->qhd", weights_low, values, preferred_element_type=F32)
        .reshape(tokens, qw)
        .astype(BF16)
    )

    w_out_col = jnp.concatenate(gather_col(w_out), axis=0)
    w_out_full = jnp.concatenate([w_out_col, swap_rows(w_out_col)], axis=1)
    w_out_own = w_out_full[:qw]
    att_blocks = gather_col(attended)
    att_full = jnp.concatenate(
        [
            jnp.roll(block.reshape(cols, own, qw), j, axis=0).reshape(tokens, qw)
            for j, block in enumerate(att_blocks)
        ],
        axis=1,
    )
    resid = x_full + mm(att_full, w_out_full)
    inverse_two = lax.rsqrt(jnp.mean(resid * resid, axis=1, keepdims=True) + EPS)
    normed_two = (resid * inverse_two * gain_two_f).astype(BF16)
    normed_two_all = jnp.concatenate([normed_two, turn(swap_rows(normed_two))], axis=0)

    w_gate_part = split_in(w_gate)
    w_up_part = split_in(w_up)
    down_padded = jnp.pad(w_down, ((0, 2 * part - ff), (0, 0)))
    w_down_part = jnp.concatenate(
        [
            lax.dynamic_slice_in_dim(down_padded, keep_at, part, 0),
            swap_rows(lax.dynamic_slice_in_dim(down_padded, send_at, part, 0)),
        ],
        axis=1,
    )
    c_mine, c_theirs = split_tokens(gather_col(cotangent))
    cot_all = jnp.concatenate(
        [
            jnp.concatenate([c_mine, swap_rows(c_theirs)], axis=1),
            jnp.concatenate([c_theirs, swap_rows(c_mine)], axis=1),
        ],
        axis=0,
    )

    gate = mm(normed_two_all, w_gate_part)
    up_part = mm(normed_two_all, w_up_part)
    grad_mixed = mm_nt(cot_all, w_down_part)
    sigmoid = jax.nn.sigmoid(gate)
    mixed = (gate * sigmoid * up_part).astype(BF16)
    grad_gate = (grad_mixed * up_part * sigmoid * (1.0 + gate * (1.0 - sigmoid))).astype(BF16)
    grad_up = (grad_mixed * gate * sigmoid).astype(BF16)

    def weight_grad(left, right):
        return mm_tn(left, right).astype(BF16)

    cot_a, cot_b = halves(cot_all)
    n2_a, n2_b = halves(normed_two_all)
    big = (
        weight_grad(mixed, cot_a),
        swap_rows(weight_grad(mixed, cot_b)),
        weight_grad(n2_a, grad_gate),
        swap_rows(weight_grad(n2_b, grad_gate)),
        weight_grad(n2_a, grad_up),
        swap_rows(weight_grad(n2_b, grad_up)),
    )
    big = lax.psum(big, "dp")

    def sum_group(partial):
        mine = partial[:tokens] + turn(swap_rows(partial[tokens:].astype(BF16))).astype(F32)
        return scatter_col(mine.reshape(cols, own, width))

    grad_normed_two = sum_group(mm_nt(grad_gate, w_gate_part) + mm_nt(grad_up, w_up_part))
    down = sum_group(mm(mixed, w_down_part))

    def exchange_out(value):
        mine, other = halves(value)
        got = swap_rows(other)
        return jnp.where(
            r == 0,
            jnp.concatenate([mine, got], axis=0),
            jnp.concatenate([got, mine], axis=0),
        )

    output = exchange_out((resid[:own] + down).astype(BF16))

    def norm_backward(grad, value, inverse, gain):
        unit = value * inverse
        scaled = grad * gain
        mean_term = jnp.mean(scaled * unit, axis=1, keepdims=True)
        return inverse * (scaled - unit * mean_term), jnp.sum(grad * unit, axis=0)

    cot_full = cot_all.reshape(2, cols, own, width)[0, 0].astype(F32)
    grad_norm_two, grad_gain_two = norm_backward(
        grad_normed_two, resid[:own], inverse_two[:own], gain_two_f
    )
    grad_resid = cot_full + grad_norm_two
    resid_low = jnp.concatenate(gather_col(grad_resid.astype(BF16)), axis=0)

    grad_attended = mm_nt(resid_low, w_out_own).astype(BF16).reshape(tokens, heads, HD)
    grad_weights = jnp.einsum("qhd,kd->hqk", grad_attended, values, preferred_element_type=F32)
    inner = jnp.sum(weights * grad_weights, axis=2, keepdims=True)
    grad_scores = (weights * (grad_weights - inner)).astype(BF16)
    grad_query_rot = (
        jnp.einsum("hqk,kd->qhd", grad_scores, keys, preferred_element_type=F32) * scaling
    )
    grad_key_rot = (
        jnp.einsum("hqk,qhd->kd", grad_scores, query_in, preferred_element_type=F32) * scaling
    )
    grad_value = jnp.einsum("hqk,qhd->kd", weights_low, grad_attended, preferred_element_type=F32)
    grad_kv = jnp.concatenate([grad_key_rot, grad_value], axis=1)
    grad_kv = grad_kv[:tokens] + swap_rows(grad_kv[tokens:].astype(BF16)).astype(F32)
    grad_query = unrotate(grad_query_rot, cos_h, sin_h).reshape(tokens, qw)
    grad_keyval = jnp.concatenate(
        [unrotate(grad_kv[:, :HD], cosine, sine), grad_kv[:, HD:]], axis=1
    )
    grad_qkv = jnp.concatenate([grad_query, grad_keyval], axis=1)
    grad_b = jnp.sum(grad_qkv, axis=0)
    qkv_low = grad_qkv.astype(BF16)
    grad_normed_one = scatter_col(mm_nt(qkv_low, w_qkv).reshape(cols, own, width))

    def sum_cores(partial):
        mine, other = halves(partial)
        return mine + swap_rows(other.astype(BF16)).astype(F32)

    grad_wqkv = sum_cores(mm_tn(qkv_low, normed_one)).T
    grad_wout = sum_cores(mm_tn(attended, resid_low))
    wout_blocks = jnp.concatenate([grad_wout[:, : feat // 2], grad_wout[:, feat // 2 :]], axis=0)
    rest = jnp.concatenate([wout_blocks, grad_wqkv], axis=1).astype(BF16)

    z_at, x_at = dp // side, dp % side
    piece = feat // groups
    middle = rest.shape[1] // 2

    def blocks_of(value, first_at, second_at):
        value = value.reshape(side, side, piece, value.shape[1])
        return roll_blocks(roll_blocks(value, first_at, 0), second_at, 1)

    rest_a = blocks_of(rest[:, :middle], x_at, z_at)
    rest_b = blocks_of(rest[:, middle:], z_at, x_at)
    rest_a = scatter_dp(rest_a, "x", side)
    rest_b = scatter_dp(rest_b, "z", side)
    rest_a = scatter_dp(rest_a, "z", side)
    rest_b = scatter_dp(rest_b, "x", side)
    kv_piece = rest_b[:, -2 * HD :]
    kv_pieces = gather_col(kv_piece)
    kv_sums = []
    for head in range(kvw // HD):
        total = jnp.zeros(kv_piece.shape, F32)
        for j in range(cols):
            same = ((c + j) % cols) // share == head
            total = total + jnp.where(same, kv_pieces[j].astype(F32), 0.0)
        kv_sums.append(total.astype(BF16))
    kv_sum = jnp.concatenate(
        [s[:, :HD] for s in kv_sums] + [s[:, HD:] for s in kv_sums], axis=1
    )
    rest_b = jnp.concatenate([rest_b[:, : -2 * HD], kv_sum], axis=1)
    rest_a = gather_dp(gather_dp(rest_a, "z", side), "x", side)
    rest_b = gather_dp(gather_dp(rest_b, "x", side), "z", side)

    def back(value, second_at, first_at):
        value = roll_blocks(roll_blocks(value, (side - first_at) % side, 0), (side - second_at) % side, 1)
        return value.reshape(feat, value.shape[-1])

    rest_a = back(rest_a, z_at, x_at)
    rest_b = back(rest_b, x_at, z_at)
    rest_sum = jnp.concatenate([rest_a, rest_b], axis=1).astype(F32)
    grad_wout = jnp.concatenate([rest_sum[:qw, :qw], rest_sum[qw:, :qw]], axis=1)
    grad_wq = rest_sum[:, qw : 2 * qw]
    grad_wkv = rest_sum[:, 2 * qw :]

    grad_norm_one, grad_gain_one = norm_backward(
        grad_normed_one, x_full[:own], inverse_one[:own], gain_one_f
    )
    grad_input = exchange_out(grad_resid + grad_norm_one)

    gains_grad = jnp.stack([grad_gain_one, grad_gain_two])
    gains_abs = jnp.where(r == 0, gains_grad, turn(gains_grad))
    bias_query = lax.dynamic_update_slice_in_dim(
        jnp.zeros((qw * cols,), F32), grad_b[:qw], c * qw, 0
    )
    bias_kv = jnp.zeros((2 * kvw,), F32)
    bias_kv = lax.dynamic_update_slice_in_dim(bias_kv, grad_b[qw : qw + HD], key_start, 0)
    bias_kv = lax.dynamic_update_slice_in_dim(bias_kv, grad_b[qw + HD :], kvw + key_start, 0)
    small = jnp.concatenate([gains_abs.reshape(-1), bias_query, bias_kv])
    small = lax.psum(small, ("dp", "row", "col"))
    gains_sum = small[: 2 * width].reshape(2, width)
    gains_sum = lax.dynamic_slice_in_dim(gains_sum, r * feat, feat, 1)
    bias_query = lax.dynamic_slice_in_dim(small, 2 * width + c * qw, qw, 0)
    bias_kv = small[2 * width + cols * qw :]

    def join(kept, got, axis):
        both = jnp.where(
            r == 0,
            jnp.concatenate([kept, got], axis=axis),
            jnp.concatenate([got, kept], axis=axis),
        )
        return lax.slice_in_dim(both, 0, ff, axis=axis).astype(F32)

    return (
        output,
        grad_input,
        gains_sum[0],
        grad_wq,
        bias_query,
        grad_wkv,
        bias_kv,
        grad_wout,
        gains_sum[1],
        join(big[2], big[3], 1),
        join(big[4], big[5], 1),
        join(big[0], big[1], 0),
    )


def solution(mesh):
    return jax.shard_map(
        body,
        mesh=mesh,
        in_specs=(
            P(("dp", "col"), "row"),
            P("dp"),
            P("row"),
            P("row", "col"),
            P("col"),
            P("row", None),
            P(),
            P("col", "row"),
            P("row"),
            P("row", "col"),
            P("row", "col"),
            P("col", "row"),
            P(("dp", "col"), "row"),
        ),
        out_specs=(
            P(("dp", "col"), "row"),
            P(("dp", "col"), "row"),
            P("row"),
            P("row", "col"),
            P("col"),
            P("row", None),
            P(),
            P("col", "row"),
            P("row"),
            P("row", "col"),
            P("row", "col"),
            P("col", "row"),
        ),
        check_vma=False,
    )
```

```python
import functools

import jax
import jax.numpy as jnp
from jax import lax
from jax.experimental import pallas as pl
from jax.experimental.pallas import tpu as pltpu
from jax.sharding import PartitionSpec as P

HD = 128
SEQ_LEN = 1024
EPS = 1e-06
THETA = 1000000.0
NEG = -1e30
BF16 = jnp.bfloat16
F32 = jnp.float32
MIB = 1 << 20
SMALL_ROWS = 16


def dot_nn(left, right):
    return lax.dot_general(left, right, (((1,), (0,)), ((), ())), preferred_element_type=F32)


def dot_nt(left, right):
    return lax.dot_general(left, right, (((1,), (1,)), ((), ())), preferred_element_type=F32)


def dot_tn(left, right):
    return lax.dot_general(left, right, (((0,), (0,)), ((), ())), preferred_element_type=F32)


def params(mib):
    return pltpu.CompilerParams(vmem_limit_bytes=mib * MIB)


def cost(flops, nbytes):
    return pl.CostEstimate(flops=int(flops), bytes_accessed=int(nbytes), transcendentals=0)


def rope(value, cosine, sine):
    return value * cosine + pltpu.roll(value, HD // 2, 1) * sine


def qkv_kernel(cols, *refs):
    r_ref, refs = refs[0], refs[1:]
    xa, refs = refs[:cols], refs[cols:]
    xb, refs = refs[:cols], refs[cols:]
    gain, wa, wb, bias, cosine, sine, x_out, n_out, q_out, kv_out = refs
    own, feat = xa[0].shape
    for j in range(cols):
        rows = pl.ds(j * own, own)
        a = xa[j][...].astype(F32)
        b = xb[j][...].astype(F32)
        total = jnp.sum(a * a, axis=1, keepdims=True) + jnp.sum(b * b, axis=1, keepdims=True)
        inverse = lax.rsqrt(total / (2 * feat) + EPS)
        x_out[rows, :feat] = xa[j][...]
        x_out[rows, feat:] = xb[j][...]
        n_out[rows, :feat] = (a * inverse * gain[:, :feat]).astype(BF16)
        n_out[rows, feat:] = (b * inverse * gain[:, feat:]).astype(BF16)
    qkv = dot_nn(n_out[:, :feat], wa[...]) + dot_nn(n_out[:, feat:], wb[...]) + bias[...]
    qw = q_out.shape[1]
    for h in range(qw // HD):
        at = slice(h * HD, (h + 1) * HD)
        q_out[:, at] = rope(qkv[:, at], cosine[...], sine[...]).astype(BF16)
    kv_out[:, :HD] = rope(qkv[:, qw : qw + HD], cosine[...], sine[...]).astype(BF16)
    kv_out[:, HD:] = qkv[:, qw + HD :].astype(BF16)


def qkv_call(r, xa, xb, gain, wa, wb, bias, cosine, sine, qw):
    cols = len(xa)
    feat = xa[0].shape[1]
    own = xa[0].shape[0] // 2
    tokens = own * cols
    whole = lambda v: pl.BlockSpec(v.shape, lambda i, r: (0,) * v.ndim)
    rest = [gain, wa, wb, bias, cosine, sine]
    outs = [
        jax.ShapeDtypeStruct((tokens, 2 * feat), BF16),
        jax.ShapeDtypeStruct((tokens, 2 * feat), BF16),
        jax.ShapeDtypeStruct((tokens, qw), BF16),
        jax.ShapeDtypeStruct((tokens, 2 * HD), BF16),
    ]
    return pl.pallas_call(
        functools.partial(qkv_kernel, cols),
        grid_spec=pltpu.PrefetchScalarGridSpec(
            num_scalar_prefetch=1,
            grid=(1,),
            in_specs=[pl.BlockSpec((own, feat), lambda i, r: (r[0], 0))] * (2 * cols)
            + [whole(v) for v in rest],
            out_specs=[whole(o) for o in outs],
        ),
        out_shape=outs,
        compiler_params=params(40),
        cost_estimate=cost(4 * tokens * feat * wa.shape[1], 8e6),
        name="qkv",
    )(r, *xa, *xb, *rest)


def softmax(q, k, visible, scaling):
    scores = jnp.where(visible, dot_nt(q, k) * scaling, NEG)
    e = jnp.exp(scores - jnp.max(scores, axis=1, keepdims=True))
    return e * (1.0 / jnp.sum(e, axis=1, keepdims=True))


def visibility(qpos, kpos, prefix_ref):
    return (kpos <= qpos) | (kpos < prefix_ref[0])


def attend_kernel(scaling, prefix, q, kv_a, kv_b, qpos, kpos, out):
    visible = visibility(qpos[...], kpos[...], prefix)
    keys = jnp.concatenate([kv_a[:, :HD], kv_b[:, :HD]], axis=0)
    values = jnp.concatenate([kv_a[:, HD:], kv_b[:, HD:]], axis=0)
    for h in range(q.shape[1] // HD):
        at = slice(h * HD, (h + 1) * HD)
        weights = softmax(q[:, at], keys, visible, scaling)
        out[:, at] = dot_nn(weights.astype(BF16), values).astype(BF16)


def attend_call(prefix, q, kv_a, kv_b, qpos, kpos, block):
    tokens, qw = q.shape
    whole = lambda v: pl.BlockSpec(v.shape, lambda i, p: (0,) * v.ndim)
    part = lambda v: pl.BlockSpec((block, v.shape[1]), lambda i, p: (i, 0))
    return pl.pallas_call(
        functools.partial(attend_kernel, HD**-0.5),
        grid_spec=pltpu.PrefetchScalarGridSpec(
            num_scalar_prefetch=1,
            grid=(tokens // block,),
            in_specs=[part(q), whole(kv_a), whole(kv_b), part(qpos), whole(kpos)],
            out_specs=part(q),
        ),
        out_shape=jax.ShapeDtypeStruct(q.shape, BF16),
        compiler_params=params(32),
        cost_estimate=cost(16 * tokens * tokens * qw, 3e6),
        name="attend",
    )(prefix, q, kv_a, kv_b, qpos, kpos)


def out_kernel(cols, own, *refs):
    att, refs = refs[:cols], refs[cols:]
    wa, refs = refs[:cols], refs[cols:]
    wb, refs = refs[:cols], refs[cols:]
    xa, xb, gain, resid_out, na, nb, acc_a, acc_b = refs
    step, steps = pl.program_id(0), pl.num_programs(0)
    chunk = xa.shape[1]
    feat = chunk * steps

    rolled = []
    for j in range(cols):
        tiles = [att[j][((i - j) % cols) * own : ((i - j) % cols + 1) * own, :] for i in range(cols)]
        rolled.append(jnp.concatenate(tiles, axis=0))
    at = pl.ds(pl.multiple_of(step * chunk, 128), chunk)
    for x, w, acc in ((xa, wa, acc_a), (xb, wb, acc_b)):
        total = x[...].astype(F32)
        for j in range(cols):
            total = total + dot_nn(rolled[j], w[j][...])
        acc[:, at] = total

    @pl.when(step == steps - 1)
    def _():
        a, b = acc_a[...], acc_b[...]
        total = jnp.sum(a * a, axis=1, keepdims=True) + jnp.sum(b * b, axis=1, keepdims=True)
        inverse = lax.rsqrt(total / (2 * feat) + EPS)
        na[...] = (a * inverse * gain[:, :feat]).astype(BF16)
        nb[...] = (b * inverse * gain[:, feat:]).astype(BF16)
        resid_out[:, :feat] = acc_a[:own, :]
        resid_out[:, feat:] = acc_b[:own, :]


def out_call(att, wa, wb, x, gain, own):
    cols = len(att)
    tokens, qw = att[0].shape
    feat = wa[0].shape[1]
    steps = 3
    chunk = feat // steps
    whole = lambda v: pl.BlockSpec(v.shape, lambda i: (0,) * v.ndim)
    outs = [
        jax.ShapeDtypeStruct((own, 2 * feat), F32),
        jax.ShapeDtypeStruct((tokens, feat), BF16),
        jax.ShapeDtypeStruct((tokens, feat), BF16),
    ]
    return pl.pallas_call(
        functools.partial(out_kernel, cols, own),
        grid=(steps,),
        in_specs=[whole(a) for a in att]
        + [pl.BlockSpec((qw, chunk), lambda i: (0, i))] * (2 * cols)
        + [
            pl.BlockSpec((tokens, chunk), lambda i: (0, i)),
            pl.BlockSpec((tokens, chunk), lambda i: (0, steps + i)),
            whole(gain),
        ],
        out_specs=[whole(o) for o in outs],
        out_shape=outs,
        scratch_shapes=[pltpu.VMEM((tokens, feat), F32)] * 2,
        compiler_params=params(40),
        cost_estimate=cost(4 * tokens * qw * cols * feat, 10e6),
        name="out_norm",
    )(*att, *wa, *wb, x, x, gain)


def assemble_kernel(cols, meta, ca, cb, out_a, out_b):
    rows = ca.shape[0] // cols
    own = rows // 2
    tokens = cols * own
    r, c = meta[0], meta[1]
    for j in range(cols):
        at = lax.rem(c + j, cols) * rows
        for src, out in ((ca, out_a), (cb, out_b)):
            out[j * own : (j + 1) * own, :] = src[pl.ds(at + r * own, own), :]
            out[tokens + j * own : tokens + (j + 1) * own, :] = src[
                pl.ds(at + (1 - r) * own, own), :
            ]


def assemble_call(meta, ca, cb, cols):
    out = jax.ShapeDtypeStruct(ca.shape, BF16)
    return pl.pallas_call(
        functools.partial(assemble_kernel, cols),
        in_specs=[pl.BlockSpec(memory_space=pltpu.SMEM)]
        + [pl.BlockSpec(memory_space=pltpu.VMEM)] * 2,
        out_specs=[pl.BlockSpec(memory_space=pltpu.VMEM)] * 2,
        out_shape=[out, out],
        compiler_params=params(24),
        cost_estimate=cost(0, 8 * ca.size),
        name="assemble",
    )(meta, ca, cb)


def hidden_kernel(na, nb, ca, cb, ga, gb, ua, ub, da, db, mixed, grad_gate, grad_up):
    gate = dot_nt(ga[...], na[...]) + dot_nt(gb[...], nb[...])
    up = dot_nt(ua[...], na[...]) + dot_nt(ub[...], nb[...])
    grad_mixed = dot_nt(da[...], ca[...]) + dot_nt(db[...], cb[...])
    s = 0.5 * jnp.tanh(0.5 * gate) + 0.5
    silu = gate * s
    mixed[...] = (silu * up).astype(BF16)
    grad_gate[...] = (grad_mixed * up * (s + silu * (1.0 - s))).astype(BF16)
    grad_up[...] = (grad_mixed * silu).astype(BF16)


def hidden_call(r, na, nb, ca, cb, half, kept, got, chunk):
    tokens, feat = na.shape
    part = got[0].shape[0]
    steps = part // chunk
    act = pl.BlockSpec((tokens, feat), lambda i, r: (0, 0))
    cot = pl.BlockSpec((tokens, feat), lambda i, r: (half, 0))
    mine = pl.BlockSpec((chunk, feat), lambda i, r: (r[0] * steps + i, 0))
    other = pl.BlockSpec((chunk, feat), lambda i, r: (i, 0))
    out = jax.ShapeDtypeStruct((part, tokens), BF16)
    return pl.pallas_call(
        lambda r, *refs: hidden_kernel(*refs),
        grid_spec=pltpu.PrefetchScalarGridSpec(
            num_scalar_prefetch=1,
            grid=(steps,),
            in_specs=[act, act, cot, cot] + [mine, other] * 3,
            out_specs=[pl.BlockSpec((chunk, tokens), lambda i, r: (i, 0))] * 3,
        ),
        out_shape=[out] * 3,
        compiler_params=params(40),
        cost_estimate=cost(12 * tokens * feat * part, 12 * feat * part + 8 * tokens * feat),
        name="hidden",
    )(r, na, nb, ca, cb, *[w for pair in zip(kept, got) for w in pair])


def wgrad_kernel(pairs, act_own, act_other, *refs):
    own, refs = refs[:pairs], refs[pairs:]
    other, outs = refs[:pairs], refs[pairs:]
    for first, second, out in zip(own, other, outs):
        total = dot_nn(first[...], act_own[...]) + dot_nn(second[...], act_other[...])
        out[...] = total.astype(BF16)


def wgrad_call(act_own, act_other, other_block, hidden_own, hidden_other, chunk):
    pairs = len(hidden_own)
    part, tokens = hidden_own[0].shape
    feat = act_own.shape[1]
    hid = pl.BlockSpec((chunk, tokens), lambda i: (i, 0))
    return pl.pallas_call(
        functools.partial(wgrad_kernel, pairs),
        grid=(part // chunk,),
        in_specs=[
            pl.BlockSpec((tokens, feat), lambda i: (0, 0)),
            pl.BlockSpec((tokens, feat), lambda i: (other_block, 0)),
        ]
        + [hid] * (2 * pairs),
        out_specs=[pl.BlockSpec((chunk, feat), lambda i: (i, 0))] * pairs,
        out_shape=[jax.ShapeDtypeStruct((part, feat), BF16)] * pairs,
        compiler_params=params(40),
        cost_estimate=cost(4 * pairs * tokens * feat * part, 2 * pairs * feat * part),
        name="weight_grads",
    )(act_own, act_other, *hidden_own, *hidden_other)


def back_kernel(pairs, *refs):
    hidden, refs = refs[:pairs], refs[pairs:]
    wa, refs = refs[:pairs], refs[pairs:]
    wb, (out_a, out_b) = refs[:pairs], refs[pairs:]
    for w, out in ((wa, out_a), (wb, out_b)):
        total = dot_tn(hidden[0][...], w[0][...])
        for i in range(1, pairs):
            total = total + dot_tn(hidden[i][...], w[i][...])
        out[...] = total.astype(out.dtype)


def back_call(r, hidden, kept, got):
    pairs = len(hidden)
    part, tokens = hidden[0].shape
    feat = got[0].shape[1]
    out = jax.ShapeDtypeStruct((tokens, feat), BF16)
    return pl.pallas_call(
        lambda r, *refs: back_kernel(pairs, *refs),
        grid_spec=pltpu.PrefetchScalarGridSpec(
            num_scalar_prefetch=1,
            grid=(1,),
            in_specs=[pl.BlockSpec((part, tokens), lambda i, r: (0, 0))] * pairs
            + [pl.BlockSpec((part, feat), lambda i, r: (r[0], 0))] * pairs
            + [pl.BlockSpec((part, feat), lambda i, r: (0, 0))] * pairs,
            out_specs=[pl.BlockSpec((tokens, feat), lambda i, r: (0, 0))] * 2,
        ),
        out_shape=[out] * 2,
        compiler_params=params(40),
        cost_estimate=cost(4 * pairs * tokens * feat * part, 4 * pairs * feat * part),
        name="back_in",
    )(r, *hidden, *kept, *got)


def attend_back_kernel(
    scaling, own, prefix, *refs
):
    (gr, wa, wb, q, kv_a, kv_b, qpos, kpos, cosine, sine,
     low_out, sum_out, gkv_own, gkv_send, gk, gv, ga_s) = refs
    step, steps = pl.program_id(0), pl.num_programs(0)
    feat = wa.shape[1]
    visible = visibility(qpos[...], kpos[...], prefix)
    keys = jnp.concatenate([kv_a[:, :HD], kv_b[:, :HD]], axis=0)
    values = jnp.concatenate([kv_a[:, HD:], kv_b[:, HD:]], axis=0)
    ga_s[...] = (dot_nt(gr[:, :feat], wa[...]) + dot_nt(gr[:, feat:], wb[...])).astype(BF16)

    @pl.when(step == 0)
    def _():
        gk[...] = jnp.zeros_like(gk)
        gv[...] = jnp.zeros_like(gv)
        sum_out[...] = jnp.zeros_like(sum_out)

    for h in range(q.shape[1] // HD):
        at = slice(h * HD, (h + 1) * HD)
        weights = softmax(q[:, at], keys, visible, scaling)
        grad_att = ga_s[:, at]
        gw = dot_nt(grad_att, values)
        inner = jnp.sum(weights * gw, axis=1, keepdims=True)
        gs = (weights * (gw - inner)).astype(BF16)
        gk[...] += dot_tn(gs, q[:, at])
        gv[...] += dot_tn(weights.astype(BF16), grad_att)
        grad_q = dot_nn(gs, keys) * scaling
        grad_q = rope(grad_q, cosine[...], sine[...])
        low_out[:, at] = grad_q.astype(BF16)
        sum_out[:, at] += jnp.sum(grad_q, axis=0, keepdims=True)

    @pl.when(step == steps - 1)
    def _():
        half = gk.shape[0] // 2
        gkv_own[:, :HD] = gk[:half, :] * scaling
        gkv_own[:, HD:] = gv[:half, :]
        gkv_send[:, :HD] = (gk[half:, :] * scaling).astype(BF16)
        gkv_send[:, HD:] = gv[half:, :].astype(BF16)


def attend_back_call(prefix, gr, wa, wb, q, kv_a, kv_b, qpos, kpos, cosine, sine, block):
    tokens, qw = q.shape
    whole = lambda v: pl.BlockSpec(v.shape, lambda i, p: (0,) * v.ndim)
    part = lambda v: pl.BlockSpec((block, v.shape[1]), lambda i, p: (i, 0))
    outs = [
        jax.ShapeDtypeStruct((tokens, qw), BF16),
        jax.ShapeDtypeStruct((1, qw), F32),
        jax.ShapeDtypeStruct((tokens, 2 * HD), F32),
        jax.ShapeDtypeStruct((tokens, 2 * HD), BF16),
    ]
    keys = 2 * tokens
    return pl.pallas_call(
        functools.partial(attend_back_kernel, HD**-0.5, block),
        grid_spec=pltpu.PrefetchScalarGridSpec(
            num_scalar_prefetch=1,
            grid=(tokens // block,),
            in_specs=[
                part(gr), whole(wa), whole(wb), part(q), whole(kv_a), whole(kv_b),
                part(qpos), whole(kpos), part(cosine), part(sine),
            ],
            out_specs=[part(outs[0]), whole(outs[1]), whole(outs[2]), whole(outs[3])],
            scratch_shapes=[
                pltpu.VMEM((keys, HD), F32),
                pltpu.VMEM((keys, HD), F32),
                pltpu.VMEM((block, qw), BF16),
            ],
        ),
        out_shape=outs,
        compiler_params=params(40),
        cost_estimate=cost(40 * tokens * tokens * qw, 6e6),
        name="attend_back",
    )(prefix, gr, wa, wb, q, kv_a, kv_b, qpos, kpos, cosine, sine)


def join_kernel(axis, width, r_ref, kept, got, out):
    part = kept.shape[axis]
    tail = out.shape[axis] - part

    def put(first, second):
        if axis == 1:
            out[:, :part] = first[...].astype(F32)
            out[:, part:] = second[:, :tail].astype(F32)
        else:
            out[:part, :] = first[...].astype(F32)
            out[part:, :] = second[:tail, :].astype(F32)

    @pl.when(r_ref[0] == 0)
    def _():
        put(kept, got)

    @pl.when(r_ref[0] != 0)
    def _():
        put(got, kept)


def join_call(r, kept, got, axis, ff, chunk):
    shape = list(kept.shape)
    shape[axis] = ff
    other = 1 - axis
    block_in, block_out = list(kept.shape), list(shape)
    block_in[other] = block_out[other] = chunk
    at = (lambda i, r: (0, i)) if axis == 0 else (lambda i, r: (i, 0))
    return pl.pallas_call(
        functools.partial(join_kernel, axis, ff),
        grid_spec=pltpu.PrefetchScalarGridSpec(
            num_scalar_prefetch=1,
            grid=(shape[other] // chunk,),
            in_specs=[pl.BlockSpec(tuple(block_in), at)] * 2,
            out_specs=pl.BlockSpec(tuple(block_out), at),
        ),
        out_shape=jax.ShapeDtypeStruct(tuple(shape), F32),
        compiler_params=params(32),
        cost_estimate=cost(0, 4 * kept.size + 4 * shape[0] * shape[1]),
        name="join",
    )(r, kept, got)


def join_blocks_kernel(count, meta, kept, got, out):
    first = pl.program_id(0) < count

    @pl.when(first == (meta[0] == 0))
    def _():
        out[...] = kept[0].astype(F32)

    @pl.when(first != (meta[0] == 0))
    def _():
        out[...] = got[0].astype(F32)


def join_blocks_call(meta, kept, got):
    count, rows, feat = kept.shape
    place = lambda at: lambda i, m: ((i % count + count - m[at]) % count, 0, 0)
    return pl.pallas_call(
        functools.partial(join_blocks_kernel, count),
        grid_spec=pltpu.PrefetchScalarGridSpec(
            num_scalar_prefetch=1,
            grid=(2 * count,),
            in_specs=[
                pl.BlockSpec((1, rows, feat), place(1)),
                pl.BlockSpec((1, rows, feat), place(2)),
            ],
            out_specs=pl.BlockSpec((rows, feat), lambda i, m: (i, 0)),
        ),
        out_shape=jax.ShapeDtypeStruct((2 * count * rows, feat), F32),
        compiler_params=params(32),
        cost_estimate=cost(0, 16 * count * rows * feat),
        name="join_blocks",
    )(meta, kept, got)
def after(value, *others):
    return lax.optimization_barrier((value,) + others)[0]


def swap_rows(value):
    return lax.ppermute(value, "row", [(0, 1), (1, 0)])


def from_col(value, offset):
    count = lax.axis_size("col")
    return lax.ppermute(value, "col", [((i + offset) % count, i) for i in range(count)])


def gather_col(value):
    third, first = from_col(value, -1), from_col(value, 1)
    return [value, first, from_col(value, 2), third]


def gather_col_ring(value):
    third, first = from_col(value, -1), from_col(value, 1)
    middle = value.shape[0] // 2
    upper = from_col(first[:middle], 1)
    lower = from_col(third[middle:], -1)
    return [value, first, jnp.concatenate([upper, lower], axis=0), third]


def scatter_col(blocks):
    third, first, second = (
        from_col(blocks[3], 1),
        from_col(blocks[1], -1),
        from_col(blocks[2], -2),
    )
    total = blocks[0].astype(F32)
    for part in (first, second, third):
        total = total + part.astype(F32)
    return total


def halves(value):
    middle = value.shape[-1] // 2
    return value[..., :middle], value[..., middle:]


def roll_blocks(value, shift, axis):
    size = value.shape[axis]
    twice = jnp.concatenate([value, value], axis=axis)
    return lax.dynamic_slice_in_dim(twice, shift, size, axis)


def shift_dp(value, along, offset, side):
    pairs = []
    for z in range(side):
        for x in range(side):
            if along == "z":
                source = ((z + offset) % side) * side + x
            else:
                source = z * side + (x + offset) % side
            pairs.append((source, z * side + x))
    return lax.ppermute(value, "dp", pairs)


def scatter_dp(value, along, at, side):
    value = jnp.pad(value, ((0, -value.shape[0] % (8 * side)), (0, 0)))
    rows = value.shape[0] // side
    block = lambda j: lax.dynamic_slice_in_dim(value, ((at + j) % side) * rows, rows, 0)
    got = [shift_dp(block(j), along, -j, side) for j in (1, side - 1, 2)]
    total = block(0).astype(F32)
    for part in got:
        total = total + part.astype(F32)
    return total.astype(BF16)


def gather_dp(value, along, side):
    got = {j: shift_dp(value, along, j, side) for j in (1, side - 1, 2)}
    return [value] + [got[j] for j in range(1, side)]


def body(
    layer_input,
    prefix,
    gain_one,
    w_query,
    b_query,
    w_keyval,
    b_keyval,
    w_out,
    gain_two,
    w_gate,
    w_up,
    w_down,
    cotangent,
):
    cols = lax.axis_size("col")
    groups = lax.axis_size("dp")
    side = int(round(groups**0.5))
    r = lax.axis_index("row")
    c = lax.axis_index("col")
    dp = lax.axis_index("dp")
    z_at, x_at = dp // side, dp % side
    core = r.astype(jnp.int32).reshape(1)
    rows_in, feat = layer_input.shape
    own = rows_in // 2
    tokens = own * cols
    width = 2 * feat
    qw = w_query.shape[1]
    kvw = w_keyval.shape[1] // 2
    share = cols // (kvw // HD)
    kv_head = c // share
    ff = w_gate.shape[1]
    part = ff // 2

    x_a = gather_col(layer_input)
    x_b = [swap_rows(v) for v in x_a]

    key_start = kv_head * HD
    w_qkv_a = jnp.concatenate(
        [
            w_query,
            lax.dynamic_slice_in_dim(w_keyval, key_start, HD, 1),
            lax.dynamic_slice_in_dim(w_keyval, kvw + key_start, HD, 1),
        ],
        axis=1,
    )
    bias = jnp.concatenate(
        [
            b_query,
            lax.dynamic_slice_in_dim(b_keyval, key_start, HD, 0),
            lax.dynamic_slice_in_dim(b_keyval, kvw + key_start, HD, 0),
        ]
    ).astype(F32)[None]
    w_qkv_b = swap_rows(w_qkv_a)
    gains_a = jnp.stack([gain_one, gain_two])
    gains = jnp.concatenate([gains_a, swap_rows(gains_a)], axis=1).astype(F32)
    gain_one_f, gain_two_f = gains[:1], gains[1:]

    kept = [w_gate.T, w_up.T, w_down]
    got = [
        swap_rows(lax.dynamic_slice_in_dim(w, (1 - r) * part, part, 0)) for w in kept
    ]

    block_first = rows_in * ((c + jnp.arange(cols, dtype=jnp.int32)) % cols)
    inside = jnp.arange(own, dtype=jnp.int32)
    pos_own = ((block_first[:, None] + own * r + inside[None]) % SEQ_LEN).reshape(-1)
    pos_other = ((block_first[:, None] + own * (1 - r) + inside[None]) % SEQ_LEN).reshape(-1)
    query_pos = pos_own[:, None]
    key_pos = jnp.concatenate([pos_own, pos_other])[None, :]
    frequency = THETA ** (-jnp.arange(0, HD // 2, dtype=F32) * 2.0 / HD)
    angle = pos_own.astype(F32)[:, None] * frequency[None, :]
    cosine, sine = jnp.cos(angle), jnp.sin(angle)
    cosine = jnp.concatenate([cosine, cosine], axis=1)
    sine_to = jnp.concatenate([-sine, sine], axis=1)
    sine_back = jnp.concatenate([sine, -sine], axis=1)

    x_full, normed_one, query, kv_own = qkv_call(
        core, x_a, x_b, gain_one_f, w_qkv_a, w_qkv_b, bias, cosine, sine_to, qw
    )
    kv_other = swap_rows(kv_own)
    attended = attend_call(prefix, query, kv_own, kv_other, query_pos, key_pos, tokens)
    att = gather_col(attended)

    quarter = qw // side
    wo_part = lax.dynamic_slice_in_dim(w_out, x_at * quarter, quarter, 0)
    wo_parts_col = gather_col(after(wo_part, *x_b, w_qkv_b))[1:]
    wo_parts = gather_dp(jnp.concatenate(wo_parts_col, axis=0), "x", side)
    wo_parts = jnp.stack(wo_parts).reshape(side, cols - 1, quarter, feat)
    wo_parts = roll_blocks(wo_parts, (side - x_at) % side, 0)
    wo_a = [w_out] + [wo_parts[:, j].reshape(qw, feat) for j in range(cols - 1)]
    wo_b = [swap_rows(v) for v in wo_a]
    resid, n2_a, n2_b = out_call(att, wo_a, wo_b, x_full, gain_two_f, own)
    n2_other_b, n2_other_a = swap_rows(n2_a), swap_rows(n2_b)

    c_a = lax.all_gather(after(cotangent, *x_a[1:]), "col", axis=0, tiled=True)
    place = jnp.stack([r, c]).astype(jnp.int32)
    cot_a, cot_b = assemble_call(place, c_a, swap_rows(c_a), cols)

    hid_own = hidden_call(core, n2_a, n2_b, cot_a, cot_b, 0, kept, got, part // 2)
    hid_other = hidden_call(
        core, n2_other_a, n2_other_b, cot_a, cot_b, 1, kept, got, part // 2
    )
    def weight_grads(n_own, n_other, cot, own, other):
        gate_up = wgrad_call(n_own, n_other, 0, own[1:], other[1:], part // 2)
        return [*gate_up, *wgrad_call(cot, cot, 1, own[:1], other[:1], part // 2)]

    turned = weight_grads(n2_b, n2_other_b, cot_b, hid_own, hid_other)
    sent = [swap_rows(v) for v in turned]
    big = weight_grads(
        n2_a, n2_other_a, cot_a, [after(v, *turned) for v in hid_own], hid_other
    )
    back_other = after(hid_other[1], *big), hid_other[2]
    back_own = after(hid_own[1], *sent), hid_own[2]
    big = lax.psum(tuple(big) + tuple(sent), "dp")

    def sum_cores(own_pair, other_pair):
        from_b, from_a = swap_rows(other_pair[0]), swap_rows(other_pair[1])
        a = own_pair[0].astype(F32) + from_a.astype(F32)
        b = own_pair[1].astype(F32) + from_b.astype(F32)
        return jnp.concatenate([a, b], axis=1).astype(BF16)

    def token_blocks(value):
        return [value[j * own : (j + 1) * own] for j in range(cols)]

    terms_other = back_call(core, back_other, kept[:2], got[:2])
    terms_own = back_call(core, back_own, kept[:2], got[:2])
    grad_normed_two = scatter_col(token_blocks(sum_cores(terms_own, terms_other)))

    def norm_backward(grad, value, gain):
        inverse = lax.rsqrt(jnp.mean(value * value, axis=1, keepdims=True) + EPS)
        unit = value * inverse
        scaled = grad * gain
        mean_term = jnp.mean(scaled * unit, axis=1, keepdims=True)
        return inverse * (scaled - unit * mean_term), jnp.sum(grad * unit, axis=0)

    grad_norm_two, grad_gain_two = norm_backward(grad_normed_two, resid, gain_two_f)
    cot_full = jnp.concatenate([cot_a[:own], cot_b[:own]], axis=1).astype(F32)
    grad_resid = cot_full + grad_norm_two
    resid_blocks = gather_col(grad_resid.astype(BF16))
    resid_low = jnp.concatenate(resid_blocks, axis=0)

    query_low, grad_b_query, gkv_own, gkv_sent = attend_back_call(
        prefix, resid_low, wo_a[0], wo_b[0], query, kv_own, kv_other,
        query_pos, key_pos, cosine, sine_back, tokens,
    )
    grad_kv = gkv_own + swap_rows(gkv_sent).astype(F32)
    grad_key = grad_kv[:, :HD]
    grad_key = grad_key * cosine + jnp.roll(grad_key, HD // 2, axis=1) * sine_back
    grad_keyval = jnp.concatenate([grad_key, grad_kv[:, HD:]], axis=1)
    grad_b_kv = jnp.sum(grad_keyval, axis=0)
    qkv_low = jnp.concatenate([query_low, grad_keyval.astype(BF16)], axis=1)
    back_one = jnp.concatenate(
        [dot_nt(qkv_low, w_qkv_a), dot_nt(qkv_low, w_qkv_b)], axis=1
    ).astype(BF16)
    grad_normed_one = scatter_col(token_blocks(back_one))

    def exchange_out(value):
        mine, other = halves(value)
        other = swap_rows(other)
        return jnp.where(
            r == 0,
            jnp.concatenate([mine, other], axis=0),
            jnp.concatenate([other, mine], axis=0),
        )

    grad_norm_one, grad_gain_one = norm_backward(
        grad_normed_one, x_full[:own].astype(F32), gain_one_f
    )
    grad_input = exchange_out(grad_resid + grad_norm_one)

    mixed_other = after(hid_other[0], grad_resid)
    mixed_own = after(hid_own[0], grad_resid)
    down_other = back_call(core, [mixed_other], kept[2:], got[2:])
    down_own = back_call(core, [mixed_own], kept[2:], got[2:])
    down = token_blocks(sum_cores(down_own, down_other))
    down = scatter_col([after(v, resid_blocks[2]) for v in down])
    output = exchange_out((resid + down).astype(BF16))

    grad_wout_a, grad_wout_b = halves(dot_tn(attended, resid_low))
    n1_a, n1_b = halves(normed_one)
    rest = dot_tn(n1_a, qkv_low) + swap_rows(dot_tn(n1_b, qkv_low).astype(BF16)).astype(F32)
    grad_wout = grad_wout_a + swap_rows(grad_wout_b.astype(BF16)).astype(F32)
    grad_wout = jnp.concatenate(halves(grad_wout), axis=0)
    rest = jnp.concatenate([grad_wout, rest], axis=1).astype(BF16)
    rest = scatter_dp(scatter_dp(rest, "x", x_at, side), "z", z_at, side)
    piece_rows = rest.shape[0]

    one_a, one_b = halves(grad_gain_one)
    two_a, two_b = halves(grad_gain_two)
    biases = jnp.concatenate([grad_b_kv, grad_b_query[0]])
    small = jnp.concatenate([one_a, two_a, biases]) + swap_rows(
        jnp.concatenate([one_b, two_b, biases])
    )

    def pack(vector, columns):
        vector = jnp.pad(vector, (0, SMALL_ROWS * columns - vector.shape[0]))
        return vector.astype(BF16).reshape(SMALL_ROWS, columns)

    kv_cols = 2 * HD
    in_col = width + kv_cols
    message = jnp.concatenate([rest[:, -kv_cols:], pack(small[:in_col], kv_cols)], axis=0)
    messages = gather_col(message)
    kv_parts = [m[:piece_rows].astype(F32) for m in messages]
    small_parts = [m[piece_rows:].astype(F32).reshape(-1)[:in_col] for m in messages]
    gains_sum = sum(v[:width] for v in small_parts)
    kv_sums, bias_sums = [], []
    for head in range(kvw // HD):
        same = [(((c + j) % cols) // share == head).astype(F32) for j in range(cols)]
        kv_sums.append(sum(s * v for s, v in zip(same, kv_parts)))
        bias_sums.append(sum(s * v[width:] for s, v in zip(same, small_parts)))
    heads_first = lambda v: [s[..., :HD] for s in v] + [s[..., HD:] for s in v]
    kv_sum = jnp.concatenate(heads_first(kv_sums), axis=1).astype(BF16)
    rest = jnp.concatenate([rest[:, :-kv_cols], kv_sum], axis=1)
    columns = rest.shape[1]
    small = jnp.concatenate([gains_sum] + heads_first(bias_sums) + [small[in_col:]])
    pieces = gather_dp(jnp.concatenate([rest, pack(small, columns)], axis=0), "z", side)
    small = sum(p[piece_rows:].astype(F32) for p in pieces).astype(BF16)
    rest = roll_blocks(
        jnp.stack([p[:piece_rows] for p in pieces]), (side - z_at) % side, 0
    ).reshape(side * piece_rows, columns)
    pieces = gather_dp(jnp.concatenate([rest, small], axis=0), "x", side)
    small = sum(p[side * piece_rows :].astype(F32) for p in pieces).reshape(-1)
    rest = roll_blocks(
        jnp.stack([p[: side * piece_rows] for p in pieces]), (side - x_at) % side, 0
    ).reshape(feat, columns)
    rest = rest.astype(F32)
    grad_wout = jnp.concatenate([rest[:qw, :qw], rest[qw:, :qw]], axis=1)
    bias_kv = small[width : width + 2 * kvw]
    bias_query = small[width + 2 * kvw : width + 2 * kvw + qw]

    join = lambda i: join_call(core, big[i], big[3 + i], 0, ff, 256)
    return (
        output,
        grad_input,
        small[:feat],
        rest[:, qw : 2 * qw],
        bias_query,
        rest[:, 2 * qw :],
        bias_kv,
        grad_wout,
        small[feat:width],
        join(0).T,
        join(1).T,
        join(2),
    )


def solution(mesh):
    return jax.shard_map(
        body,
        mesh=mesh,
        in_specs=(
            P(("dp", "col"), "row"),
            P("dp"),
            P("row"),
            P("row", "col"),
            P("col"),
            P("row", None),
            P(),
            P("col", "row"),
            P("row"),
            P("row", "col"),
            P("row", "col"),
            P("col", "row"),
            P(("dp", "col"), "row"),
        ),
        out_specs=(
            P(("dp", "col"), "row"),
            P(("dp", "col"), "row"),
            P("row"),
            P("row", "col"),
            P("col"),
            P("row", None),
            P(),
            P("col", "row"),
            P("row"),
            P("row", "col"),
            P("row", "col"),
            P("col", "row"),
        ),
        check_vma=False,
    )
```

```python
import functools

import jax
import jax.numpy as jnp
from jax import lax
from jax.experimental import pallas as pl
from jax.experimental.pallas import tpu as pltpu
from jax.sharding import PartitionSpec as P

HD = 128
SEQ_LEN = 1024
EPS = 1e-06
THETA = 1000000.0
NEG = -1e30
BF16 = jnp.bfloat16
F32 = jnp.float32
MIB = 1 << 20
SMALL_ROWS = 16
LITTLE = 1000


def dot_nn(left, right):
    return lax.dot_general(left, right, (((1,), (0,)), ((), ())), preferred_element_type=F32)


def dot_nt(left, right):
    return lax.dot_general(left, right, (((1,), (1,)), ((), ())), preferred_element_type=F32)


def dot_tn(left, right):
    return lax.dot_general(left, right, (((0,), (0,)), ((), ())), preferred_element_type=F32)


def params(mib):
    return pltpu.CompilerParams(vmem_limit_bytes=mib * MIB)


def cost(flops, nbytes):
    return pl.CostEstimate(flops=int(flops), bytes_accessed=int(nbytes), transcendentals=0)


def rope(value, cosine, sine):
    return value * cosine + pltpu.roll(value, HD // 2, 1) * sine


def qkv_kernel(cols, own, *refs):
    r_ref, refs = refs[0], refs[1:]
    xa, refs = refs[:cols], refs[cols:]
    xb, refs = refs[:cols], refs[cols:]
    gain, wa, wb, bias, cosine, sine, x_out, n_out, q_out, kv_out = refs
    feat = xa[0].shape[1]
    for j in range(cols):
        rows = pl.ds(j * own, own)
        a = xa[j][...].astype(F32)
        b = xb[j][...].astype(F32)
        total = jnp.sum(a * a, axis=1, keepdims=True) + jnp.sum(b * b, axis=1, keepdims=True)
        inverse = lax.rsqrt(total / (2 * feat) + EPS)
        x_out[rows, :feat] = xa[j][...]
        x_out[rows, feat:] = xb[j][...]
        n_out[rows, :feat] = (a * inverse * gain[:, :feat]).astype(BF16)
        n_out[rows, feat:] = (b * inverse * gain[:, feat:]).astype(BF16)
    qkv = dot_nn(n_out[:, :feat], wa[...]) + dot_nn(n_out[:, feat:], wb[...]) + bias[...]
    qw = q_out.shape[1]
    for h in range(qw // HD):
        at = slice(h * HD, (h + 1) * HD)
        q_out[:, at] = rope(qkv[:, at], cosine[...], sine[...]).astype(BF16)
    kv_out[:, :HD] = rope(qkv[:, qw : qw + HD], cosine[...], sine[...]).astype(BF16)
    kv_out[:, HD:] = qkv[:, qw + HD :].astype(BF16)


def qkv_call(r, xa, xb, gain, wa, wb, bias, cosine, sine, qw, own):
    cols = len(xa)
    feat = xa[0].shape[1]
    tokens = own * cols
    whole = lambda v: pl.BlockSpec(v.shape, lambda i, r: (0,) * v.ndim)
    rest = [gain, wa, wb, bias, cosine, sine]
    outs = [
        jax.ShapeDtypeStruct((tokens, 2 * feat), BF16),
        jax.ShapeDtypeStruct((tokens, 2 * feat), BF16),
        jax.ShapeDtypeStruct((tokens, qw), BF16),
        jax.ShapeDtypeStruct((tokens, 2 * HD), BF16),
    ]
    return pl.pallas_call(
        functools.partial(qkv_kernel, cols, own),
        grid_spec=pltpu.PrefetchScalarGridSpec(
            num_scalar_prefetch=1,
            grid=(1,),
            in_specs=[pl.BlockSpec((own, feat), lambda i, r: (r[0], 0))] * (2 * cols)
            + [whole(v) for v in rest],
            out_specs=[whole(o) for o in outs],
        ),
        out_shape=outs,
        compiler_params=params(40),
        cost_estimate=cost(LITTLE, LITTLE),
        name="qkv",
    )(r, *xa, *xb, *rest)


def softmax(q, k, visible, scaling):
    scores = jnp.where(visible, dot_nt(q, k) * scaling, NEG)
    e = jnp.exp(scores - jnp.max(scores, axis=1, keepdims=True))
    return e * (1.0 / jnp.sum(e, axis=1, keepdims=True))


def visibility(qpos, kpos, prefix_ref):
    return (kpos <= qpos) | (kpos < prefix_ref[0])


def attend_kernel(scaling, prefix, q, kv_a, kv_b, qpos, kpos, out):
    visible = visibility(qpos[...], kpos[...], prefix)
    keys = jnp.concatenate([kv_a[:, :HD], kv_b[:, :HD]], axis=0)
    values = jnp.concatenate([kv_a[:, HD:], kv_b[:, HD:]], axis=0)
    for h in range(q.shape[1] // HD):
        at = slice(h * HD, (h + 1) * HD)
        weights = softmax(q[:, at], keys, visible, scaling)
        out[:, at] = dot_nn(weights.astype(BF16), values).astype(BF16)


def attend_call(prefix, q, kv_a, kv_b, qpos, kpos, block):
    tokens, qw = q.shape
    whole = lambda v: pl.BlockSpec(v.shape, lambda i, p: (0,) * v.ndim)
    part = lambda v: pl.BlockSpec((block, v.shape[1]), lambda i, p: (i, 0))
    return pl.pallas_call(
        functools.partial(attend_kernel, HD**-0.5),
        grid_spec=pltpu.PrefetchScalarGridSpec(
            num_scalar_prefetch=1,
            grid=(tokens // block,),
            in_specs=[part(q), whole(kv_a), whole(kv_b), part(qpos), whole(kpos)],
            out_specs=part(q),
        ),
        out_shape=jax.ShapeDtypeStruct(q.shape, BF16),
        compiler_params=params(32),
        cost_estimate=cost(LITTLE, LITTLE),
        name="attend",
    )(prefix, q, kv_a, kv_b, qpos, kpos)


def out_kernel(cols, own, side, x_at, *refs):
    att, refs = refs[:cols], refs[cols:]
    wa, wb, refs = refs[0], refs[1], refs[2:]
    pa, refs = refs[:side], refs[side:]
    pb, refs = refs[:side], refs[side:]
    xa, xb, gain, resid_out, na, nb, acc_a, acc_b, whole_a, whole_b = refs
    step, steps = pl.program_id(0), pl.num_programs(0)
    chunk = xa.shape[1]
    feat = chunk * steps
    quarter = wa.shape[0] // side

    rolled = []
    for j in range(cols):
        tiles = [att[j][((i - j) % cols) * own : ((i - j) % cols + 1) * own, :] for i in range(cols)]
        rolled.append(jnp.concatenate(tiles, axis=0))
    at = pl.ds(pl.multiple_of(step * chunk, 128), chunk)
    for parts, whole in ((pa, whole_a), (pb, whole_b)):
        for i in range(side):
            place = lax.rem(x_at[0] + i, side) * quarter
            for j in range(cols - 1):
                rows = parts[i][j * quarter : (j + 1) * quarter, :]
                whole[j, pl.ds(pl.multiple_of(place, 32), quarter), :] = rows
    for x, w, whole, acc in ((xa, wa, whole_a, acc_a), (xb, wb, whole_b, acc_b)):
        total = x[...].astype(F32) + dot_nn(rolled[0], w[...])
        for j in range(1, cols):
            total = total + dot_nn(rolled[j], whole[j - 1])
        acc[:, at] = total

    @pl.when(step == steps - 1)
    def _():
        a, b = acc_a[...], acc_b[...]
        total = jnp.sum(a * a, axis=1, keepdims=True) + jnp.sum(b * b, axis=1, keepdims=True)
        inverse = lax.rsqrt(total / (2 * feat) + EPS)
        na[...] = (a * inverse * gain[:, :feat]).astype(BF16)
        nb[...] = (b * inverse * gain[:, feat:]).astype(BF16)
        resid_out[:, :feat] = acc_a[:own, :]
        resid_out[:, feat:] = acc_b[:own, :]


def out_call(x_at, att, wa, wb, pa, pb, x, gain, own):
    cols, side = len(att), len(pa)
    tokens, qw = att[0].shape
    feat = wa.shape[1]
    steps = 3
    chunk = feat // steps
    whole = lambda v: pl.BlockSpec(v.shape, lambda i, p: (0,) * v.ndim)
    part = lambda v: pl.BlockSpec((v.shape[0], chunk), lambda i, p: (0, i))
    outs = [
        jax.ShapeDtypeStruct((own, 2 * feat), F32),
        jax.ShapeDtypeStruct((tokens, feat), BF16),
        jax.ShapeDtypeStruct((tokens, feat), BF16),
    ]
    return pl.pallas_call(
        functools.partial(out_kernel, cols, own, side),
        grid_spec=pltpu.PrefetchScalarGridSpec(
            num_scalar_prefetch=1,
            grid=(steps,),
            in_specs=[whole(a) for a in att]
            + [part(v) for v in (wa, wb, *pa, *pb)]
            + [part(x), pl.BlockSpec((tokens, chunk), lambda i, p: (0, steps + i)), whole(gain)],
            out_specs=[whole(o) for o in outs],
            scratch_shapes=[
                pltpu.VMEM((tokens, feat), F32),
                pltpu.VMEM((tokens, feat), F32),
                pltpu.VMEM((cols - 1, qw, chunk), BF16),
                pltpu.VMEM((cols - 1, qw, chunk), BF16),
            ],
        ),
        out_shape=outs,
        compiler_params=params(40),
        cost_estimate=cost(LITTLE, LITTLE),
        name="out_norm",
    )(x_at, *att, wa, wb, *pa, *pb, x, x, gain)


def assemble_kernel(cols, own, r_ref, *refs):
    ca, cb, (out_a, out_b) = refs[:cols], refs[cols : 2 * cols], refs[2 * cols :]
    tokens = cols * own
    first = ca[0].shape[0] - 2 * own
    r = r_ref[0]
    for j in range(cols):
        for src, out in ((ca[j], out_a), (cb[j], out_b)):
            out[j * own : (j + 1) * own, :] = src[pl.ds(first + r * own, own), :]
            out[tokens + j * own : tokens + (j + 1) * own, :] = src[
                pl.ds(first + (1 - r) * own, own), :
            ]


def assemble_call(r, ca, cb, own):
    cols = len(ca)
    out = jax.ShapeDtypeStruct((2 * cols * own, ca[0].shape[1]), BF16)
    return pl.pallas_call(
        functools.partial(assemble_kernel, cols, own),
        in_specs=[pl.BlockSpec(memory_space=pltpu.SMEM)]
        + [pl.BlockSpec(memory_space=pltpu.VMEM)] * (2 * cols),
        out_specs=[pl.BlockSpec(memory_space=pltpu.VMEM)] * 2,
        out_shape=[out, out],
        compiler_params=params(24),
        cost_estimate=cost(LITTLE, LITTLE),
        name="assemble",
    )(r, *ca, *cb)


def gated_kernel(na, nb, ga, gb, ua, ub, mixed, to_gate, to_up):
    gate = dot_nt(ga[...], na[...]) + dot_nt(gb[...], nb[...])
    up = dot_nt(ua[...], na[...]) + dot_nt(ub[...], nb[...])
    s = 0.5 * jnp.tanh(0.5 * gate) + 0.5
    silu = gate * s
    mixed[...] = (silu * up).astype(BF16)
    to_gate[...] = (up * (s + silu * (1.0 - s))).astype(BF16)
    to_up[...] = silu.astype(BF16)


def hidden_grad_kernel(ca, cb, da, db, to_gate, to_up, grad_gate, grad_up):
    grad_mixed = dot_nt(da[...], ca[...]) + dot_nt(db[...], cb[...])
    grad_gate[...] = (grad_mixed * to_gate[...].astype(F32)).astype(BF16)
    grad_up[...] = (grad_mixed * to_up[...].astype(F32)).astype(BF16)


def gated_call(r, na, nb, kept, got, chunk):
    tokens, feat = na.shape
    part = got.shape[1]
    steps = part // chunk
    act = pl.BlockSpec((tokens, feat), lambda i, r: (0, 0))
    mine = pl.BlockSpec((chunk, feat), lambda i, r: (r[0] * steps + i, 0))
    other = lambda k: pl.BlockSpec((None, chunk, feat), lambda i, r: (k, i, 0))
    return pl.pallas_call(
        lambda r, *refs: gated_kernel(*refs),
        grid_spec=pltpu.PrefetchScalarGridSpec(
            num_scalar_prefetch=1,
            grid=(steps,),
            in_specs=[act, act, mine, other(0), mine, other(1)],
            out_specs=[pl.BlockSpec((chunk, tokens), lambda i, r: (i, 0))] * 3,
        ),
        out_shape=[jax.ShapeDtypeStruct((part, tokens), BF16)] * 3,
        compiler_params=params(40),
        cost_estimate=cost(LITTLE, LITTLE),
        name="gated",
    )(r, na, nb, kept[0], got, kept[1], got)


def hidden_grad_call(r, ca, cb, half, kept, got, to_gate, to_up, chunk):
    part, tokens = to_gate.shape
    feat = ca.shape[1]
    steps = part // chunk
    cot = pl.BlockSpec((tokens, feat), lambda i, r: (half, 0))
    hid = pl.BlockSpec((chunk, tokens), lambda i, r: (i, 0))
    return pl.pallas_call(
        lambda r, *refs: hidden_grad_kernel(*refs),
        grid_spec=pltpu.PrefetchScalarGridSpec(
            num_scalar_prefetch=1,
            grid=(steps,),
            in_specs=[
                cot,
                cot,
                pl.BlockSpec((chunk, feat), lambda i, r: (r[0] * steps + i, 0)),
                pl.BlockSpec((None, chunk, feat), lambda i, r: (2, i, 0)),
                hid,
                hid,
            ],
            out_specs=[hid, hid],
        ),
        out_shape=[jax.ShapeDtypeStruct((part, tokens), BF16)] * 2,
        compiler_params=params(40),
        cost_estimate=cost(LITTLE, LITTLE),
        name="hidden_grads",
    )(r, ca, cb, kept[2], got, to_gate, to_up)


def wgrad_kernel(pairs, act_own, act_other, *refs):
    own, refs = refs[:pairs], refs[pairs:]
    other, outs = refs[:pairs], refs[pairs:]
    for first, second, out in zip(own, other, outs):
        total = dot_nn(first[...], act_own[...]) + dot_nn(second[...], act_other[...])
        out[...] = total.astype(BF16)


def wgrad_call(act_own, act_other, other_block, hidden_own, hidden_other, chunk):
    pairs = len(hidden_own)
    part, tokens = hidden_own[0].shape
    feat = act_own.shape[1]
    hid = pl.BlockSpec((chunk, tokens), lambda i: (i, 0))
    return pl.pallas_call(
        functools.partial(wgrad_kernel, pairs),
        grid=(part // chunk,),
        in_specs=[
            pl.BlockSpec((tokens, feat), lambda i: (0, 0)),
            pl.BlockSpec((tokens, feat), lambda i: (other_block, 0)),
        ]
        + [hid] * (2 * pairs),
        out_specs=[pl.BlockSpec((chunk, feat), lambda i: (i, 0))] * pairs,
        out_shape=[jax.ShapeDtypeStruct((part, feat), BF16)] * pairs,
        compiler_params=params(40),
        cost_estimate=cost(LITTLE, LITTLE),
        name="weight_grads",
    )(act_own, act_other, *hidden_own, *hidden_other)


def back_kernel(pairs, *refs):
    hidden, refs = (refs[:pairs], refs[pairs : 2 * pairs]), refs[2 * pairs :]
    wa, refs = refs[:pairs], refs[pairs:]
    wb, outs = refs[:pairs], refs[pairs:]
    for half in (1, 0):
        for w, out in ((wa, outs[2 * half]), (wb, outs[2 * half + 1])):
            total = dot_tn(hidden[half][0][...], w[0][...])
            for i in range(1, pairs):
                total = total + dot_tn(hidden[half][i][...], w[i][...])
            out[...] = total.astype(out.dtype)


def back_call(r, own, other, kept, got, first):
    pairs = len(own)
    part, tokens = own[0].shape
    feat = got.shape[2]
    out = jax.ShapeDtypeStruct((tokens, feat), BF16)
    of_other = lambda k: pl.BlockSpec((None, part, feat), lambda i, r: (first + k, 0, 0))
    return pl.pallas_call(
        lambda r, *refs: back_kernel(pairs, *refs),
        grid_spec=pltpu.PrefetchScalarGridSpec(
            num_scalar_prefetch=1,
            grid=(1,),
            in_specs=[pl.BlockSpec((part, tokens), lambda i, r: (0, 0))] * (2 * pairs)
            + [pl.BlockSpec((part, feat), lambda i, r: (r[0], 0))] * pairs
            + [of_other(k) for k in range(pairs)],
            out_specs=[pl.BlockSpec((tokens, feat), lambda i, r: (0, 0))] * 4,
        ),
        out_shape=[out] * 4,
        compiler_params=params(44),
        cost_estimate=cost(LITTLE, LITTLE),
        name="back_in",
    )(r, *own, *other, *kept, *([got] * pairs))


def attend_back_kernel(
    scaling, own, prefix, *refs
):
    (gr, wa, wb, q, kv_a, kv_b, qpos, kpos, cosine, sine,
     low_out, sum_out, gkv_own, gkv_send, gk, gv, ga_s) = refs
    step, steps = pl.program_id(0), pl.num_programs(0)
    feat = wa.shape[1]
    visible = visibility(qpos[...], kpos[...], prefix)
    keys = jnp.concatenate([kv_a[:, :HD], kv_b[:, :HD]], axis=0)
    values = jnp.concatenate([kv_a[:, HD:], kv_b[:, HD:]], axis=0)
    ga_s[...] = (dot_nt(gr[:, :feat], wa[...]) + dot_nt(gr[:, feat:], wb[...])).astype(BF16)

    @pl.when(step == 0)
    def _():
        gk[...] = jnp.zeros_like(gk)
        gv[...] = jnp.zeros_like(gv)
        sum_out[...] = jnp.zeros_like(sum_out)

    for h in range(q.shape[1] // HD):
        at = slice(h * HD, (h + 1) * HD)
        weights = softmax(q[:, at], keys, visible, scaling)
        grad_att = ga_s[:, at]
        gw = dot_nt(grad_att, values)
        inner = jnp.sum(weights * gw, axis=1, keepdims=True)
        gs = (weights * (gw - inner)).astype(BF16)
        gk[...] += dot_tn(gs, q[:, at])
        gv[...] += dot_tn(weights.astype(BF16), grad_att)
        grad_q = dot_nn(gs, keys) * scaling
        grad_q = rope(grad_q, cosine[...], sine[...])
        low_out[:, at] = grad_q.astype(BF16)
        sum_out[:, at] += jnp.sum(grad_q, axis=0, keepdims=True)

    @pl.when(step == steps - 1)
    def _():
        half = gk.shape[0] // 2
        gkv_own[:, :HD] = gk[:half, :] * scaling
        gkv_own[:, HD:] = gv[:half, :]
        gkv_send[:, :HD] = (gk[half:, :] * scaling).astype(BF16)
        gkv_send[:, HD:] = gv[half:, :].astype(BF16)


def attend_back_call(prefix, gr, wa, wb, q, kv_a, kv_b, qpos, kpos, cosine, sine, block):
    tokens, qw = q.shape
    whole = lambda v: pl.BlockSpec(v.shape, lambda i, p: (0,) * v.ndim)
    part = lambda v: pl.BlockSpec((block, v.shape[1]), lambda i, p: (i, 0))
    outs = [
        jax.ShapeDtypeStruct((tokens, qw), BF16),
        jax.ShapeDtypeStruct((1, qw), F32),
        jax.ShapeDtypeStruct((tokens, 2 * HD), F32),
        jax.ShapeDtypeStruct((tokens, 2 * HD), BF16),
    ]
    keys = 2 * tokens
    return pl.pallas_call(
        functools.partial(attend_back_kernel, HD**-0.5, block),
        grid_spec=pltpu.PrefetchScalarGridSpec(
            num_scalar_prefetch=1,
            grid=(tokens // block,),
            in_specs=[
                part(gr), whole(wa), whole(wb), part(q), whole(kv_a), whole(kv_b),
                part(qpos), whole(kpos), part(cosine), part(sine),
            ],
            out_specs=[part(outs[0]), whole(outs[1]), whole(outs[2]), whole(outs[3])],
            scratch_shapes=[
                pltpu.VMEM((keys, HD), F32),
                pltpu.VMEM((keys, HD), F32),
                pltpu.VMEM((block, qw), BF16),
            ],
        ),
        out_shape=outs,
        compiler_params=params(40),
        cost_estimate=cost(LITTLE, LITTLE),
        name="attend_back",
    )(prefix, gr, wa, wb, q, kv_a, kv_b, qpos, kpos, cosine, sine)


def qkv_back_kernel(own, got, query_low, cosine, sine, wa, wb, low, sums, back):
    qw = query_low.shape[1]
    total = own[...] + got[...].astype(F32)
    key = rope(total[:, :HD], cosine[...], sine[...])
    value = total[:, HD:]
    sums[:, :HD] = jnp.sum(key, axis=0, keepdims=True)
    sums[:, HD:] = jnp.sum(value, axis=0, keepdims=True)
    low[:, :qw] = query_low[...]
    low[:, qw : qw + HD] = key.astype(BF16)
    low[:, qw + HD :] = value.astype(BF16)
    feat = wa.shape[0]
    back[:, :feat] = dot_nt(low[...], wa[...]).astype(BF16)
    back[:, feat:] = dot_nt(low[...], wb[...]).astype(BF16)


def qkv_back_call(own, got, query_low, cosine, sine, wa, wb):
    tokens = own.shape[0]
    feat, columns = wa.shape
    return pl.pallas_call(
        qkv_back_kernel,
        out_shape=[
            jax.ShapeDtypeStruct((tokens, columns), BF16),
            jax.ShapeDtypeStruct((1, 2 * HD), F32),
            jax.ShapeDtypeStruct((tokens, 2 * feat), BF16),
        ],
        compiler_params=params(32),
        cost_estimate=cost(LITTLE, LITTLE),
        name="qkv_back",
    )(own, got, query_low, cosine, sine, wa, wb)


def rest_kernel(n1, low, attended, grad, in_a, in_b, out_a, out_b):
    feat = n1.shape[1] // 2
    in_b[...] = dot_tn(n1[:, feat:], low[...]).astype(BF16)
    out_b[...] = dot_tn(attended[...], grad[:, feat:]).astype(BF16)
    in_a[...] = dot_tn(n1[:, :feat], low[...]).astype(BF16)
    out_a[...] = dot_tn(attended[...], grad[:, :feat]).astype(BF16)


def rest_call(n1, low, attended, grad):
    feat = n1.shape[1] // 2
    into = jax.ShapeDtypeStruct((feat, low.shape[1]), BF16)
    out = jax.ShapeDtypeStruct((attended.shape[1], feat), BF16)
    return pl.pallas_call(
        rest_kernel,
        out_shape=[into, into, out, out],
        compiler_params=params(32),
        cost_estimate=cost(LITTLE, LITTLE),
        name="rest",
    )(n1, low, attended, grad)


def join_kernel(axis, width, r_ref, kept, got, out):
    part = kept.shape[axis]
    tail = out.shape[axis] - part

    def put(first, second):
        if axis == 1:
            out[:, :part] = first[...].astype(F32)
            out[:, part:] = second[:, :tail].astype(F32)
        else:
            out[:part, :] = first[...].astype(F32)
            out[part:, :] = second[:tail, :].astype(F32)

    @pl.when(r_ref[0] == 0)
    def _():
        put(kept, got)

    @pl.when(r_ref[0] != 0)
    def _():
        put(got, kept)


def join_call(r, kept, got, axis, ff, chunk):
    shape = list(kept.shape)
    shape[axis] = ff
    other = 1 - axis
    block_in, block_out = list(kept.shape), list(shape)
    block_in[other] = block_out[other] = chunk
    at = (lambda i, r: (0, i)) if axis == 0 else (lambda i, r: (i, 0))
    return pl.pallas_call(
        functools.partial(join_kernel, axis, ff),
        grid_spec=pltpu.PrefetchScalarGridSpec(
            num_scalar_prefetch=1,
            grid=(shape[other] // chunk,),
            in_specs=[pl.BlockSpec(tuple(block_in), at)] * 2,
            out_specs=pl.BlockSpec(tuple(block_out), at),
        ),
        out_shape=jax.ShapeDtypeStruct(tuple(shape), F32),
        compiler_params=params(32),
        cost_estimate=cost(LITTLE, LITTLE),
        name="join",
    )(r, kept, got)


def join_blocks_kernel(count, meta, kept, got, out):
    first = pl.program_id(0) < count

    @pl.when(first == (meta[0] == 0))
    def _():
        out[...] = kept[0].astype(F32)

    @pl.when(first != (meta[0] == 0))
    def _():
        out[...] = got[0].astype(F32)


def join_blocks_call(meta, kept, got):
    count, rows, feat = kept.shape
    place = lambda at: lambda i, m: ((i % count + count - m[at]) % count, 0, 0)
    return pl.pallas_call(
        functools.partial(join_blocks_kernel, count),
        grid_spec=pltpu.PrefetchScalarGridSpec(
            num_scalar_prefetch=1,
            grid=(2 * count,),
            in_specs=[
                pl.BlockSpec((1, rows, feat), place(1)),
                pl.BlockSpec((1, rows, feat), place(2)),
            ],
            out_specs=pl.BlockSpec((rows, feat), lambda i, m: (i, 0)),
        ),
        out_shape=jax.ShapeDtypeStruct((2 * count * rows, feat), F32),
        compiler_params=params(32),
        cost_estimate=cost(LITTLE, LITTLE),
        name="join_blocks",
    )(meta, kept, got)
def after(value, *others):
    return lax.optimization_barrier((value,) + others)[0]


def swap_rows(value):
    return lax.ppermute(value, "row", [(0, 1), (1, 0)])


def from_col(value, offset):
    count = lax.axis_size("col")
    return lax.ppermute(value, "col", [((i + offset) % count, i) for i in range(count)])


def gather_col(value):
    third, first = from_col(value, -1), from_col(value, 1)
    return [value, first, from_col(value, 2), third]


def gather_col_ring(value, behind=()):
    third, first = from_col(value, -1), from_col(value, 1)
    middle = value.shape[0] // 2
    upper = from_col(after(first, *behind)[:middle], 1)
    lower = from_col(after(third, *behind)[middle:], -1)
    return [value, first, jnp.concatenate([upper, lower], axis=0), third]


def scatter_col(blocks, behind=()):
    third, first, second = (
        from_col(blocks[3], 1),
        from_col(blocks[1], -1),
        from_col(blocks[2], -2),
    )
    total = blocks[0].astype(F32)
    for part in (first, second, third):
        total = total + after(part, *behind).astype(F32)
    return total


def halves(value):
    middle = value.shape[-1] // 2
    return value[..., :middle], value[..., middle:]


def roll_blocks(value, shift, axis):
    size = value.shape[axis]
    twice = jnp.concatenate([value, value], axis=axis)
    return lax.dynamic_slice_in_dim(twice, shift, size, axis)


def shift_dp(value, along, offset, side):
    pairs = []
    for z in range(side):
        for x in range(side):
            if along == "z":
                source = ((z + offset) % side) * side + x
            else:
                source = z * side + (x + offset) % side
            pairs.append((source, z * side + x))
    return lax.ppermute(value, "dp", pairs)


def scatter_dp(value, along, at, side):
    value = jnp.pad(value, ((0, -value.shape[0] % (8 * side)), (0, 0)))
    rows = value.shape[0] // side
    block = lambda j: lax.dynamic_slice_in_dim(value, ((at + j) % side) * rows, rows, 0)
    got = [shift_dp(block(j), along, -j, side) for j in (1, side - 1, 2)]
    total = block(0).astype(F32)
    for part in got:
        total = total + part.astype(F32)
    return total.astype(BF16)


def gather_dp_ring(value, along, side):
    third, first = shift_dp(value, along, -1, side), shift_dp(value, along, 1, side)
    middle = value.shape[0] // 2
    upper = shift_dp(first[:middle], along, 1, side)
    lower = shift_dp(third[middle:], along, -1, side)
    return [value, first, jnp.concatenate([upper, lower], axis=0), third]


def gather_dp(value, along, side):
    got = {j: shift_dp(value, along, j, side) for j in (1, side - 1, 2)}
    return [value] + [got[j] for j in range(1, side)]


def body(
    layer_input,
    prefix,
    gain_one,
    w_query,
    b_query,
    w_keyval,
    b_keyval,
    w_out,
    gain_two,
    w_gate,
    w_up,
    w_down,
    cotangent,
):
    cols = lax.axis_size("col")
    groups = lax.axis_size("dp")
    side = int(round(groups**0.5))
    r = lax.axis_index("row")
    c = lax.axis_index("col")
    dp = lax.axis_index("dp")
    z_at, x_at = dp // side, dp % side
    core = r.astype(jnp.int32).reshape(1)
    rows_in, feat = layer_input.shape
    own = rows_in // 2
    tokens = own * cols
    width = 2 * feat
    qw = w_query.shape[1]
    kvw = w_keyval.shape[1] // 2
    share = cols // (kvw // HD)
    kv_head = c // share
    ff = w_gate.shape[1]
    part = ff // 2

    quarter = qw // side
    wo_parts = lax.dynamic_slice_in_dim(w_out, x_at * quarter, quarter, 0)
    wo_parts = gather_col(wo_parts)[1:]
    both = jnp.concatenate([layer_input, cotangent], axis=0)
    x_a = gather_col_ring(both, wo_parts)
    wo_parts = gather_dp_ring(jnp.concatenate(wo_parts, axis=0), "x", side)

    key_start = kv_head * HD
    w_qkv_a = jnp.concatenate(
        [
            w_query,
            lax.dynamic_slice_in_dim(w_keyval, key_start, HD, 1),
            lax.dynamic_slice_in_dim(w_keyval, kvw + key_start, HD, 1),
        ],
        axis=1,
    )
    bias = jnp.concatenate(
        [
            b_query,
            lax.dynamic_slice_in_dim(b_keyval, key_start, HD, 0),
            lax.dynamic_slice_in_dim(b_keyval, kvw + key_start, HD, 0),
        ]
    ).astype(F32)[None]
    w_qkv_b = swap_rows(w_qkv_a)
    gains_a = jnp.stack([gain_one, gain_two])
    gains = jnp.concatenate([gains_a, swap_rows(gains_a)], axis=1).astype(F32)
    gain_one_f, gain_two_f = gains[:1], gains[1:]

    kept = [w_gate.T, w_up.T, w_down]
    sent = [
        lax.dynamic_slice_in_dim(after(w, x_a[1], x_a[3]), (1 - r) * part, part, 0)
        for w in kept
    ]
    sent = jnp.stack(sent)

    block_first = rows_in * ((c + jnp.arange(cols, dtype=jnp.int32)) % cols)
    inside = jnp.arange(own, dtype=jnp.int32)
    pos_own = ((block_first[:, None] + own * r + inside[None]) % SEQ_LEN).reshape(-1)
    pos_other = ((block_first[:, None] + own * (1 - r) + inside[None]) % SEQ_LEN).reshape(-1)
    query_pos = pos_own[:, None]
    key_pos = jnp.concatenate([pos_own, pos_other])[None, :]
    frequency = THETA ** (-jnp.arange(0, HD // 2, dtype=F32) * 2.0 / HD)
    angle = pos_own.astype(F32)[:, None] * frequency[None, :]
    cosine, sine = jnp.cos(angle), jnp.sin(angle)
    cosine = jnp.concatenate([cosine, cosine], axis=1)
    sine_to = jnp.concatenate([-sine, sine], axis=1)
    sine_back = jnp.concatenate([sine, -sine], axis=1)

    ready = (wo_parts[1], wo_parts[3], cosine, sine_to, sine_back, query_pos, key_pos, w_qkv_b, gains, bias, sent)
    x_b = [swap_rows(v) for v in x_a[:2]]
    x_b += [swap_rows(after(x_a[2], *ready)), swap_rows(x_a[3])]
    x_full, normed_one, query, kv_own = qkv_call(
        core, x_a, x_b, gain_one_f, w_qkv_a, w_qkv_b, bias, cosine, sine_to, qw, own
    )
    kv_other = swap_rows(kv_own)
    attended = attend_call(prefix, query, kv_own, kv_other, query_pos, key_pos, tokens)
    got = swap_rows(after(sent, attended))
    wo_parts_b = [swap_rows(v) for v in wo_parts]
    att = gather_col_ring(attended)

    wo_a, wo_b = w_out, swap_rows(after(w_out, att[1], att[3]))
    resid, n2_a, n2_b = out_call(
        x_at.astype(jnp.int32).reshape(1), att, wo_a, wo_b, wo_parts, wo_parts_b, x_full,
        gain_two_f, own,
    )
    n2_other_b, n2_other_a = swap_rows(n2_a), swap_rows(n2_b)

    cot_a, cot_b = assemble_call(core, x_a, x_b, own)

    gated_own = gated_call(core, n2_a, n2_b, kept, got, part // 2)
    gated_other = gated_call(core, n2_other_a, n2_other_b, kept, got, part // 2)

    def hidden_grads(half, gated):
        grads = hidden_grad_call(
            core, cot_a, cot_b, half, kept, got, gated[1], gated[2], part // 2
        )
        return [gated[0], *grads]

    hid_own = hidden_grads(0, gated_own)
    hid_other = hidden_grads(1, gated_other)

    def weight_grads(n_own, n_other, cot, own, other):
        gate_up = wgrad_call(n_own, n_other, 0, own[1:], other[1:], part // 2)
        return [*gate_up, *wgrad_call(cot, cot, 1, own[:1], other[:1], part // 2)]

    big_b = weight_grads(n2_b, n2_other_b, cot_b, hid_own, hid_other)
    big_a = weight_grads(n2_a, n2_other_a, cot_a, hid_own, hid_other)
    own_grads = (*big_a, *big_b)
    big = lax.psum(own_grads, "dp")
    big_got = [swap_rows(v) for v in big[3:]]

    def sum_cores(own_pair, other_pair):
        from_b, from_a = swap_rows(other_pair[0]), swap_rows(other_pair[1])
        a = own_pair[0].astype(F32) + from_a.astype(F32)
        b = own_pair[1].astype(F32) + from_b.astype(F32)
        return jnp.concatenate([a, b], axis=1).astype(BF16)

    def token_blocks(value):
        return [value[j * own : (j + 1) * own] for j in range(cols)]

    back_own = [after(v, *own_grads) for v in hid_own[1:]]
    terms = back_call(core, back_own, hid_other[1:], kept[:2], got, 0)
    grad_normed_two = scatter_col(token_blocks(sum_cores(terms[:2], terms[2:])))


    def norm_backward(grad, value, gain):
        inverse = lax.rsqrt(jnp.mean(value * value, axis=1, keepdims=True) + EPS)
        unit = value * inverse
        scaled = grad * gain
        mean_term = jnp.mean(scaled * unit, axis=1, keepdims=True)
        return inverse * (scaled - unit * mean_term), jnp.sum(grad * unit, axis=0)

    grad_norm_two, grad_gain_two = norm_backward(grad_normed_two, resid, gain_two_f)
    cot_full = jnp.concatenate([cot_a[:own], cot_b[:own]], axis=1).astype(F32)
    grad_resid = cot_full + grad_norm_two
    resid_blocks = gather_col(grad_resid.astype(BF16))
    resid_low = jnp.concatenate(resid_blocks, axis=0)

    query_low, grad_b_query, gkv_own, gkv_sent = attend_back_call(
        prefix, resid_low, wo_a, wo_b, query, kv_own, kv_other,
        query_pos, key_pos, cosine, sine_back, tokens,
    )
    qkv_low, grad_b_kv, back_one = qkv_back_call(
        gkv_own, swap_rows(gkv_sent), query_low, cosine, sine_back, w_qkv_a, w_qkv_b
    )
    grad_normed_one = scatter_col(token_blocks(back_one))

    def exchange_out(value):
        mine, other = halves(value)
        other = swap_rows(other)
        return jnp.where(
            r == 0,
            jnp.concatenate([mine, other], axis=0),
            jnp.concatenate([other, mine], axis=0),
        )

    grad_norm_one, grad_gain_one = norm_backward(
        grad_normed_one, x_full[:own].astype(F32), gain_one_f
    )
    grad_input = exchange_out(grad_resid + grad_norm_one)

    mixed_other = after(hid_other[0], grad_normed_one)
    terms = back_call(core, hid_own[:1], [mixed_other], kept[2:], got, 2)
    down = token_blocks(sum_cores(terms[:2], terms[2:]))
    down = scatter_col([after(v, grad_normed_one) for v in down])
    output = exchange_out((resid + down).astype(BF16))

    in_a, in_b, out_a, out_b = rest_call(normed_one, qkv_low, attended, resid_low)
    rest = in_a.astype(F32) + swap_rows(in_b).astype(F32)
    grad_wout = out_a.astype(F32) + swap_rows(out_b).astype(F32)
    grad_wout = jnp.concatenate(halves(grad_wout), axis=0)
    rest = jnp.concatenate([grad_wout, rest], axis=1).astype(BF16)
    rest = scatter_dp(scatter_dp(rest, "x", x_at, side), "z", z_at, side)
    piece_rows = rest.shape[0]

    one_a, one_b = halves(grad_gain_one)
    two_a, two_b = halves(grad_gain_two)
    biases = jnp.concatenate([grad_b_kv[0], grad_b_query[0]])
    small_sent = after(jnp.concatenate([one_b, two_b, biases]), big[0])
    small = jnp.concatenate([one_a, two_a, biases]) + swap_rows(small_sent)

    def pack(vector, columns):
        vector = jnp.pad(vector, (0, SMALL_ROWS * columns - vector.shape[0]))
        return vector.astype(BF16).reshape(SMALL_ROWS, columns)

    kv_cols = 2 * HD
    in_col = width + kv_cols
    message = jnp.concatenate([rest[:, -kv_cols:], pack(small[:in_col], kv_cols)], axis=0)
    messages = gather_col(message)
    kv_parts = [m[:piece_rows].astype(F32) for m in messages]
    small_parts = [m[piece_rows:].astype(F32).reshape(-1)[:in_col] for m in messages]
    gains_sum = sum(v[:width] for v in small_parts)
    kv_sums, bias_sums = [], []
    for head in range(kvw // HD):
        same = [(((c + j) % cols) // share == head).astype(F32) for j in range(cols)]
        kv_sums.append(sum(s * v for s, v in zip(same, kv_parts)))
        bias_sums.append(sum(s * v[width:] for s, v in zip(same, small_parts)))
    heads_first = lambda v: [s[..., :HD] for s in v] + [s[..., HD:] for s in v]
    kv_sum = jnp.concatenate(heads_first(kv_sums), axis=1).astype(BF16)
    rest = jnp.concatenate([rest[:, :-kv_cols], kv_sum], axis=1)
    columns = rest.shape[1]
    small = jnp.concatenate([gains_sum] + heads_first(bias_sums) + [small[in_col:]])
    half = columns // 2
    first = jnp.concatenate([rest[:, :half], pack(small, half)], axis=0)
    first = gather_dp(first, "z", side)
    second = gather_dp(rest[:, half:], "x", side)
    small = sum(p[piece_rows:].astype(F32) for p in first).astype(BF16)
    first = roll_blocks(jnp.stack([p[:piece_rows] for p in first]), (side - z_at) % side, 0)
    first = jnp.concatenate([first.reshape(side * piece_rows, half), small], axis=0)
    second = roll_blocks(jnp.stack(second), (side - x_at) % side, 0)
    first = gather_dp(first, "x", side)
    second = gather_dp(second.reshape(side * piece_rows, half), "z", side)
    small = sum(p[side * piece_rows :].astype(F32) for p in first).reshape(-1)
    first = roll_blocks(
        jnp.stack([p[: side * piece_rows] for p in first]), (side - x_at) % side, 0
    )
    second = roll_blocks(jnp.stack(second), (side - z_at) % side, 0)
    second = second.reshape(side, side, piece_rows, half).swapaxes(0, 1)
    rest = jnp.concatenate([first.reshape(feat, half), second.reshape(feat, half)], axis=1)
    rest = rest.astype(F32)
    grad_wout = jnp.concatenate([rest[:qw, :qw], rest[qw:, :qw]], axis=1)
    bias_kv = small[width : width + 2 * kvw]
    bias_query = small[width + 2 * kvw : width + 2 * kvw + qw]

    join = lambda i: join_call(core, big[i], big_got[i], 0, ff, 256)
    return (
        output,
        grad_input,
        small[:feat],
        rest[:, qw : 2 * qw],
        bias_query,
        rest[:, 2 * qw :],
        bias_kv,
        grad_wout,
        small[feat:width],
        join(0).T,
        join(1).T,
        join(2),
    )


def solution(mesh):
    return jax.shard_map(
        body,
        mesh=mesh,
        in_specs=(
            P(("dp", "col"), "row"),
            P("dp"),
            P("row"),
            P("row", "col"),
            P("col"),
            P("row", None),
            P(),
            P("col", "row"),
            P("row"),
            P("row", "col"),
            P("row", "col"),
            P("col", "row"),
            P(("dp", "col"), "row"),
        ),
        out_specs=(
            P(("dp", "col"), "row"),
            P(("dp", "col"), "row"),
            P("row"),
            P("row", "col"),
            P("col"),
            P("row", None),
            P(),
            P("col", "row"),
            P("row"),
            P("row", "col"),
            P("row", "col"),
            P("col", "row"),
        ),
        check_vma=False,
    )
```

```python
import functools

import jax
import jax.numpy as jnp
from jax import lax
from jax.experimental import pallas as pl
from jax.experimental.pallas import tpu as pltpu
from jax.sharding import PartitionSpec as P

HD = 128
SEQ_LEN = 1024
EPS = 1e-06
THETA = 1000000.0
NEG = -1e30
BF16 = jnp.bfloat16
F32 = jnp.float32
MIB = 1 << 20
SMALL_ROWS = 32
LITTLE = 1000
GRANT = 40


def dot_nn(left, right):
    return lax.dot_general(left, right, (((1,), (0,)), ((), ())), preferred_element_type=F32)


def dot_nt(left, right):
    return lax.dot_general(left, right, (((1,), (1,)), ((), ())), preferred_element_type=F32)


def dot_tn(left, right):
    return lax.dot_general(left, right, (((0,), (0,)), ((), ())), preferred_element_type=F32)


def params(mib):
    return pltpu.CompilerParams(vmem_limit_bytes=mib * MIB)


def cost(flops, nbytes):
    return pl.CostEstimate(flops=int(flops), bytes_accessed=int(nbytes), transcendentals=0)


def rope(value, cosine, sine):
    return value * cosine + pltpu.roll(value, HD // 2, 1) * sine


def qkv_kernel(cols, own, *refs):
    r_ref, refs = refs[0], refs[1:]
    xa, refs = refs[:cols], refs[cols:]
    xb, refs = refs[:cols], refs[cols:]
    gain, wa, wb, bias, cosine, sine, x_out, n_out, q_out, kv_out = refs
    feat = xa[0].shape[1]
    for j in range(cols):
        rows = pl.ds(j * own, own)
        a = xa[j][...].astype(F32)
        b = xb[j][...].astype(F32)
        total = jnp.sum(a * a, axis=1, keepdims=True) + jnp.sum(b * b, axis=1, keepdims=True)
        inverse = lax.rsqrt(total / (2 * feat) + EPS)
        x_out[rows, :feat] = xa[j][...]
        x_out[rows, feat:] = xb[j][...]
        n_out[rows, :feat] = (a * inverse * gain[:, :feat]).astype(BF16)
        n_out[rows, feat:] = (b * inverse * gain[:, feat:]).astype(BF16)
    qkv = dot_nn(n_out[:, :feat], wa[...]) + dot_nn(n_out[:, feat:], wb[...]) + bias[...]
    qw = q_out.shape[1]
    for h in range(qw // HD):
        at = slice(h * HD, (h + 1) * HD)
        q_out[:, at] = rope(qkv[:, at], cosine[...], sine[...]).astype(BF16)
    kv_out[:, :HD] = rope(qkv[:, qw : qw + HD], cosine[...], sine[...]).astype(BF16)
    kv_out[:, HD:] = qkv[:, qw + HD :].astype(BF16)


def qkv_call(r, xa, xb, gain, wa, wb, bias, cosine, sine, qw, own):
    cols = len(xa)
    feat = xa[0].shape[1]
    tokens = own * cols
    whole = lambda v: pl.BlockSpec(v.shape, lambda i, r: (0,) * v.ndim)
    rest = [gain, wa, wb, bias, cosine, sine]
    outs = [
        jax.ShapeDtypeStruct((tokens, 2 * feat), BF16),
        jax.ShapeDtypeStruct((tokens, 2 * feat), BF16),
        jax.ShapeDtypeStruct((tokens, qw), BF16),
        jax.ShapeDtypeStruct((tokens, 2 * HD), BF16),
    ]
    return pl.pallas_call(
        functools.partial(qkv_kernel, cols, own),
        grid_spec=pltpu.PrefetchScalarGridSpec(
            num_scalar_prefetch=1,
            grid=(1,),
            in_specs=[pl.BlockSpec((own, feat), lambda i, r: (r[0], 0))] * (2 * cols)
            + [whole(v) for v in rest],
            out_specs=[whole(o) for o in outs],
        ),
        out_shape=outs,
        compiler_params=params(40),
        cost_estimate=cost(LITTLE, LITTLE),
        name="qkv",
    )(r, *xa, *xb, *rest)


def softmax(q, k, visible, scaling):
    scores = jnp.where(visible, dot_nt(q, k) * scaling, NEG)
    e = jnp.exp(scores - jnp.max(scores, axis=1, keepdims=True))
    return e * (1.0 / jnp.sum(e, axis=1, keepdims=True))


def visibility(qpos, kpos, prefix_ref):
    return (kpos <= qpos) | (kpos < prefix_ref[0])


def attend_kernel(scaling, prefix, q, kv_a, kv_b, qpos, kpos, out):
    visible = visibility(qpos[...], kpos[...], prefix)
    keys = jnp.concatenate([kv_a[:, :HD], kv_b[:, :HD]], axis=0)
    values = jnp.concatenate([kv_a[:, HD:], kv_b[:, HD:]], axis=0)
    for h in range(q.shape[1] // HD):
        at = slice(h * HD, (h + 1) * HD)
        weights = softmax(q[:, at], keys, visible, scaling)
        out[:, at] = dot_nn(weights.astype(BF16), values).astype(BF16)


def attend_call(prefix, q, kv_a, kv_b, qpos, kpos, block):
    tokens, qw = q.shape
    whole = lambda v: pl.BlockSpec(v.shape, lambda i, p: (0,) * v.ndim)
    part = lambda v: pl.BlockSpec((block, v.shape[1]), lambda i, p: (i, 0))
    return pl.pallas_call(
        functools.partial(attend_kernel, HD**-0.5),
        grid_spec=pltpu.PrefetchScalarGridSpec(
            num_scalar_prefetch=1,
            grid=(tokens // block,),
            in_specs=[part(q), whole(kv_a), whole(kv_b), part(qpos), whole(kpos)],
            out_specs=part(q),
        ),
        out_shape=jax.ShapeDtypeStruct(q.shape, BF16),
        compiler_params=params(32),
        cost_estimate=cost(LITTLE, LITTLE),
        name="attend",
    )(prefix, q, kv_a, kv_b, qpos, kpos)


def out_kernel(cols, own, side, x_at, *refs):
    att, refs = refs[:cols], refs[cols:]
    wa, wb, refs = refs[0], refs[1], refs[2:]
    pa, refs = refs[:side], refs[side:]
    pb, refs = refs[:side], refs[side:]
    xa, xb, gain, resid_out, na, nb, acc_a, acc_b, whole_a, whole_b = refs
    step, steps = pl.program_id(0), pl.num_programs(0)
    chunk = xa.shape[1]
    feat = chunk * steps
    quarter = wa.shape[0] // side

    rolled = []
    for j in range(cols):
        tiles = [att[j][((i - j) % cols) * own : ((i - j) % cols + 1) * own, :] for i in range(cols)]
        rolled.append(jnp.concatenate(tiles, axis=0))
    at = pl.ds(pl.multiple_of(step * chunk, 128), chunk)
    for parts, whole in ((pa, whole_a), (pb, whole_b)):
        for i in range(side):
            place = lax.rem(x_at[0] + i, side) * quarter
            for j in range(cols - 1):
                rows = parts[i][j * quarter : (j + 1) * quarter, :]
                whole[j, pl.ds(pl.multiple_of(place, 32), quarter), :] = rows
    for x, w, whole, acc in ((xa, wa, whole_a, acc_a), (xb, wb, whole_b, acc_b)):
        total = x[...].astype(F32) + dot_nn(rolled[0], w[...])
        for j in range(1, cols):
            total = total + dot_nn(rolled[j], whole[j - 1])
        acc[:, at] = total

    @pl.when(step == steps - 1)
    def _():
        a, b = acc_a[...], acc_b[...]
        total = jnp.sum(a * a, axis=1, keepdims=True) + jnp.sum(b * b, axis=1, keepdims=True)
        inverse = lax.rsqrt(total / (2 * feat) + EPS)
        na[...] = (a * inverse * gain[:, :feat]).astype(BF16)
        nb[...] = (b * inverse * gain[:, feat:]).astype(BF16)
        resid_out[:, :feat] = acc_a[:own, :]
        resid_out[:, feat:] = acc_b[:own, :]


def out_call(x_at, att, wa, wb, pa, pb, x, gain, own):
    cols, side = len(att), len(pa)
    tokens, qw = att[0].shape
    feat = wa.shape[1]
    steps = 3
    chunk = feat // steps
    whole = lambda v: pl.BlockSpec(v.shape, lambda i, p: (0,) * v.ndim)
    part = lambda v: pl.BlockSpec((v.shape[0], chunk), lambda i, p: (0, i))
    outs = [
        jax.ShapeDtypeStruct((own, 2 * feat), F32),
        jax.ShapeDtypeStruct((tokens, feat), BF16),
        jax.ShapeDtypeStruct((tokens, feat), BF16),
    ]
    return pl.pallas_call(
        functools.partial(out_kernel, cols, own, side),
        grid_spec=pltpu.PrefetchScalarGridSpec(
            num_scalar_prefetch=1,
            grid=(steps,),
            in_specs=[whole(a) for a in att]
            + [part(v) for v in (wa, wb, *pa, *pb)]
            + [part(x), pl.BlockSpec((tokens, chunk), lambda i, p: (0, steps + i)), whole(gain)],
            out_specs=[whole(o) for o in outs],
            scratch_shapes=[
                pltpu.VMEM((tokens, feat), F32),
                pltpu.VMEM((tokens, feat), F32),
                pltpu.VMEM((cols - 1, qw, chunk), BF16),
                pltpu.VMEM((cols - 1, qw, chunk), BF16),
            ],
        ),
        out_shape=outs,
        compiler_params=params(40),
        cost_estimate=cost(LITTLE, LITTLE),
        name="out_norm",
    )(x_at, *att, wa, wb, *pa, *pb, x, x, gain)


def assemble_kernel(cols, own, r_ref, *refs):
    ca, cb, (out_a, out_b) = refs[:cols], refs[cols : 2 * cols], refs[2 * cols :]
    tokens = cols * own
    first = ca[0].shape[0] - 2 * own
    r = r_ref[0]
    for j in range(cols):
        for src, out in ((ca[j], out_a), (cb[j], out_b)):
            out[j * own : (j + 1) * own, :] = src[pl.ds(first + r * own, own), :]
            out[tokens + j * own : tokens + (j + 1) * own, :] = src[
                pl.ds(first + (1 - r) * own, own), :
            ]


def assemble_call(r, ca, cb, own):
    cols = len(ca)
    out = jax.ShapeDtypeStruct((2 * cols * own, ca[0].shape[1]), BF16)
    return pl.pallas_call(
        functools.partial(assemble_kernel, cols, own),
        in_specs=[pl.BlockSpec(memory_space=pltpu.SMEM)]
        + [pl.BlockSpec(memory_space=pltpu.VMEM)] * (2 * cols),
        out_specs=[pl.BlockSpec(memory_space=pltpu.VMEM)] * 2,
        out_shape=[out, out],
        compiler_params=params(24),
        cost_estimate=cost(LITTLE, LITTLE),
        name="assemble",
    )(r, *ca, *cb)


def gated_kernel(na, nb, ga, gb, ua, ub, mixed, to_gate, to_up):
    gate = dot_nt(ga[...], na[...]) + dot_nt(gb[...], nb[...])
    up = dot_nt(ua[...], na[...]) + dot_nt(ub[...], nb[...])
    s = 0.5 * jnp.tanh(0.5 * gate) + 0.5
    silu = gate * s
    mixed[...] = (silu * up).astype(BF16)
    to_gate[...] = (up * (s + silu * (1.0 - s))).astype(BF16)
    to_up[...] = silu.astype(BF16)


def hidden_grad_kernel(ca, cb, da, db, to_gate, to_up, grad_gate, grad_up):
    grad_mixed = dot_nt(da[...], ca[...]) + dot_nt(db[...], cb[...])
    grad_gate[...] = (grad_mixed * to_gate[...].astype(F32)).astype(BF16)
    grad_up[...] = (grad_mixed * to_up[...].astype(F32)).astype(BF16)


def gated_call(r, na, nb, kept, got, chunk):
    tokens, feat = na.shape
    part = got.shape[1]
    steps = part // chunk
    act = pl.BlockSpec((tokens, feat), lambda i, r: (0, 0))
    mine = pl.BlockSpec((chunk, feat), lambda i, r: (r[0] * steps + i, 0))
    other = lambda k: pl.BlockSpec((None, chunk, feat), lambda i, r: (k, i, 0))
    return pl.pallas_call(
        lambda r, *refs: gated_kernel(*refs),
        grid_spec=pltpu.PrefetchScalarGridSpec(
            num_scalar_prefetch=1,
            grid=(steps,),
            in_specs=[act, act, mine, other(0), mine, other(1)],
            out_specs=[pl.BlockSpec((chunk, tokens), lambda i, r: (i, 0))] * 3,
        ),
        out_shape=[jax.ShapeDtypeStruct((part, tokens), BF16)] * 3,
        compiler_params=params(GRANT),
        cost_estimate=cost(LITTLE, LITTLE),
        name="gated",
    )(r, na, nb, kept[0], got, kept[1], got)


def hidden_grad_call(r, ca, cb, half, kept, got, to_gate, to_up, chunk):
    part, tokens = to_gate.shape
    feat = ca.shape[1]
    steps = part // chunk
    cot = pl.BlockSpec((tokens, feat), lambda i, r: (half, 0))
    hid = pl.BlockSpec((chunk, tokens), lambda i, r: (i, 0))
    return pl.pallas_call(
        lambda r, *refs: hidden_grad_kernel(*refs),
        grid_spec=pltpu.PrefetchScalarGridSpec(
            num_scalar_prefetch=1,
            grid=(steps,),
            in_specs=[
                cot,
                cot,
                pl.BlockSpec((chunk, feat), lambda i, r: (r[0] * steps + i, 0)),
                pl.BlockSpec((None, chunk, feat), lambda i, r: (2, i, 0)),
                hid,
                hid,
            ],
            out_specs=[hid, hid],
        ),
        out_shape=[jax.ShapeDtypeStruct((part, tokens), BF16)] * 2,
        compiler_params=params(GRANT),
        cost_estimate=cost(LITTLE, LITTLE),
        name="hidden_grads",
    )(r, ca, cb, kept[2], got, to_gate, to_up)


def wgrad_kernel(pairs, act_own, act_other, *refs):
    own, other, out = refs[:pairs], refs[pairs : 2 * pairs], refs[2 * pairs]
    for k in range(pairs):
        total = dot_nn(own[k][...], act_own[...]) + dot_nn(other[k][...], act_other[...])
        out[k] = total.astype(BF16)


def wgrad_call(act_own, act_other, other_block, hidden_own, hidden_other, chunk):
    pairs = len(hidden_own)
    part, tokens = hidden_own[0].shape
    feat = act_own.shape[1]
    hid = pl.BlockSpec((chunk, tokens), lambda i: (i, 0))
    return pl.pallas_call(
        functools.partial(wgrad_kernel, pairs),
        grid=(part // chunk,),
        in_specs=[
            pl.BlockSpec((tokens, feat), lambda i: (0, 0)),
            pl.BlockSpec((tokens, feat), lambda i: (other_block, 0)),
        ]
        + [hid] * (2 * pairs),
        out_specs=pl.BlockSpec((pairs, chunk, feat), lambda i: (0, i, 0)),
        out_shape=jax.ShapeDtypeStruct((pairs, part, feat), BF16),
        compiler_params=params(GRANT),
        cost_estimate=cost(LITTLE, LITTLE),
        name="weight_grads",
    )(act_own, act_other, *hidden_own, *hidden_other)


def back_kernel(pairs, *refs):
    hidden, refs = (refs[:pairs], refs[pairs : 2 * pairs]), refs[2 * pairs :]
    wa, refs = refs[:pairs], refs[pairs:]
    wb, outs = refs[:pairs], refs[pairs:]
    for half in (1, 0):
        for w, out in ((wa, outs[2 * half]), (wb, outs[2 * half + 1])):
            total = dot_tn(hidden[half][0][...], w[0][...])
            for i in range(1, pairs):
                total = total + dot_tn(hidden[half][i][...], w[i][...])
            out[...] = total.astype(out.dtype)


def back_call(r, own, other, kept, got, first):
    pairs = len(own)
    part, tokens = own[0].shape
    feat = got.shape[2]
    out = jax.ShapeDtypeStruct((tokens, feat), BF16)
    of_other = lambda k: pl.BlockSpec((None, part, feat), lambda i, r: (first + k, 0, 0))
    return pl.pallas_call(
        lambda r, *refs: back_kernel(pairs, *refs),
        grid_spec=pltpu.PrefetchScalarGridSpec(
            num_scalar_prefetch=1,
            grid=(1,),
            in_specs=[pl.BlockSpec((part, tokens), lambda i, r: (0, 0))] * (2 * pairs)
            + [pl.BlockSpec((part, feat), lambda i, r: (r[0], 0))] * pairs
            + [of_other(k) for k in range(pairs)],
            out_specs=[pl.BlockSpec((tokens, feat), lambda i, r: (0, 0))] * 4,
        ),
        out_shape=[out] * 4,
        compiler_params=params(GRANT),
        cost_estimate=cost(LITTLE, LITTLE),
        name="back_in",
    )(r, *own, *other, *kept, *([got] * pairs))


def attend_back_kernel(
    scaling, own, prefix, *refs
):
    (gr, wa, wb, q, kv_a, kv_b, qpos, kpos, cosine, sine,
     low_out, sum_out, gkv_own, gkv_send, gk, gv, ga_s) = refs
    step, steps = pl.program_id(0), pl.num_programs(0)
    feat = wa.shape[1]
    visible = visibility(qpos[...], kpos[...], prefix)
    keys = jnp.concatenate([kv_a[:, :HD], kv_b[:, :HD]], axis=0)
    values = jnp.concatenate([kv_a[:, HD:], kv_b[:, HD:]], axis=0)
    ga_s[...] = (dot_nt(gr[:, :feat], wa[...]) + dot_nt(gr[:, feat:], wb[...])).astype(BF16)

    @pl.when(step == 0)
    def _():
        gk[...] = jnp.zeros_like(gk)
        gv[...] = jnp.zeros_like(gv)
        sum_out[...] = jnp.zeros_like(sum_out)

    for h in range(q.shape[1] // HD):
        at = slice(h * HD, (h + 1) * HD)
        weights = softmax(q[:, at], keys, visible, scaling)
        grad_att = ga_s[:, at]
        gw = dot_nt(grad_att, values)
        inner = jnp.sum(weights * gw, axis=1, keepdims=True)
        gs = (weights * (gw - inner)).astype(BF16)
        gk[...] += dot_tn(gs, q[:, at])
        gv[...] += dot_tn(weights.astype(BF16), grad_att)
        grad_q = dot_nn(gs, keys) * scaling
        grad_q = rope(grad_q, cosine[...], sine[...])
        low_out[:, at] = grad_q.astype(BF16)
        sum_out[:, at] += jnp.sum(grad_q, axis=0, keepdims=True)

    @pl.when(step == steps - 1)
    def _():
        half = gk.shape[0] // 2
        gkv_own[:, :HD] = gk[:half, :] * scaling
        gkv_own[:, HD:] = gv[:half, :]
        gkv_send[:, :HD] = (gk[half:, :] * scaling).astype(BF16)
        gkv_send[:, HD:] = gv[half:, :].astype(BF16)


def attend_back_call(prefix, gr, wa, wb, q, kv_a, kv_b, qpos, kpos, cosine, sine, block):
    tokens, qw = q.shape
    whole = lambda v: pl.BlockSpec(v.shape, lambda i, p: (0,) * v.ndim)
    part = lambda v: pl.BlockSpec((block, v.shape[1]), lambda i, p: (i, 0))
    outs = [
        jax.ShapeDtypeStruct((tokens, qw), BF16),
        jax.ShapeDtypeStruct((1, qw), F32),
        jax.ShapeDtypeStruct((tokens, 2 * HD), F32),
        jax.ShapeDtypeStruct((tokens, 2 * HD), BF16),
    ]
    keys = 2 * tokens
    return pl.pallas_call(
        functools.partial(attend_back_kernel, HD**-0.5, block),
        grid_spec=pltpu.PrefetchScalarGridSpec(
            num_scalar_prefetch=1,
            grid=(tokens // block,),
            in_specs=[
                part(gr), whole(wa), whole(wb), part(q), whole(kv_a), whole(kv_b),
                part(qpos), whole(kpos), part(cosine), part(sine),
            ],
            out_specs=[part(outs[0]), whole(outs[1]), whole(outs[2]), whole(outs[3])],
            scratch_shapes=[
                pltpu.VMEM((keys, HD), F32),
                pltpu.VMEM((keys, HD), F32),
                pltpu.VMEM((block, qw), BF16),
            ],
        ),
        out_shape=outs,
        compiler_params=params(40),
        cost_estimate=cost(LITTLE, LITTLE),
        name="attend_back",
    )(prefix, gr, wa, wb, q, kv_a, kv_b, qpos, kpos, cosine, sine)


def qkv_back_kernel(own, got, query_low, cosine, sine, wa, wb, low, sums, back):
    qw = query_low.shape[1]
    total = own[...] + got[...].astype(F32)
    key = rope(total[:, :HD], cosine[...], sine[...])
    value = total[:, HD:]
    sums[:, :HD] = jnp.sum(key, axis=0, keepdims=True)
    sums[:, HD:] = jnp.sum(value, axis=0, keepdims=True)
    low[:, :qw] = query_low[...]
    low[:, qw : qw + HD] = key.astype(BF16)
    low[:, qw + HD :] = value.astype(BF16)
    feat = wa.shape[0]
    back[:, :feat] = dot_nt(low[...], wa[...]).astype(BF16)
    back[:, feat:] = dot_nt(low[...], wb[...]).astype(BF16)


def qkv_back_call(own, got, query_low, cosine, sine, wa, wb):
    tokens = own.shape[0]
    feat, columns = wa.shape
    return pl.pallas_call(
        qkv_back_kernel,
        out_shape=[
            jax.ShapeDtypeStruct((tokens, columns), BF16),
            jax.ShapeDtypeStruct((1, 2 * HD), F32),
            jax.ShapeDtypeStruct((tokens, 2 * feat), BF16),
        ],
        compiler_params=params(32),
        cost_estimate=cost(LITTLE, LITTLE),
        name="qkv_back",
    )(own, got, query_low, cosine, sine, wa, wb)


def rest_kernel(n1, low, attended, grad, in_a, in_b, out_a, out_b):
    feat = n1.shape[1] // 2
    in_b[...] = dot_tn(n1[:, feat:], low[...]).astype(BF16)
    out_b[...] = dot_tn(attended[...], grad[:, feat:]).astype(BF16)
    in_a[...] = dot_tn(n1[:, :feat], low[...]).astype(BF16)
    out_a[...] = dot_tn(attended[...], grad[:, :feat]).astype(BF16)


def rest_call(n1, low, attended, grad):
    feat = n1.shape[1] // 2
    into = jax.ShapeDtypeStruct((feat, low.shape[1]), BF16)
    out = jax.ShapeDtypeStruct((attended.shape[1], feat), BF16)
    return pl.pallas_call(
        rest_kernel,
        out_shape=[into, into, out, out],
        compiler_params=params(32),
        cost_estimate=cost(LITTLE, LITTLE),
        name="rest",
    )(n1, low, attended, grad)


def join_kernel(r_ref, kept, got, out):
    part = kept.shape[0]

    @pl.when(r_ref[0] == 0)
    def _():
        out[:part, :] = kept[...].astype(F32)
        out[part:, :] = got[...].astype(F32)

    @pl.when(r_ref[0] != 0)
    def _():
        out[:part, :] = got[...].astype(F32)
        out[part:, :] = kept[...].astype(F32)


def join_call(r, kept, got, which, chunk):
    part, feat = kept.shape[1:]
    half = pl.BlockSpec((None, part, chunk), lambda i, r: (which, 0, i))
    return pl.pallas_call(
        join_kernel,
        grid_spec=pltpu.PrefetchScalarGridSpec(
            num_scalar_prefetch=1,
            grid=(feat // chunk,),
            in_specs=[half, half],
            out_specs=pl.BlockSpec((2 * part, chunk), lambda i, r: (0, i)),
        ),
        out_shape=jax.ShapeDtypeStruct((2 * part, feat), F32),
        compiler_params=params(32),
        cost_estimate=cost(LITTLE, LITTLE),
        name="join",
    )(r, kept, got)


def pack_kernel(one, two, bias_kv, bias_query, mine, sent):
    feat = one.shape[1] // 2
    for out, first in ((mine, 0), (sent, feat)):
        out[...] = jnp.zeros_like(out)
        at = 0
        for vector, start, size in (
            (one, first, feat),
            (two, first, feat),
            (bias_kv, 0, bias_kv.shape[1]),
            (bias_query, 0, bias_query.shape[1]),
        ):
            for k in range(size // HD):
                out[at : at + 1, :] = vector[:, start + k * HD : start + (k + 1) * HD]
                at += 1


def pack_call(one, two, bias_kv, bias_query):
    out = jax.ShapeDtypeStruct((SMALL_ROWS, HD), F32)
    return pl.pallas_call(
        pack_kernel,
        out_shape=[out, out],
        cost_estimate=cost(LITTLE, LITTLE),
        name="pack",
    )(one, two, bias_kv, bias_query)


def message_kernel(mine, got, rest, out, small):
    rows = rest.shape[0]
    total = mine[...] + got[...]
    small[...] = total
    out[:rows, :] = rest[:, rest.shape[1] - 2 * HD :]
    out[rows:, :HD] = total.astype(BF16)
    out[rows:, HD:] = jnp.zeros((SMALL_ROWS, HD), BF16)


def message_call(mine, got, rest):
    rows = rest.shape[0]
    return pl.pallas_call(
        message_kernel,
        out_shape=[
            jax.ShapeDtypeStruct((rows + SMALL_ROWS, 2 * HD), BF16),
            jax.ShapeDtypeStruct((SMALL_ROWS, HD), F32),
        ],
        cost_estimate=cost(LITTLE, LITTLE),
        name="message",
    )(mine, got, rest)


def head_sum_kernel(cols, heads, gain_rows, chip, *refs):
    messages, (small, rest, out_a, out_b, total) = refs[:cols], refs[cols:]
    rows, columns = rest.shape
    half = out_a.shape[1]
    share = cols // heads
    total[...] = jnp.zeros_like(total)
    total[:gain_rows, :] = sum(m[rows : rows + gain_rows, :HD].astype(F32) for m in messages)
    for head in range(heads):
        both = jnp.zeros((rows, 2 * HD), F32)
        bias = jnp.zeros((SMALL_ROWS, HD), F32)
        for j in range(cols):
            same = jnp.where(lax.rem(chip[0] + j, cols) // share == head, 1.0, 0.0)
            both = both + same * messages[j][:rows, :].astype(F32)
            bias = bias + same * messages[j][rows:, :HD].astype(F32)
        own_columns = columns - 2 * HD - half
        at = own_columns + head * HD
        out_b[:, at : at + HD] = both[:, :HD].astype(BF16)
        at += heads * HD
        out_b[:, at : at + HD] = both[:, HD:].astype(BF16)
        for k in range(2):
            row = gain_rows + k * heads + head
            total[row : row + 1, :] = bias[gain_rows + k : gain_rows + k + 1, :]
    queries = small[gain_rows + 2 :, :]
    first = gain_rows + 2 * heads
    total[first:, :] = queries[: SMALL_ROWS - first, :]
    out_a[:rows, :] = rest[:, :half]
    out_b[:, : columns - 2 * HD - half] = rest[:, half : columns - 2 * HD]
    out_a[rows:, :HD] = total[...].astype(BF16)
    out_a[rows:, HD:] = jnp.zeros((SMALL_ROWS, half - HD), BF16)


def head_sum_call(chip, messages, small, rest, heads, gain_rows):
    rows, columns = rest.shape
    half = (columns + 2 * HD * (heads - 1)) // 2
    vmem = pl.BlockSpec(memory_space=pltpu.VMEM)
    return pl.pallas_call(
        functools.partial(head_sum_kernel, len(messages), heads, gain_rows),
        in_specs=[pl.BlockSpec(memory_space=pltpu.SMEM)] + [vmem] * (len(messages) + 2),
        out_specs=[vmem, vmem],
        out_shape=[
            jax.ShapeDtypeStruct((rows + SMALL_ROWS, half), BF16),
            jax.ShapeDtypeStruct((rows, half), BF16),
        ],
        scratch_shapes=[pltpu.VMEM((SMALL_ROWS, HD), F32)],
        cost_estimate=cost(LITTLE, LITTLE),
        name="head_sums",
    )(chip, *messages, small, rest)


def order_kernel(side, places, *refs):
    first, second, (out_a, out_b) = refs[:side], refs[side : 2 * side], refs[2 * side :]
    rows = second[0].shape[0]
    for i in range(side):
        at = lax.rem(places[1] + i, side) * rows
        out_a[pl.ds(pl.multiple_of(at, 16), rows), :] = first[i][:rows, :]
        at = lax.rem(places[0] + i, side) * rows
        out_b[pl.ds(pl.multiple_of(at, 16), rows), :] = second[i][...]
    total = sum(v[rows:, :].astype(F32) for v in first)
    out_a[side * rows :, :] = total.astype(BF16)


def order_call(places, first, second):
    side = len(first)
    rows, half = second[0].shape
    vmem = pl.BlockSpec(memory_space=pltpu.VMEM)
    return pl.pallas_call(
        functools.partial(order_kernel, side),
        in_specs=[pl.BlockSpec(memory_space=pltpu.SMEM)] + [vmem] * (2 * side),
        out_specs=[vmem, vmem],
        out_shape=[
            jax.ShapeDtypeStruct((side * rows + SMALL_ROWS, half), BF16),
            jax.ShapeDtypeStruct((side * rows, half), BF16),
        ],
        cost_estimate=cost(LITTLE, LITTLE),
        name="order",
    )(places, *first, *second)


def finish_kernel(side, heads, places, *refs):
    first, second, outs = refs[:side], refs[side : 2 * side], refs[2 * side :]
    w_out, w_query, w_keyval, one, two, bias_kv, bias_query, total = outs
    qw = w_query.shape[1]
    block, half = second[0].shape
    rows = block // side
    count = qw // block
    for i in range(side):
        at = lax.rem(places[0] + i, side)
        place = pl.ds(pl.multiple_of(at * block, 16), block)
        w_query[place, : half - qw] = first[i][:block, qw:].astype(F32)
        values = first[i][:block, :qw].astype(F32)

        @pl.when(at < count)
        def _():
            w_out[pl.ds(pl.multiple_of(at * block, 16), block), :qw] = values

        @pl.when(at >= count)
        def _():
            w_out[pl.ds(pl.multiple_of((at - count) * block, 16), block), qw:] = values

        at = lax.rem(places[1] + i, side)
        for k in range(side):
            place = pl.ds(pl.multiple_of(k * block + at * rows, 16), rows)
            piece = second[i][k * rows : (k + 1) * rows, :].astype(F32)
            w_query[place, half - qw :] = piece[:, : 2 * qw - half]
            w_keyval[place, :] = piece[:, 2 * qw - half :]
    total[...] = sum(v[block:, :HD].astype(F32) for v in first)
    at = 0
    for out in (one, two, bias_kv, bias_query):
        out[...] = total[at : at + out.shape[0], :]
        at += out.shape[0]


def finish_call(places, first, second, qw, feat, heads):
    side = len(first)
    vmem = pl.BlockSpec(memory_space=pltpu.VMEM)
    shapes = [(qw, feat), (feat, qw), (feat, 2 * heads * HD)]
    shapes += [(feat // HD, HD), (feat // HD, HD), (2 * heads, HD), (qw // HD, HD)]
    return pl.pallas_call(
        functools.partial(finish_kernel, side, heads),
        in_specs=[pl.BlockSpec(memory_space=pltpu.SMEM)] + [vmem] * (2 * side),
        out_specs=[vmem] * len(shapes),
        out_shape=[jax.ShapeDtypeStruct(s, F32) for s in shapes],
        scratch_shapes=[pltpu.VMEM((SMALL_ROWS, HD), F32)],
        compiler_params=params(32),
        cost_estimate=cost(LITTLE, LITTLE),
        name="finish",
    )(places, *first, *second)
def after(value, *others):
    return lax.optimization_barrier((value,) + others)[0]


def swap_rows(value):
    return lax.ppermute(value, "row", [(0, 1), (1, 0)])


def from_col(value, offset):
    count = lax.axis_size("col")
    return lax.ppermute(value, "col", [((i + offset) % count, i) for i in range(count)])


def gather_col(value):
    third, first = from_col(value, -1), from_col(value, 1)
    return [value, first, from_col(value, 2), third]


def gather_col_ring(value, behind=()):
    third, first = from_col(value, -1), from_col(value, 1)
    middle = value.shape[0] // 2
    upper = from_col(after(first, *behind)[:middle], 1)
    lower = from_col(after(third, *behind)[middle:], -1)
    return [value, first, jnp.concatenate([upper, lower], axis=0), third]


def scatter_col(blocks, behind=()):
    third, first, second = (
        from_col(blocks[3], 1),
        from_col(blocks[1], -1),
        from_col(blocks[2], -2),
    )
    total = blocks[0].astype(F32)
    for part in (first, second, third):
        total = total + after(part, *behind).astype(F32)
    return total


def halves(value):
    middle = value.shape[-1] // 2
    return value[..., :middle], value[..., middle:]


def roll_blocks(value, shift, axis):
    size = value.shape[axis]
    twice = jnp.concatenate([value, value], axis=axis)
    return lax.dynamic_slice_in_dim(twice, shift, size, axis)


def shift_dp(value, along, offset, side):
    pairs = []
    for z in range(side):
        for x in range(side):
            if along == "z":
                source = ((z + offset) % side) * side + x
            else:
                source = z * side + (x + offset) % side
            pairs.append((source, z * side + x))
    return lax.ppermute(value, "dp", pairs)


def scatter_dp(value, along, at, side):
    value = jnp.pad(value, ((0, -value.shape[0] % (8 * side)), (0, 0)))
    rows = value.shape[0] // side
    block = lambda j: lax.dynamic_slice_in_dim(value, ((at + j) % side) * rows, rows, 0)
    got = [shift_dp(block(j), along, -j, side) for j in (1, side - 1, 2)]
    total = block(0).astype(F32)
    for part in got:
        total = total + part.astype(F32)
    return total.astype(BF16)


def gather_dp_ring(value, along, side):
    third, first = shift_dp(value, along, -1, side), shift_dp(value, along, 1, side)
    middle = value.shape[0] // 2
    upper = shift_dp(first[:middle], along, 1, side)
    lower = shift_dp(third[middle:], along, -1, side)
    return [value, first, jnp.concatenate([upper, lower], axis=0), third]


def gather_dp(value, along, side):
    got = {j: shift_dp(value, along, j, side) for j in (1, side - 1, 2)}
    return [value] + [got[j] for j in range(1, side)]


def body(
    layer_input,
    prefix,
    gain_one,
    w_query,
    b_query,
    w_keyval,
    b_keyval,
    w_out,
    gain_two,
    w_gate,
    w_up,
    w_down,
    cotangent,
):
    cols = lax.axis_size("col")
    groups = lax.axis_size("dp")
    side = int(round(groups**0.5))
    r = lax.axis_index("row")
    c = lax.axis_index("col")
    dp = lax.axis_index("dp")
    z_at, x_at = dp // side, dp % side
    core = r.astype(jnp.int32).reshape(1)
    rows_in, feat = layer_input.shape
    own = rows_in // 2
    tokens = own * cols
    width = 2 * feat
    qw = w_query.shape[1]
    kvw = w_keyval.shape[1] // 2
    share = cols // (kvw // HD)
    kv_head = c // share
    ff = w_gate.shape[1]
    part = ff // 2

    quarter = qw // side
    wo_parts = lax.dynamic_slice_in_dim(w_out, x_at * quarter, quarter, 0)
    wo_parts = gather_col_ring(wo_parts)
    x_a = gather_col_ring(layer_input, (wo_parts[1], wo_parts[3]))
    wo_parts = wo_parts[1:]
    wo_parts = gather_dp_ring(jnp.concatenate(wo_parts, axis=0), "x", side)

    key_start = kv_head * HD
    w_qkv_a = jnp.concatenate(
        [
            w_query,
            lax.dynamic_slice_in_dim(w_keyval, key_start, HD, 1),
            lax.dynamic_slice_in_dim(w_keyval, kvw + key_start, HD, 1),
        ],
        axis=1,
    )
    bias = jnp.concatenate(
        [
            b_query,
            lax.dynamic_slice_in_dim(b_keyval, key_start, HD, 0),
            lax.dynamic_slice_in_dim(b_keyval, kvw + key_start, HD, 0),
        ]
    ).astype(F32)[None]
    w_qkv_b = swap_rows(w_qkv_a)
    gains_a = jnp.stack([gain_one, gain_two])
    gains = jnp.concatenate([gains_a, swap_rows(gains_a)], axis=1).astype(F32)
    gain_one_f, gain_two_f = gains[:1], gains[1:]

    kept = [w_gate.T, w_up.T, w_down]
    sent = [
        lax.dynamic_slice_in_dim(after(w, x_a[1], x_a[3]), (1 - r) * part, part, 0)
        for w in kept
    ]
    sent = jnp.stack(sent)

    block_first = rows_in * ((c + jnp.arange(cols, dtype=jnp.int32)) % cols)
    inside = jnp.arange(own, dtype=jnp.int32)
    pos_own = ((block_first[:, None] + own * r + inside[None]) % SEQ_LEN).reshape(-1)
    pos_other = ((block_first[:, None] + own * (1 - r) + inside[None]) % SEQ_LEN).reshape(-1)
    query_pos = pos_own[:, None]
    key_pos = jnp.concatenate([pos_own, pos_other])[None, :]
    frequency = THETA ** (-jnp.arange(0, HD // 2, dtype=F32) * 2.0 / HD)
    angle = pos_own.astype(F32)[:, None] * frequency[None, :]
    cosine, sine = jnp.cos(angle), jnp.sin(angle)
    cosine = jnp.concatenate([cosine, cosine], axis=1)
    sine_to = jnp.concatenate([-sine, sine], axis=1)
    sine_back = jnp.concatenate([sine, -sine], axis=1)

    ready = (cosine, sine_to, sine_back, query_pos, key_pos, w_qkv_b, gains, bias, sent)
    x_b = [swap_rows(v) for v in x_a[:2]]
    x_b += [swap_rows(after(x_a[2], *ready)), swap_rows(x_a[3])]
    x_full, normed_one, query, kv_own = qkv_call(
        core, x_a, x_b, gain_one_f, w_qkv_a, w_qkv_b, bias, cosine, sine_to, qw, own
    )
    kv_other = swap_rows(kv_own)
    wo_parts_b = [swap_rows(v) for v in wo_parts]
    wo_a, wo_b = w_out, swap_rows(w_out)
    query = after(query, wo_b, wo_parts_b[0], wo_parts_b[1], wo_parts_b[3])
    attended = attend_call(prefix, query, kv_own, kv_other, query_pos, key_pos, tokens)
    got = swap_rows(after(sent, attended))
    att = gather_col_ring(attended, (got,))

    c_a = gather_col_ring(after(cotangent, att[1], att[3]))
    x_full = after(x_full, c_a[1], c_a[3])
    resid, n2_a, n2_b = out_call(
        x_at.astype(jnp.int32).reshape(1), att, wo_a, wo_b, wo_parts, wo_parts_b, x_full,
        gain_two_f, own,
    )
    n2_other_b, n2_other_a = swap_rows(n2_a), swap_rows(n2_b)


    gated_own = gated_call(core, n2_a, n2_b, kept, got, part // 2)
    gated_other = gated_call(core, n2_other_a, n2_other_b, kept, got, part // 2)

    c_b = [swap_rows(after(v, gated_own[0])) for v in c_a]
    cot_a, cot_b = assemble_call(after(core, gated_other[0]), c_a, c_b, own)

    def hidden_grads(half, gated):
        grads = hidden_grad_call(
            core, cot_a, cot_b, half, kept, got, gated[1], gated[2], part // 2
        )
        return [gated[0], *grads]

    hid_own = hidden_grads(0, gated_own)
    hid_other = hidden_grads(1, gated_other)

    def weight_grads(n_own, n_other, cot, own, other):
        return [
            wgrad_call(n_own, n_other, 0, own[1:], other[1:], part // 2),
            wgrad_call(cot, cot, 1, own[:1], other[:1], part // 2),
        ]

    big_b = weight_grads(n2_b, n2_other_b, cot_b, hid_own, hid_other)
    big_a = weight_grads(n2_a, n2_other_a, cot_a, hid_own, hid_other)
    own_grads = (*big_a, *big_b)
    big = lax.psum(own_grads, "dp")

    def sum_cores(own_pair, other_pair):
        from_b, from_a = swap_rows(other_pair[0]), swap_rows(other_pair[1])
        a = own_pair[0].astype(F32) + from_a.astype(F32)
        b = own_pair[1].astype(F32) + from_b.astype(F32)
        return jnp.concatenate([a, b], axis=1).astype(BF16)

    def token_blocks(value):
        return [value[j * own : (j + 1) * own] for j in range(cols)]

    back_own = [after(v, *own_grads) for v in hid_own[1:]]
    terms = back_call(core, back_own, hid_other[1:], kept[:2], got, 0)
    grad_normed_two = scatter_col(token_blocks(sum_cores(terms[:2], terms[2:])))


    def norm_backward(grad, value, gain):
        inverse = lax.rsqrt(jnp.mean(value * value, axis=1, keepdims=True) + EPS)
        unit = value * inverse
        scaled = grad * gain
        mean_term = jnp.mean(scaled * unit, axis=1, keepdims=True)
        return inverse * (scaled - unit * mean_term), jnp.sum(grad * unit, axis=0, keepdims=True)

    grad_norm_two, grad_gain_two = norm_backward(grad_normed_two, resid, gain_two_f)
    cot_full = jnp.concatenate([cot_a[:own], cot_b[:own]], axis=1).astype(F32)
    grad_resid = cot_full + grad_norm_two
    resid_blocks = gather_col(grad_resid.astype(BF16))
    resid_low = jnp.concatenate(resid_blocks, axis=0)

    query_low, grad_b_query, gkv_own, gkv_sent = attend_back_call(
        prefix, resid_low, wo_a, wo_b, query, kv_own, kv_other,
        query_pos, key_pos, cosine, sine_back, tokens,
    )
    qkv_low, grad_b_kv, back_one = qkv_back_call(
        gkv_own, swap_rows(gkv_sent), query_low, cosine, sine_back, w_qkv_a, w_qkv_b
    )
    grad_normed_one = scatter_col(token_blocks(back_one))

    def exchange_out(value):
        mine, other = halves(value)
        other = swap_rows(other)
        return jnp.where(
            r == 0,
            jnp.concatenate([mine, other], axis=0),
            jnp.concatenate([other, mine], axis=0),
        )

    grad_norm_one, grad_gain_one = norm_backward(
        grad_normed_one, x_full[:own].astype(F32), gain_one_f
    )
    grad_input = exchange_out(grad_resid + grad_norm_one)

    mixed_other = after(hid_other[0], grad_normed_one)
    terms = back_call(core, hid_own[:1], [mixed_other], kept[2:], got, 2)
    down = token_blocks(sum_cores(terms[:2], terms[2:]))
    down = scatter_col([after(v, grad_normed_one) for v in down])
    output = exchange_out((resid + down).astype(BF16))

    in_a, in_b, out_a, out_b = rest_call(normed_one, qkv_low, attended, resid_low)
    rest = in_a.astype(F32) + swap_rows(in_b).astype(F32)
    grad_wout = out_a.astype(F32) + swap_rows(out_b).astype(F32)
    grad_wout = jnp.concatenate(halves(grad_wout), axis=0)
    rest = jnp.concatenate([grad_wout, rest], axis=1).astype(BF16)
    rest = scatter_dp(scatter_dp(rest, "x", x_at, side), "z", z_at, side)
    piece_rows = rest.shape[0]

    heads = kvw // HD
    big_got = [swap_rows(after(v, rest, output)) for v in big[2:]]
    mine, sent = pack_call(grad_gain_one, grad_gain_two, grad_b_kv, grad_b_query)
    message, small = message_call(mine, swap_rows(after(sent, big[0], rest, output)), rest)
    chip = c.astype(jnp.int32).reshape(1)
    first, second = head_sum_call(chip, gather_col(message), small, rest, heads, width // HD)
    places = jnp.stack([x_at, z_at]).astype(jnp.int32)
    grad_w_gate = join_call(core, big[0], big_got[0], 0, 256)
    grad_w_up = join_call(core, big[0], big_got[0], 1, 256)
    grad_w_down = join_call(core, big[1], big_got[1], 0, 256)
    first, second = gather_dp(first, "z", side), gather_dp(second, "x", side)
    places = after(places, grad_w_gate, grad_w_up)
    first, second = order_call(places, first, second)
    first, second = gather_dp(first, "x", side), gather_dp(second, "z", side)
    places = after(places, grad_w_down)
    grad_wout, grad_wq, grad_wkv, one, two, bias_kv, bias_query = finish_call(
        places, first, second, qw, feat, heads
    )

    return (
        output,
        grad_input,
        one.reshape(-1),
        grad_wq,
        bias_query.reshape(-1),
        grad_wkv,
        bias_kv.reshape(-1),
        grad_wout,
        two.reshape(-1),
        grad_w_gate.T,
        grad_w_up.T,
        grad_w_down,
    )


def solution(mesh):
    return jax.shard_map(
        body,
        mesh=mesh,
        in_specs=(
            P(("dp", "col"), "row"),
            P("dp"),
            P("row"),
            P("row", "col"),
            P("col"),
            P("row", None),
            P(),
            P("col", "row"),
            P("row"),
            P("row", "col"),
            P("row", "col"),
            P("col", "row"),
            P(("dp", "col"), "row"),
        ),
        out_specs=(
            P(("dp", "col"), "row"),
            P(("dp", "col"), "row"),
            P("row"),
            P("row", "col"),
            P("col"),
            P("row", None),
            P(),
            P("col", "row"),
            P("row"),
            P("row", "col"),
            P("row", "col"),
            P("col", "row"),
        ),
        check_vma=False,
    )
```

```python
import functools

import jax
import jax.numpy as jnp
from jax import lax
from jax.experimental import pallas as pl
from jax.experimental.pallas import tpu as pltpu
from jax.sharding import PartitionSpec as P

HD = 128
SEQ_LEN = 1024
EPS = 1e-06
THETA = 1000000.0
NEG = -1e30
BF16 = jnp.bfloat16
F32 = jnp.float32
MIB = 1 << 20
SMALL_ROWS = 32
LITTLE = 1000
GRANT = 60


def dot_nn(left, right):
    return lax.dot_general(left, right, (((1,), (0,)), ((), ())), preferred_element_type=F32)


def dot_nt(left, right):
    return lax.dot_general(left, right, (((1,), (1,)), ((), ())), preferred_element_type=F32)


def dot_tn(left, right):
    return lax.dot_general(left, right, (((0,), (0,)), ((), ())), preferred_element_type=F32)


def params(mib):
    return pltpu.CompilerParams(vmem_limit_bytes=mib * MIB)


def cost(flops, nbytes):
    return pl.CostEstimate(flops=int(flops), bytes_accessed=int(nbytes), transcendentals=0)


def rope(value, cosine, sine):
    return value * cosine + pltpu.roll(value, HD // 2, 1) * sine


def qkv_kernel(cols, own, *refs):
    r_ref, refs = refs[0], refs[1:]
    xa, refs = refs[:cols], refs[cols:]
    xb, refs = refs[:cols], refs[cols:]
    gain, wa, wb, bias, cosine, sine, x_out, n_out, q_out, kv_out = refs
    feat = xa[0].shape[1]
    for j in range(cols):
        rows = pl.ds(j * own, own)
        a = xa[j][...].astype(F32)
        b = xb[j][...].astype(F32)
        total = jnp.sum(a * a, axis=1, keepdims=True) + jnp.sum(b * b, axis=1, keepdims=True)
        inverse = lax.rsqrt(total / (2 * feat) + EPS)
        x_out[rows, :feat] = xa[j][...]
        x_out[rows, feat:] = xb[j][...]
        n_out[rows, :feat] = (a * inverse * gain[:, :feat]).astype(BF16)
        n_out[rows, feat:] = (b * inverse * gain[:, feat:]).astype(BF16)
    qkv = dot_nn(n_out[:, :feat], wa[...]) + dot_nn(n_out[:, feat:], wb[...]) + bias[...]
    qw = q_out.shape[1]
    for h in range(qw // HD):
        at = slice(h * HD, (h + 1) * HD)
        q_out[:, at] = rope(qkv[:, at], cosine[...], sine[...]).astype(BF16)
    kv_out[:, :HD] = rope(qkv[:, qw : qw + HD], cosine[...], sine[...]).astype(BF16)
    kv_out[:, HD:] = qkv[:, qw + HD :].astype(BF16)


def qkv_call(r, xa, xb, gain, wa, wb, bias, cosine, sine, qw, own):
    cols = len(xa)
    feat = xa[0].shape[1]
    tokens = own * cols
    whole = lambda v: pl.BlockSpec(v.shape, lambda i, r: (0,) * v.ndim)
    rest = [gain, wa, wb, bias, cosine, sine]
    outs = [
        jax.ShapeDtypeStruct((tokens, 2 * feat), BF16),
        jax.ShapeDtypeStruct((tokens, 2 * feat), BF16),
        jax.ShapeDtypeStruct((tokens, qw), BF16),
        jax.ShapeDtypeStruct((tokens, 2 * HD), BF16),
    ]
    return pl.pallas_call(
        functools.partial(qkv_kernel, cols, own),
        grid_spec=pltpu.PrefetchScalarGridSpec(
            num_scalar_prefetch=1,
            grid=(1,),
            in_specs=[pl.BlockSpec((own, feat), lambda i, r: (r[0], 0))] * (2 * cols)
            + [whole(v) for v in rest],
            out_specs=[whole(o) for o in outs],
        ),
        out_shape=outs,
        compiler_params=params(40),
        cost_estimate=cost(LITTLE, LITTLE),
        name="qkv",
    )(r, *xa, *xb, *rest)


def softmax(q, k, visible, scaling):
    scores = jnp.where(visible, dot_nt(q, k) * scaling, NEG)
    e = jnp.exp(scores - jnp.max(scores, axis=1, keepdims=True))
    return e * (1.0 / jnp.sum(e, axis=1, keepdims=True))


def visibility(qpos, kpos, prefix_ref):
    return (kpos <= qpos) | (kpos < prefix_ref[0])


def attend_kernel(scaling, prefix, q, kv_a, kv_b, qpos, kpos, out):
    visible = visibility(qpos[...], kpos[...], prefix)
    keys = jnp.concatenate([kv_a[:, :HD], kv_b[:, :HD]], axis=0)
    values = jnp.concatenate([kv_a[:, HD:], kv_b[:, HD:]], axis=0)
    for h in range(q.shape[1] // HD):
        at = slice(h * HD, (h + 1) * HD)
        weights = softmax(q[:, at], keys, visible, scaling)
        out[:, at] = dot_nn(weights.astype(BF16), values).astype(BF16)


def attend_call(prefix, q, kv_a, kv_b, qpos, kpos, block):
    tokens, qw = q.shape
    whole = lambda v: pl.BlockSpec(v.shape, lambda i, p: (0,) * v.ndim)
    part = lambda v: pl.BlockSpec((block, v.shape[1]), lambda i, p: (i, 0))
    return pl.pallas_call(
        functools.partial(attend_kernel, HD**-0.5),
        grid_spec=pltpu.PrefetchScalarGridSpec(
            num_scalar_prefetch=1,
            grid=(tokens // block,),
            in_specs=[part(q), whole(kv_a), whole(kv_b), part(qpos), whole(kpos)],
            out_specs=part(q),
        ),
        out_shape=jax.ShapeDtypeStruct(q.shape, BF16),
        compiler_params=params(32),
        cost_estimate=cost(LITTLE, LITTLE),
        name="attend",
    )(prefix, q, kv_a, kv_b, qpos, kpos)


def out_kernel(cols, own, side, x_at, *refs):
    att, refs = refs[:cols], refs[cols:]
    wa, wb, refs = refs[0], refs[1], refs[2:]
    pa, refs = refs[:side], refs[side:]
    pb, refs = refs[:side], refs[side:]
    xa, xb, gain, resid_out, na, nb, acc_a, acc_b, whole_a, whole_b = refs
    step, steps = pl.program_id(0), pl.num_programs(0)
    chunk = xa.shape[1]
    feat = chunk * steps
    quarter = wa.shape[0] // side

    rolled = []
    for j in range(cols):
        tiles = [att[j][((i - j) % cols) * own : ((i - j) % cols + 1) * own, :] for i in range(cols)]
        rolled.append(jnp.concatenate(tiles, axis=0))
    at = pl.ds(pl.multiple_of(step * chunk, 128), chunk)
    for parts, whole in ((pa, whole_a), (pb, whole_b)):
        for i in range(side):
            place = lax.rem(x_at[0] + i, side) * quarter
            for j in range(cols - 1):
                rows = parts[i][j * quarter : (j + 1) * quarter, :]
                whole[j, pl.ds(pl.multiple_of(place, 32), quarter), :] = rows
    for x, w, whole, acc in ((xa, wa, whole_a, acc_a), (xb, wb, whole_b, acc_b)):
        total = x[...].astype(F32) + dot_nn(rolled[0], w[...])
        for j in range(1, cols):
            total = total + dot_nn(rolled[j], whole[j - 1])
        acc[:, at] = total

    @pl.when(step == steps - 1)
    def _():
        a, b = acc_a[...], acc_b[...]
        total = jnp.sum(a * a, axis=1, keepdims=True) + jnp.sum(b * b, axis=1, keepdims=True)
        inverse = lax.rsqrt(total / (2 * feat) + EPS)
        na[...] = (a * inverse * gain[:, :feat]).astype(BF16)
        nb[...] = (b * inverse * gain[:, feat:]).astype(BF16)
        resid_out[:, :feat] = acc_a[:own, :]
        resid_out[:, feat:] = acc_b[:own, :]


def out_call(x_at, att, wa, wb, pa, pb, x, gain, own):
    cols, side = len(att), len(pa)
    tokens, qw = att[0].shape
    feat = wa.shape[1]
    steps = 3
    chunk = feat // steps
    whole = lambda v: pl.BlockSpec(v.shape, lambda i, p: (0,) * v.ndim)
    part = lambda v: pl.BlockSpec((v.shape[0], chunk), lambda i, p: (0, i))
    outs = [
        jax.ShapeDtypeStruct((own, 2 * feat), F32),
        jax.ShapeDtypeStruct((tokens, feat), BF16),
        jax.ShapeDtypeStruct((tokens, feat), BF16),
    ]
    return pl.pallas_call(
        functools.partial(out_kernel, cols, own, side),
        grid_spec=pltpu.PrefetchScalarGridSpec(
            num_scalar_prefetch=1,
            grid=(steps,),
            in_specs=[whole(a) for a in att]
            + [part(v) for v in (wa, wb, *pa, *pb)]
            + [part(x), pl.BlockSpec((tokens, chunk), lambda i, p: (0, steps + i)), whole(gain)],
            out_specs=[whole(o) for o in outs],
            scratch_shapes=[
                pltpu.VMEM((tokens, feat), F32),
                pltpu.VMEM((tokens, feat), F32),
                pltpu.VMEM((cols - 1, qw, chunk), BF16),
                pltpu.VMEM((cols - 1, qw, chunk), BF16),
            ],
        ),
        out_shape=outs,
        compiler_params=params(40),
        cost_estimate=cost(LITTLE, LITTLE),
        name="out_norm",
    )(x_at, *att, wa, wb, *pa, *pb, x, x, gain)


def assemble_kernel(cols, own, r_ref, *refs):
    ca, cb, (out_a, out_b) = refs[:cols], refs[cols : 2 * cols], refs[2 * cols :]
    tokens = cols * own
    first = ca[0].shape[0] - 2 * own
    r = r_ref[0]
    for j in range(cols):
        for src, out in ((ca[j], out_a), (cb[j], out_b)):
            out[j * own : (j + 1) * own, :] = src[pl.ds(first + r * own, own), :]
            out[tokens + j * own : tokens + (j + 1) * own, :] = src[
                pl.ds(first + (1 - r) * own, own), :
            ]


def assemble_call(r, ca, cb, own):
    cols = len(ca)
    out = jax.ShapeDtypeStruct((2 * cols * own, ca[0].shape[1]), BF16)
    return pl.pallas_call(
        functools.partial(assemble_kernel, cols, own),
        in_specs=[pl.BlockSpec(memory_space=pltpu.SMEM)]
        + [pl.BlockSpec(memory_space=pltpu.VMEM)] * (2 * cols),
        out_specs=[pl.BlockSpec(memory_space=pltpu.VMEM)] * 2,
        out_shape=[out, out],
        compiler_params=params(24),
        cost_estimate=cost(LITTLE, LITTLE),
        name="assemble",
    )(r, *ca, *cb)


def gated_kernel(na, nb, ga, gb, ua, ub, mixed, to_gate, to_up):
    gate = dot_nt(ga[...], na[...]) + dot_nt(gb[...], nb[...])
    up = dot_nt(ua[...], na[...]) + dot_nt(ub[...], nb[...])
    s = 0.5 * jnp.tanh(0.5 * gate) + 0.5
    silu = gate * s
    mixed[...] = (silu * up).astype(BF16)
    to_gate[...] = (up * (s + silu * (1.0 - s))).astype(BF16)
    to_up[...] = silu.astype(BF16)


def hidden_grad_kernel(ca, cb, da, db, to_gate, to_up, grad_gate, grad_up):
    grad_mixed = dot_nt(da[...], ca[...]) + dot_nt(db[...], cb[...])
    grad_gate[...] = (grad_mixed * to_gate[...].astype(F32)).astype(BF16)
    grad_up[...] = (grad_mixed * to_up[...].astype(F32)).astype(BF16)


def gated_call(r, na, nb, kept, got, chunk):
    tokens, feat = na.shape
    part = got.shape[1]
    steps = part // chunk
    act = pl.BlockSpec((tokens, feat), lambda i, r: (0, 0))
    mine = pl.BlockSpec((chunk, feat), lambda i, r: (r[0] * steps + i, 0))
    other = lambda k: pl.BlockSpec((None, chunk, feat), lambda i, r: (k, i, 0))
    return pl.pallas_call(
        lambda r, *refs: gated_kernel(*refs),
        grid_spec=pltpu.PrefetchScalarGridSpec(
            num_scalar_prefetch=1,
            grid=(steps,),
            in_specs=[act, act, mine, other(0), mine, other(1)],
            out_specs=[pl.BlockSpec((chunk, tokens), lambda i, r: (i, 0))] * 3,
        ),
        out_shape=[jax.ShapeDtypeStruct((part, tokens), BF16)] * 3,
        compiler_params=params(GRANT),
        cost_estimate=cost(LITTLE, LITTLE),
        name="gated",
    )(r, na, nb, kept[0], got, kept[1], got)


def hidden_grad_call(r, ca, cb, half, kept, got, to_gate, to_up, chunk):
    part, tokens = to_gate.shape
    feat = ca.shape[1]
    steps = part // chunk
    cot = pl.BlockSpec((tokens, feat), lambda i, r: (half, 0))
    hid = pl.BlockSpec((chunk, tokens), lambda i, r: (i, 0))
    return pl.pallas_call(
        lambda r, *refs: hidden_grad_kernel(*refs),
        grid_spec=pltpu.PrefetchScalarGridSpec(
            num_scalar_prefetch=1,
            grid=(steps,),
            in_specs=[
                cot,
                cot,
                pl.BlockSpec((chunk, feat), lambda i, r: (r[0] * steps + i, 0)),
                pl.BlockSpec((None, chunk, feat), lambda i, r: (2, i, 0)),
                hid,
                hid,
            ],
            out_specs=[hid, hid],
        ),
        out_shape=[jax.ShapeDtypeStruct((part, tokens), BF16)] * 2,
        compiler_params=params(GRANT),
        cost_estimate=cost(LITTLE, LITTLE),
        name="hidden_grads",
    )(r, ca, cb, kept[2], got, to_gate, to_up)


def wgrad_kernel(pairs, act_own, act_other, *refs):
    own, other, out = refs[:pairs], refs[pairs : 2 * pairs], refs[2 * pairs]
    for k in range(pairs):
        total = dot_nn(own[k][...], act_own[...]) + dot_nn(other[k][...], act_other[...])
        out[k] = total.astype(BF16)


def wgrad_call(act_own, act_other, other_block, hidden_own, hidden_other, chunk):
    pairs = len(hidden_own)
    part, tokens = hidden_own[0].shape
    feat = act_own.shape[1]
    hid = pl.BlockSpec((chunk, tokens), lambda i: (i, 0))
    return pl.pallas_call(
        functools.partial(wgrad_kernel, pairs),
        grid=(part // chunk,),
        in_specs=[
            pl.BlockSpec((tokens, feat), lambda i: (0, 0)),
            pl.BlockSpec((tokens, feat), lambda i: (other_block, 0)),
        ]
        + [hid] * (2 * pairs),
        out_specs=pl.BlockSpec((pairs, chunk, feat), lambda i: (0, i, 0)),
        out_shape=jax.ShapeDtypeStruct((pairs, part, feat), BF16),
        compiler_params=params(GRANT),
        cost_estimate=cost(LITTLE, LITTLE),
        name="weight_grads",
    )(act_own, act_other, *hidden_own, *hidden_other)


def back_kernel(pairs, *refs):
    hidden, refs = (refs[:pairs], refs[pairs : 2 * pairs]), refs[2 * pairs :]
    wa, refs = refs[:pairs], refs[pairs:]
    wb, outs = refs[:pairs], refs[pairs:]
    for half in (1, 0):
        for w, out in ((wa, outs[2 * half]), (wb, outs[2 * half + 1])):
            total = dot_tn(hidden[half][0][...], w[0][...])
            for i in range(1, pairs):
                total = total + dot_tn(hidden[half][i][...], w[i][...])
            out[...] = total.astype(out.dtype)


def back_call(r, own, other, kept, got, first):
    pairs = len(own)
    part, tokens = own[0].shape
    feat = got.shape[2]
    out = jax.ShapeDtypeStruct((tokens, feat), BF16)
    of_other = lambda k: pl.BlockSpec((None, part, feat), lambda i, r: (first + k, 0, 0))
    return pl.pallas_call(
        lambda r, *refs: back_kernel(pairs, *refs),
        grid_spec=pltpu.PrefetchScalarGridSpec(
            num_scalar_prefetch=1,
            grid=(1,),
            in_specs=[pl.BlockSpec((part, tokens), lambda i, r: (0, 0))] * (2 * pairs)
            + [pl.BlockSpec((part, feat), lambda i, r: (r[0], 0))] * pairs
            + [of_other(k) for k in range(pairs)],
            out_specs=[pl.BlockSpec((tokens, feat), lambda i, r: (0, 0))] * 4,
        ),
        out_shape=[out] * 4,
        compiler_params=params(GRANT),
        cost_estimate=cost(LITTLE, LITTLE),
        name="back_in",
    )(r, *own, *other, *kept, *([got] * pairs))


def attend_back_kernel(
    scaling, own, prefix, *refs
):
    (gr, wa, wb, q, kv_a, kv_b, qpos, kpos, cosine, sine,
     low_out, sum_out, gkv_own, gkv_send, gk, gv, ga_s) = refs
    step, steps = pl.program_id(0), pl.num_programs(0)
    feat = wa.shape[1]
    visible = visibility(qpos[...], kpos[...], prefix)
    keys = jnp.concatenate([kv_a[:, :HD], kv_b[:, :HD]], axis=0)
    values = jnp.concatenate([kv_a[:, HD:], kv_b[:, HD:]], axis=0)
    ga_s[...] = (dot_nt(gr[:, :feat], wa[...]) + dot_nt(gr[:, feat:], wb[...])).astype(BF16)

    @pl.when(step == 0)
    def _():
        gk[...] = jnp.zeros_like(gk)
        gv[...] = jnp.zeros_like(gv)
        sum_out[...] = jnp.zeros_like(sum_out)

    for h in range(q.shape[1] // HD):
        at = slice(h * HD, (h + 1) * HD)
        weights = softmax(q[:, at], keys, visible, scaling)
        grad_att = ga_s[:, at]
        gw = dot_nt(grad_att, values)
        inner = jnp.sum(weights * gw, axis=1, keepdims=True)
        gs = (weights * (gw - inner)).astype(BF16)
        gk[...] += dot_tn(gs, q[:, at])
        gv[...] += dot_tn(weights.astype(BF16), grad_att)
        grad_q = dot_nn(gs, keys) * scaling
        grad_q = rope(grad_q, cosine[...], sine[...])
        low_out[:, at] = grad_q.astype(BF16)
        sum_out[:, at] += jnp.sum(grad_q, axis=0, keepdims=True)

    @pl.when(step == steps - 1)
    def _():
        half = gk.shape[0] // 2
        gkv_own[:, :HD] = gk[:half, :] * scaling
        gkv_own[:, HD:] = gv[:half, :]
        gkv_send[:, :HD] = (gk[half:, :] * scaling).astype(BF16)
        gkv_send[:, HD:] = gv[half:, :].astype(BF16)


def attend_back_call(prefix, gr, wa, wb, q, kv_a, kv_b, qpos, kpos, cosine, sine, block):
    tokens, qw = q.shape
    whole = lambda v: pl.BlockSpec(v.shape, lambda i, p: (0,) * v.ndim)
    part = lambda v: pl.BlockSpec((block, v.shape[1]), lambda i, p: (i, 0))
    outs = [
        jax.ShapeDtypeStruct((tokens, qw), BF16),
        jax.ShapeDtypeStruct((1, qw), F32),
        jax.ShapeDtypeStruct((tokens, 2 * HD), F32),
        jax.ShapeDtypeStruct((tokens, 2 * HD), BF16),
    ]
    keys = 2 * tokens
    return pl.pallas_call(
        functools.partial(attend_back_kernel, HD**-0.5, block),
        grid_spec=pltpu.PrefetchScalarGridSpec(
            num_scalar_prefetch=1,
            grid=(tokens // block,),
            in_specs=[
                part(gr), whole(wa), whole(wb), part(q), whole(kv_a), whole(kv_b),
                part(qpos), whole(kpos), part(cosine), part(sine),
            ],
            out_specs=[part(outs[0]), whole(outs[1]), whole(outs[2]), whole(outs[3])],
            scratch_shapes=[
                pltpu.VMEM((keys, HD), F32),
                pltpu.VMEM((keys, HD), F32),
                pltpu.VMEM((block, qw), BF16),
            ],
        ),
        out_shape=outs,
        compiler_params=params(40),
        cost_estimate=cost(LITTLE, LITTLE),
        name="attend_back",
    )(prefix, gr, wa, wb, q, kv_a, kv_b, qpos, kpos, cosine, sine)


def qkv_back_kernel(own, got, query_low, cosine, sine, wa, wb, low, sums, back):
    qw = query_low.shape[1]
    total = own[...] + got[...].astype(F32)
    key = rope(total[:, :HD], cosine[...], sine[...])
    value = total[:, HD:]
    sums[:, :HD] = jnp.sum(key, axis=0, keepdims=True)
    sums[:, HD:] = jnp.sum(value, axis=0, keepdims=True)
    low[:, :qw] = query_low[...]
    low[:, qw : qw + HD] = key.astype(BF16)
    low[:, qw + HD :] = value.astype(BF16)
    feat = wa.shape[0]
    back[:, :feat] = dot_nt(low[...], wa[...]).astype(BF16)
    back[:, feat:] = dot_nt(low[...], wb[...]).astype(BF16)


def qkv_back_call(own, got, query_low, cosine, sine, wa, wb):
    tokens = own.shape[0]
    feat, columns = wa.shape
    return pl.pallas_call(
        qkv_back_kernel,
        out_shape=[
            jax.ShapeDtypeStruct((tokens, columns), BF16),
            jax.ShapeDtypeStruct((1, 2 * HD), F32),
            jax.ShapeDtypeStruct((tokens, 2 * feat), BF16),
        ],
        compiler_params=params(32),
        cost_estimate=cost(LITTLE, LITTLE),
        name="qkv_back",
    )(own, got, query_low, cosine, sine, wa, wb)


def rest_kernel(n1, low, attended, grad, in_a, in_b, out_a, out_b):
    feat = n1.shape[1] // 2
    in_b[...] = dot_tn(n1[:, feat:], low[...]).astype(BF16)
    out_b[...] = dot_tn(attended[...], grad[:, feat:]).astype(BF16)
    in_a[...] = dot_tn(n1[:, :feat], low[...]).astype(BF16)
    out_a[...] = dot_tn(attended[...], grad[:, :feat]).astype(BF16)


def rest_call(n1, low, attended, grad):
    feat = n1.shape[1] // 2
    into = jax.ShapeDtypeStruct((feat, low.shape[1]), BF16)
    out = jax.ShapeDtypeStruct((attended.shape[1], feat), BF16)
    return pl.pallas_call(
        rest_kernel,
        out_shape=[into, into, out, out],
        compiler_params=params(32),
        cost_estimate=cost(LITTLE, LITTLE),
        name="rest",
    )(n1, low, attended, grad)


def join_kernel(r_ref, kept, got, out):
    part = kept.shape[0]

    @pl.when(r_ref[0] == 0)
    def _():
        out[:part, :] = kept[...].astype(F32)
        out[part:, :] = got[...].astype(F32)

    @pl.when(r_ref[0] != 0)
    def _():
        out[:part, :] = got[...].astype(F32)
        out[part:, :] = kept[...].astype(F32)


def join_call(r, kept, got, which, chunk):
    part, feat = kept.shape[1:]
    half = pl.BlockSpec((None, part, chunk), lambda i, r: (which, 0, i))
    return pl.pallas_call(
        join_kernel,
        grid_spec=pltpu.PrefetchScalarGridSpec(
            num_scalar_prefetch=1,
            grid=(feat // chunk,),
            in_specs=[half, half],
            out_specs=pl.BlockSpec((2 * part, chunk), lambda i, r: (0, i)),
        ),
        out_shape=jax.ShapeDtypeStruct((2 * part, feat), F32),
        compiler_params=params(32),
        cost_estimate=cost(LITTLE, LITTLE),
        name="join",
    )(r, kept, got)


def pack_kernel(one, two, bias_kv, bias_query, mine, sent):
    feat = one.shape[1] // 2
    for out, first in ((mine, 0), (sent, feat)):
        out[...] = jnp.zeros_like(out)
        at = 0
        for vector, start, size in (
            (one, first, feat),
            (two, first, feat),
            (bias_kv, 0, bias_kv.shape[1]),
            (bias_query, 0, bias_query.shape[1]),
        ):
            for k in range(size // HD):
                out[at : at + 1, :] = vector[:, start + k * HD : start + (k + 1) * HD]
                at += 1


def pack_call(one, two, bias_kv, bias_query):
    out = jax.ShapeDtypeStruct((SMALL_ROWS, HD), F32)
    return pl.pallas_call(
        pack_kernel,
        out_shape=[out, out],
        cost_estimate=cost(LITTLE, LITTLE),
        name="pack",
    )(one, two, bias_kv, bias_query)


def message_kernel(mine, got, rest, out, small):
    rows = rest.shape[0]
    total = mine[...] + got[...]
    small[...] = total
    out[:rows, :] = rest[:, rest.shape[1] - 2 * HD :]
    out[rows:, :HD] = total.astype(BF16)
    out[rows:, HD:] = jnp.zeros((SMALL_ROWS, HD), BF16)


def message_call(mine, got, rest):
    rows = rest.shape[0]
    return pl.pallas_call(
        message_kernel,
        out_shape=[
            jax.ShapeDtypeStruct((rows + SMALL_ROWS, 2 * HD), BF16),
            jax.ShapeDtypeStruct((SMALL_ROWS, HD), F32),
        ],
        cost_estimate=cost(LITTLE, LITTLE),
        name="message",
    )(mine, got, rest)


def head_sum_kernel(cols, heads, gain_rows, chip, *refs):
    messages, (small, rest, out_a, out_b, total) = refs[:cols], refs[cols:]
    rows, columns = rest.shape
    half = out_a.shape[1]
    share = cols // heads
    total[...] = jnp.zeros_like(total)
    total[:gain_rows, :] = sum(m[rows : rows + gain_rows, :HD].astype(F32) for m in messages)
    for head in range(heads):
        both = jnp.zeros((rows, 2 * HD), F32)
        bias = jnp.zeros((SMALL_ROWS, HD), F32)
        for j in range(cols):
            same = jnp.where(lax.rem(chip[0] + j, cols) // share == head, 1.0, 0.0)
            both = both + same * messages[j][:rows, :].astype(F32)
            bias = bias + same * messages[j][rows:, :HD].astype(F32)
        own_columns = columns - 2 * HD - half
        at = own_columns + head * HD
        out_b[:, at : at + HD] = both[:, :HD].astype(BF16)
        at += heads * HD
        out_b[:, at : at + HD] = both[:, HD:].astype(BF16)
        for k in range(2):
            row = gain_rows + k * heads + head
            total[row : row + 1, :] = bias[gain_rows + k : gain_rows + k + 1, :]
    queries = small[gain_rows + 2 :, :]
    first = gain_rows + 2 * heads
    total[first:, :] = queries[: SMALL_ROWS - first, :]
    out_a[:rows, :] = rest[:, :half]
    out_b[:, : columns - 2 * HD - half] = rest[:, half : columns - 2 * HD]
    out_a[rows:, :HD] = total[...].astype(BF16)
    out_a[rows:, HD:] = jnp.zeros((SMALL_ROWS, half - HD), BF16)


def head_sum_call(chip, messages, small, rest, heads, gain_rows):
    rows, columns = rest.shape
    half = (columns + 2 * HD * (heads - 1)) // 2
    vmem = pl.BlockSpec(memory_space=pltpu.VMEM)
    return pl.pallas_call(
        functools.partial(head_sum_kernel, len(messages), heads, gain_rows),
        in_specs=[pl.BlockSpec(memory_space=pltpu.SMEM)] + [vmem] * (len(messages) + 2),
        out_specs=[vmem, vmem],
        out_shape=[
            jax.ShapeDtypeStruct((rows + SMALL_ROWS, half), BF16),
            jax.ShapeDtypeStruct((rows, half), BF16),
        ],
        scratch_shapes=[pltpu.VMEM((SMALL_ROWS, HD), F32)],
        cost_estimate=cost(LITTLE, LITTLE),
        name="head_sums",
    )(chip, *messages, small, rest)


def order_kernel(side, places, *refs):
    first, second, (out_a, out_b) = refs[:side], refs[side : 2 * side], refs[2 * side :]
    rows = second[0].shape[0]
    for i in range(side):
        at = lax.rem(places[1] + i, side) * rows
        out_a[pl.ds(pl.multiple_of(at, 16), rows), :] = first[i][:rows, :]
        at = lax.rem(places[0] + i, side) * rows
        out_b[pl.ds(pl.multiple_of(at, 16), rows), :] = second[i][...]
    total = sum(v[rows:, :].astype(F32) for v in first)
    out_a[side * rows :, :] = total.astype(BF16)


def order_call(places, first, second):
    side = len(first)
    rows, half = second[0].shape
    vmem = pl.BlockSpec(memory_space=pltpu.VMEM)
    return pl.pallas_call(
        functools.partial(order_kernel, side),
        in_specs=[pl.BlockSpec(memory_space=pltpu.SMEM)] + [vmem] * (2 * side),
        out_specs=[vmem, vmem],
        out_shape=[
            jax.ShapeDtypeStruct((side * rows + SMALL_ROWS, half), BF16),
            jax.ShapeDtypeStruct((side * rows, half), BF16),
        ],
        cost_estimate=cost(LITTLE, LITTLE),
        name="order",
    )(places, *first, *second)


def finish_kernel(side, heads, places, *refs):
    first, second, outs = refs[:side], refs[side : 2 * side], refs[2 * side :]
    w_out, w_query, w_keyval, one, two, bias_kv, bias_query, total = outs
    qw = w_query.shape[1]
    block, half = second[0].shape
    rows = block // side
    count = qw // block
    for i in range(side):
        at = lax.rem(places[0] + i, side)
        place = pl.ds(pl.multiple_of(at * block, 16), block)
        w_query[place, : half - qw] = first[i][:block, qw:].astype(F32)
        values = first[i][:block, :qw].astype(F32)

        @pl.when(at < count)
        def _():
            w_out[pl.ds(pl.multiple_of(at * block, 16), block), :qw] = values

        @pl.when(at >= count)
        def _():
            w_out[pl.ds(pl.multiple_of((at - count) * block, 16), block), qw:] = values

        at = lax.rem(places[1] + i, side)
        for k in range(side):
            place = pl.ds(pl.multiple_of(k * block + at * rows, 16), rows)
            piece = second[i][k * rows : (k + 1) * rows, :].astype(F32)
            w_query[place, half - qw :] = piece[:, : 2 * qw - half]
            w_keyval[place, :] = piece[:, 2 * qw - half :]
    total[...] = sum(v[block:, :HD].astype(F32) for v in first)
    at = 0
    for out in (one, two, bias_kv, bias_query):
        out[...] = total[at : at + out.shape[0], :]
        at += out.shape[0]


def finish_call(places, first, second, qw, feat, heads):
    side = len(first)
    vmem = pl.BlockSpec(memory_space=pltpu.VMEM)
    shapes = [(qw, feat), (feat, qw), (feat, 2 * heads * HD)]
    shapes += [(feat // HD, HD), (feat // HD, HD), (2 * heads, HD), (qw // HD, HD)]
    return pl.pallas_call(
        functools.partial(finish_kernel, side, heads),
        in_specs=[pl.BlockSpec(memory_space=pltpu.SMEM)] + [vmem] * (2 * side),
        out_specs=[vmem] * len(shapes),
        out_shape=[jax.ShapeDtypeStruct(s, F32) for s in shapes],
        scratch_shapes=[pltpu.VMEM((SMALL_ROWS, HD), F32)],
        compiler_params=params(32),
        cost_estimate=cost(LITTLE, LITTLE),
        name="finish",
    )(places, *first, *second)
def after(value, *others):
    return lax.optimization_barrier((value,) + others)[0]


def swap_rows(value):
    return lax.ppermute(value, "row", [(0, 1), (1, 0)])


def from_col(value, offset):
    count = lax.axis_size("col")
    return lax.ppermute(value, "col", [((i + offset) % count, i) for i in range(count)])


def gather_col(value):
    third, first = from_col(value, -1), from_col(value, 1)
    return [value, first, from_col(value, 2), third]


def gather_col_ring(value, behind=()):
    third, first = from_col(value, -1), from_col(value, 1)
    middle = value.shape[0] // 2
    upper = from_col(after(first, *behind)[:middle], 1)
    lower = from_col(after(third, *behind)[middle:], -1)
    return [value, first, jnp.concatenate([upper, lower], axis=0), third]


def scatter_col(blocks, behind=()):
    third, first, second = (
        from_col(blocks[3], 1),
        from_col(blocks[1], -1),
        from_col(blocks[2], -2),
    )
    total = blocks[0].astype(F32)
    for part in (first, second, third):
        total = total + after(part, *behind).astype(F32)
    return total


def halves(value):
    middle = value.shape[-1] // 2
    return value[..., :middle], value[..., middle:]


def roll_blocks(value, shift, axis):
    size = value.shape[axis]
    twice = jnp.concatenate([value, value], axis=axis)
    return lax.dynamic_slice_in_dim(twice, shift, size, axis)


def shift_dp(value, along, offset, side):
    pairs = []
    for z in range(side):
        for x in range(side):
            if along == "z":
                source = ((z + offset) % side) * side + x
            else:
                source = z * side + (x + offset) % side
            pairs.append((source, z * side + x))
    return lax.ppermute(value, "dp", pairs)


def scatter_dp(value, along, at, side):
    value = jnp.pad(value, ((0, -value.shape[0] % (8 * side)), (0, 0)))
    rows = value.shape[0] // side
    block = lambda j: lax.dynamic_slice_in_dim(value, ((at + j) % side) * rows, rows, 0)
    got = [shift_dp(block(j), along, -j, side) for j in (1, side - 1, 2)]
    total = block(0).astype(F32)
    for part in got:
        total = total + part.astype(F32)
    return total.astype(BF16)


def gather_dp_ring(value, along, side):
    third, first = shift_dp(value, along, -1, side), shift_dp(value, along, 1, side)
    middle = value.shape[0] // 2
    upper = shift_dp(first[:middle], along, 1, side)
    lower = shift_dp(third[middle:], along, -1, side)
    return [value, first, jnp.concatenate([upper, lower], axis=0), third]


def gather_dp(value, along, side):
    got = {j: shift_dp(value, along, j, side) for j in (1, side - 1, 2)}
    return [value] + [got[j] for j in range(1, side)]


def body(
    layer_input,
    prefix,
    gain_one,
    w_query,
    b_query,
    w_keyval,
    b_keyval,
    w_out,
    gain_two,
    w_gate,
    w_up,
    w_down,
    cotangent,
):
    cols = lax.axis_size("col")
    groups = lax.axis_size("dp")
    side = int(round(groups**0.5))
    r = lax.axis_index("row")
    c = lax.axis_index("col")
    dp = lax.axis_index("dp")
    z_at, x_at = dp // side, dp % side
    core = r.astype(jnp.int32).reshape(1)
    rows_in, feat = layer_input.shape
    own = rows_in // 2
    tokens = own * cols
    width = 2 * feat
    qw = w_query.shape[1]
    kvw = w_keyval.shape[1] // 2
    share = cols // (kvw // HD)
    kv_head = c // share
    ff = w_gate.shape[1]
    part = ff // 2

    x_a = gather_col(layer_input)

    key_start = kv_head * HD
    w_qkv_a = jnp.concatenate(
        [
            w_query,
            lax.dynamic_slice_in_dim(w_keyval, key_start, HD, 1),
            lax.dynamic_slice_in_dim(w_keyval, kvw + key_start, HD, 1),
        ],
        axis=1,
    )
    bias = jnp.concatenate(
        [
            b_query,
            lax.dynamic_slice_in_dim(b_keyval, key_start, HD, 0),
            lax.dynamic_slice_in_dim(b_keyval, kvw + key_start, HD, 0),
        ]
    ).astype(F32)[None]
    w_qkv_b = swap_rows(w_qkv_a)
    gains_a = jnp.stack([gain_one, gain_two])
    gains = jnp.concatenate([gains_a, swap_rows(gains_a)], axis=1).astype(F32)
    gain_one_f, gain_two_f = gains[:1], gains[1:]

    kept = [w_gate.T, w_up.T, w_down]
    sent = [
        lax.dynamic_slice_in_dim(w, (1 - r) * part, part, 0)
        for w in kept
    ]
    sent = jnp.stack(sent)

    block_first = rows_in * ((c + jnp.arange(cols, dtype=jnp.int32)) % cols)
    inside = jnp.arange(own, dtype=jnp.int32)
    pos_own = ((block_first[:, None] + own * r + inside[None]) % SEQ_LEN).reshape(-1)
    pos_other = ((block_first[:, None] + own * (1 - r) + inside[None]) % SEQ_LEN).reshape(-1)
    query_pos = pos_own[:, None]
    key_pos = jnp.concatenate([pos_own, pos_other])[None, :]
    frequency = THETA ** (-jnp.arange(0, HD // 2, dtype=F32) * 2.0 / HD)
    angle = pos_own.astype(F32)[:, None] * frequency[None, :]
    cosine, sine = jnp.cos(angle), jnp.sin(angle)
    cosine = jnp.concatenate([cosine, cosine], axis=1)
    sine_to = jnp.concatenate([-sine, sine], axis=1)
    sine_back = jnp.concatenate([sine, -sine], axis=1)

    quarter = qw // side
    wo_parts = lax.dynamic_slice_in_dim(w_out, x_at * quarter, quarter, 0)
    wo_parts = gather_col(after(wo_parts, w_qkv_b, gains))[1:]
    wo_parts = jnp.concatenate(wo_parts, axis=0)
    x_b = [swap_rows(after(v, wo_parts, cosine, sine_to, sine_back, sent)) for v in x_a]
    wo_parts = gather_dp_ring(wo_parts, "x", side)
    x_full, normed_one, query, kv_own = qkv_call(
        core, x_a, x_b, gain_one_f, w_qkv_a, w_qkv_b, bias, cosine, sine_to, qw, own
    )
    kv_other = swap_rows(kv_own)
    wo_parts_b = [swap_rows(v) for v in wo_parts]
    wo_a, wo_b = w_out, swap_rows(w_out)
    c_a = gather_col_ring(after(cotangent, *x_a[1:]))
    query = after(query, wo_b, wo_parts_b[0], wo_parts_b[1], wo_parts_b[3], c_a[1], c_a[3])
    attended = attend_call(prefix, query, kv_own, kv_other, query_pos, key_pos, tokens)
    got = swap_rows(after(sent, attended))
    att = gather_col_ring(attended, (got,))
    resid, n2_a, n2_b = out_call(
        x_at.astype(jnp.int32).reshape(1), att, wo_a, wo_b, wo_parts, wo_parts_b, x_full,
        gain_two_f, own,
    )
    n2_other_b, n2_other_a = swap_rows(n2_a), swap_rows(n2_b)


    gated_own = gated_call(core, n2_a, n2_b, kept, got, part // 2)
    gated_other = gated_call(core, n2_other_a, n2_other_b, kept, got, part // 2)

    c_b = [swap_rows(after(v, gated_own[0])) for v in c_a]
    cot_a, cot_b = assemble_call(after(core, gated_other[0]), c_a, c_b, own)

    def hidden_grads(half, gated):
        grads = hidden_grad_call(
            core, cot_a, cot_b, half, kept, got, gated[1], gated[2], part // 2
        )
        return [gated[0], *grads]

    hid_own = hidden_grads(0, gated_own)
    hid_other = hidden_grads(1, gated_other)

    def weight_grads(n_own, n_other, cot, own, other):
        return [
            wgrad_call(n_own, n_other, 0, own[1:], other[1:], part // 2),
            wgrad_call(cot, cot, 1, own[:1], other[:1], part // 2),
        ]

    big_b = weight_grads(n2_b, n2_other_b, cot_b, hid_own, hid_other)
    big_a = weight_grads(n2_a, n2_other_a, cot_a, hid_own, hid_other)
    own_grads = (*big_a, *big_b)
    big = lax.psum(own_grads, "dp")

    def sum_cores(own_pair, other_pair):
        from_b, from_a = swap_rows(other_pair[0]), swap_rows(other_pair[1])
        a = own_pair[0].astype(F32) + from_a.astype(F32)
        b = own_pair[1].astype(F32) + from_b.astype(F32)
        return jnp.concatenate([a, b], axis=1).astype(BF16)

    def token_blocks(value):
        return [value[j * own : (j + 1) * own] for j in range(cols)]

    back_own = [after(v, *own_grads) for v in hid_own[1:]]
    terms = back_call(core, back_own, hid_other[1:], kept[:2], got, 0)
    grad_normed_two = scatter_col(token_blocks(sum_cores(terms[:2], terms[2:])))


    def norm_backward(grad, value, gain):
        inverse = lax.rsqrt(jnp.mean(value * value, axis=1, keepdims=True) + EPS)
        unit = value * inverse
        scaled = grad * gain
        mean_term = jnp.mean(scaled * unit, axis=1, keepdims=True)
        return inverse * (scaled - unit * mean_term), jnp.sum(grad * unit, axis=0, keepdims=True)

    grad_norm_two, grad_gain_two = norm_backward(grad_normed_two, resid, gain_two_f)
    cot_full = jnp.concatenate([cot_a[:own], cot_b[:own]], axis=1).astype(F32)
    grad_resid = cot_full + grad_norm_two
    resid_blocks = gather_col(grad_resid.astype(BF16))
    resid_low = jnp.concatenate(resid_blocks, axis=0)

    query_low, grad_b_query, gkv_own, gkv_sent = attend_back_call(
        prefix, resid_low, wo_a, wo_b, query, kv_own, kv_other,
        query_pos, key_pos, cosine, sine_back, tokens,
    )
    qkv_low, grad_b_kv, back_one = qkv_back_call(
        gkv_own, swap_rows(gkv_sent), query_low, cosine, sine_back, w_qkv_a, w_qkv_b
    )
    grad_normed_one = scatter_col(token_blocks(back_one))

    def exchange_out(value):
        mine, other = halves(value)
        other = swap_rows(other)
        return jnp.where(
            r == 0,
            jnp.concatenate([mine, other], axis=0),
            jnp.concatenate([other, mine], axis=0),
        )

    grad_norm_one, grad_gain_one = norm_backward(
        grad_normed_one, x_full[:own].astype(F32), gain_one_f
    )
    grad_input = exchange_out(grad_resid + grad_norm_one)

    mixed_other = after(hid_other[0], grad_normed_one)
    terms = back_call(core, hid_own[:1], [mixed_other], kept[2:], got, 2)
    down = token_blocks(sum_cores(terms[:2], terms[2:]))
    down = scatter_col([after(v, grad_normed_one) for v in down])
    output = exchange_out((resid + down).astype(BF16))

    in_a, in_b, out_a, out_b = rest_call(normed_one, qkv_low, attended, resid_low)
    rest = in_a.astype(F32) + swap_rows(in_b).astype(F32)
    grad_wout = out_a.astype(F32) + swap_rows(out_b).astype(F32)
    grad_wout = jnp.concatenate(halves(grad_wout), axis=0)
    rest = jnp.concatenate([grad_wout, rest], axis=1).astype(BF16)
    rest = scatter_dp(scatter_dp(rest, "x", x_at, side), "z", z_at, side)
    piece_rows = rest.shape[0]

    heads = kvw // HD
    big_got = [swap_rows(after(v, rest, output)) for v in big[2:]]
    mine, sent = pack_call(grad_gain_one, grad_gain_two, grad_b_kv, grad_b_query)
    message, small = message_call(mine, swap_rows(sent), rest)
    chip = c.astype(jnp.int32).reshape(1)
    first, second = head_sum_call(chip, gather_col(after(message, big[0], output)), small, rest, heads, width // HD)
    places = jnp.stack([x_at, z_at]).astype(jnp.int32)
    grad_w_gate = join_call(core, big[0], big_got[0], 0, 256)
    grad_w_up = join_call(core, big[0], big_got[0], 1, 256)
    grad_w_down = join_call(core, big[1], big_got[1], 0, 256)
    first, second = gather_dp(first, "z", side), gather_dp(second, "x", side)
    places = after(places, grad_w_gate, grad_w_up)
    first, second = order_call(places, first, second)
    first, second = gather_dp(first, "x", side), gather_dp(second, "z", side)
    places = after(places, grad_w_down)
    grad_wout, grad_wq, grad_wkv, one, two, bias_kv, bias_query = finish_call(
        places, first, second, qw, feat, heads
    )

    return (
        output,
        grad_input,
        one.reshape(-1),
        grad_wq,
        bias_query.reshape(-1),
        grad_wkv,
        bias_kv.reshape(-1),
        grad_wout,
        two.reshape(-1),
        grad_w_gate.T,
        grad_w_up.T,
        grad_w_down,
    )


def solution(mesh):
    return jax.shard_map(
        body,
        mesh=mesh,
        in_specs=(
            P(("dp", "col"), "row"),
            P("dp"),
            P("row"),
            P("row", "col"),
            P("col"),
            P("row", None),
            P(),
            P("col", "row"),
            P("row"),
            P("row", "col"),
            P("row", "col"),
            P("col", "row"),
            P(("dp", "col"), "row"),
        ),
        out_specs=(
            P(("dp", "col"), "row"),
            P(("dp", "col"), "row"),
            P("row"),
            P("row", "col"),
            P("col"),
            P("row", None),
            P(),
            P("col", "row"),
            P("row"),
            P("row", "col"),
            P("row", "col"),
            P("col", "row"),
        ),
        check_vma=False,
    )
```

```python
import functools

import jax
import jax.numpy as jnp
from jax import lax
from jax.experimental import pallas as pl
from jax.experimental.pallas import tpu as pltpu
from jax.sharding import PartitionSpec as P

HD = 128
SEQ_LEN = 1024
EPS = 1e-06
THETA = 1000000.0
NEG = -1e30
BF16 = jnp.bfloat16
F32 = jnp.float32
MIB = 1 << 20
SMALL_ROWS = 32
LITTLE = 1000
GRANT = 40


def dot_nn(left, right):
    return lax.dot_general(left, right, (((1,), (0,)), ((), ())), preferred_element_type=F32)


def dot_nt(left, right):
    return lax.dot_general(left, right, (((1,), (1,)), ((), ())), preferred_element_type=F32)


def dot_tn(left, right):
    return lax.dot_general(left, right, (((0,), (0,)), ((), ())), preferred_element_type=F32)


def params(mib):
    return pltpu.CompilerParams(vmem_limit_bytes=mib * MIB)


def cost(flops, nbytes):
    return pl.CostEstimate(flops=int(flops), bytes_accessed=int(nbytes), transcendentals=0)


def rope(value, cosine, sine):
    return value * cosine + pltpu.roll(value, HD // 2, 1) * sine


def qkv_kernel(cols, own, *refs):
    r_ref, refs = refs[0], refs[1:]
    xa, refs = refs[:cols], refs[cols:]
    xb, refs = refs[:cols], refs[cols:]
    gain, wa, wb, bias, cosine, sine, x_out, n_out, q_out, kv_out = refs
    feat = xa[0].shape[1]
    for j in range(cols):
        rows = pl.ds(j * own, own)
        a = xa[j][...].astype(F32)
        b = xb[j][...].astype(F32)
        total = jnp.sum(a * a, axis=1, keepdims=True) + jnp.sum(b * b, axis=1, keepdims=True)
        inverse = lax.rsqrt(total / (2 * feat) + EPS)
        x_out[rows, :feat] = xa[j][...]
        x_out[rows, feat:] = xb[j][...]
        n_out[rows, :feat] = (a * inverse * gain[:, :feat]).astype(BF16)
        n_out[rows, feat:] = (b * inverse * gain[:, feat:]).astype(BF16)
    qkv = dot_nn(n_out[:, :feat], wa[...]) + dot_nn(n_out[:, feat:], wb[...]) + bias[...]
    qw = q_out.shape[1]
    for h in range(qw // HD):
        at = slice(h * HD, (h + 1) * HD)
        q_out[:, at] = rope(qkv[:, at], cosine[...], sine[...]).astype(BF16)
    kv_out[:, :HD] = rope(qkv[:, qw : qw + HD], cosine[...], sine[...]).astype(BF16)
    kv_out[:, HD:] = qkv[:, qw + HD :].astype(BF16)


def qkv_call(r, xa, xb, gain, wa, wb, bias, cosine, sine, qw, own):
    cols = len(xa)
    feat = xa[0].shape[1]
    tokens = own * cols
    whole = lambda v: pl.BlockSpec(v.shape, lambda i, r: (0,) * v.ndim)
    rest = [gain, wa, wb, bias, cosine, sine]
    outs = [
        jax.ShapeDtypeStruct((tokens, 2 * feat), BF16),
        jax.ShapeDtypeStruct((tokens, 2 * feat), BF16),
        jax.ShapeDtypeStruct((tokens, qw), BF16),
        jax.ShapeDtypeStruct((tokens, 2 * HD), BF16),
    ]
    return pl.pallas_call(
        functools.partial(qkv_kernel, cols, own),
        grid_spec=pltpu.PrefetchScalarGridSpec(
            num_scalar_prefetch=1,
            grid=(1,),
            in_specs=[pl.BlockSpec((own, feat), lambda i, r: (r[0], 0))] * (2 * cols)
            + [whole(v) for v in rest],
            out_specs=[whole(o) for o in outs],
        ),
        out_shape=outs,
        compiler_params=params(40),
        cost_estimate=cost(LITTLE, LITTLE),
        name="qkv",
    )(r, *xa, *xb, *rest)


def softmax(q, k, visible, scaling):
    scores = jnp.where(visible, dot_nt(q, k) * scaling, NEG)
    e = jnp.exp(scores - jnp.max(scores, axis=1, keepdims=True))
    return e * (1.0 / jnp.sum(e, axis=1, keepdims=True))


def visibility(qpos, kpos, prefix_ref):
    return (kpos <= qpos) | (kpos < prefix_ref[0])


def attend_kernel(scaling, prefix, q, kv_a, kv_b, qpos, kpos, out):
    visible = visibility(qpos[...], kpos[...], prefix)
    keys = jnp.concatenate([kv_a[:, :HD], kv_b[:, :HD]], axis=0)
    values = jnp.concatenate([kv_a[:, HD:], kv_b[:, HD:]], axis=0)
    for h in range(q.shape[1] // HD):
        at = slice(h * HD, (h + 1) * HD)
        weights = softmax(q[:, at], keys, visible, scaling)
        out[:, at] = dot_nn(weights.astype(BF16), values).astype(BF16)


def attend_call(prefix, q, kv_a, kv_b, qpos, kpos, block):
    tokens, qw = q.shape
    whole = lambda v: pl.BlockSpec(v.shape, lambda i, p: (0,) * v.ndim)
    part = lambda v: pl.BlockSpec((block, v.shape[1]), lambda i, p: (i, 0))
    return pl.pallas_call(
        functools.partial(attend_kernel, HD**-0.5),
        grid_spec=pltpu.PrefetchScalarGridSpec(
            num_scalar_prefetch=1,
            grid=(tokens // block,),
            in_specs=[part(q), whole(kv_a), whole(kv_b), part(qpos), whole(kpos)],
            out_specs=part(q),
        ),
        out_shape=jax.ShapeDtypeStruct(q.shape, BF16),
        compiler_params=params(32),
        cost_estimate=cost(LITTLE, LITTLE),
        name="attend",
    )(prefix, q, kv_a, kv_b, qpos, kpos)


def out_kernel(cols, own, *refs):
    att, refs = refs[:cols], refs[cols:]
    wa, refs = refs[:cols], refs[cols:]
    wb, refs = refs[:cols], refs[cols:]
    xa, xb, gain, resid_out, na, nb, acc_a, acc_b = refs
    step, steps = pl.program_id(0), pl.num_programs(0)
    chunk = xa.shape[1]
    feat = chunk * steps

    rolled = []
    for j in range(cols):
        tiles = [att[j][((i - j) % cols) * own : ((i - j) % cols + 1) * own, :] for i in range(cols)]
        rolled.append(jnp.concatenate(tiles, axis=0))
    at = pl.ds(pl.multiple_of(step * chunk, 128), chunk)
    for x, w, acc in ((xa, wa, acc_a), (xb, wb, acc_b)):
        total = x[...].astype(F32)
        for j in range(cols):
            total = total + dot_nn(rolled[j], w[j][...])
        acc[:, at] = total

    @pl.when(step == steps - 1)
    def _():
        a, b = acc_a[...], acc_b[...]
        total = jnp.sum(a * a, axis=1, keepdims=True) + jnp.sum(b * b, axis=1, keepdims=True)
        inverse = lax.rsqrt(total / (2 * feat) + EPS)
        na[...] = (a * inverse * gain[:, :feat]).astype(BF16)
        nb[...] = (b * inverse * gain[:, feat:]).astype(BF16)
        resid_out[:, :feat] = acc_a[:own, :]
        resid_out[:, feat:] = acc_b[:own, :]


def out_call(att, wa, wb, x, gain, own):
    cols = len(att)
    tokens, qw = att[0].shape
    feat = wa[0].shape[1]
    steps = 3
    chunk = feat // steps
    whole = lambda v: pl.BlockSpec(v.shape, lambda i: (0,) * v.ndim)
    outs = [
        jax.ShapeDtypeStruct((own, 2 * feat), F32),
        jax.ShapeDtypeStruct((tokens, feat), BF16),
        jax.ShapeDtypeStruct((tokens, feat), BF16),
    ]
    return pl.pallas_call(
        functools.partial(out_kernel, cols, own),
        grid=(steps,),
        in_specs=[whole(a) for a in att]
        + [pl.BlockSpec((qw, chunk), lambda i: (0, i))] * (2 * cols)
        + [
            pl.BlockSpec((tokens, chunk), lambda i: (0, i)),
            pl.BlockSpec((tokens, chunk), lambda i: (0, steps + i)),
            whole(gain),
        ],
        out_specs=[whole(o) for o in outs],
        out_shape=outs,
        scratch_shapes=[pltpu.VMEM((tokens, feat), F32)] * 2,
        compiler_params=params(40),
        cost_estimate=cost(LITTLE, LITTLE),
        name="out_norm",
    )(*att, *wa, *wb, x, x, gain)


def assemble_kernel(cols, meta, ca, cb, out_a, out_b):
    rows = ca.shape[0] // cols
    own = rows // 2
    tokens = cols * own
    r, c = meta[0], meta[1]
    for j in range(cols):
        at = lax.rem(c + j, cols) * rows
        for src, out in ((ca, out_a), (cb, out_b)):
            out[j * own : (j + 1) * own, :] = src[pl.ds(at + r * own, own), :]
            out[tokens + j * own : tokens + (j + 1) * own, :] = src[
                pl.ds(at + (1 - r) * own, own), :
            ]


def assemble_call(meta, ca, cb, cols):
    out = jax.ShapeDtypeStruct(ca.shape, BF16)
    return pl.pallas_call(
        functools.partial(assemble_kernel, cols),
        in_specs=[pl.BlockSpec(memory_space=pltpu.SMEM)]
        + [pl.BlockSpec(memory_space=pltpu.VMEM)] * 2,
        out_specs=[pl.BlockSpec(memory_space=pltpu.VMEM)] * 2,
        out_shape=[out, out],
        compiler_params=params(24),
        cost_estimate=cost(LITTLE, LITTLE),
        name="assemble",
    )(meta, ca, cb)


def gated_kernel(na, nb, ga, gb, ua, ub, mixed, to_gate, to_up):
    gate = dot_nt(ga[...], na[...]) + dot_nt(gb[...], nb[...])
    up = dot_nt(ua[...], na[...]) + dot_nt(ub[...], nb[...])
    s = 0.5 * jnp.tanh(0.5 * gate) + 0.5
    silu = gate * s
    mixed[...] = (silu * up).astype(BF16)
    to_gate[...] = (up * (s + silu * (1.0 - s))).astype(BF16)
    to_up[...] = silu.astype(BF16)


def hidden_grad_kernel(ca, cb, da, db, to_gate, to_up, grad_gate, grad_up):
    grad_mixed = dot_nt(da[...], ca[...]) + dot_nt(db[...], cb[...])
    grad_gate[...] = (grad_mixed * to_gate[...].astype(F32)).astype(BF16)
    grad_up[...] = (grad_mixed * to_up[...].astype(F32)).astype(BF16)


def gated_call(r, na, nb, kept, got, chunk):
    tokens, feat = na.shape
    part = got.shape[1]
    steps = part // chunk
    act = pl.BlockSpec((tokens, feat), lambda i, r: (0, 0))
    mine = pl.BlockSpec((chunk, feat), lambda i, r: (r[0] * steps + i, 0))
    other = lambda k: pl.BlockSpec((None, chunk, feat), lambda i, r: (k, i, 0))
    return pl.pallas_call(
        lambda r, *refs: gated_kernel(*refs),
        grid_spec=pltpu.PrefetchScalarGridSpec(
            num_scalar_prefetch=1,
            grid=(steps,),
            in_specs=[act, act, mine, other(0), mine, other(1)],
            out_specs=[pl.BlockSpec((chunk, tokens), lambda i, r: (i, 0))] * 3,
        ),
        out_shape=[jax.ShapeDtypeStruct((part, tokens), BF16)] * 3,
        compiler_params=params(GRANT),
        cost_estimate=cost(LITTLE, LITTLE),
        name="gated",
    )(r, na, nb, kept[0], got, kept[1], got)


def hidden_grad_call(r, ca, cb, half, kept, got, to_gate, to_up, chunk):
    part, tokens = to_gate.shape
    feat = ca.shape[1]
    steps = part // chunk
    cot = pl.BlockSpec((tokens, feat), lambda i, r: (half, 0))
    hid = pl.BlockSpec((chunk, tokens), lambda i, r: (i, 0))
    return pl.pallas_call(
        lambda r, *refs: hidden_grad_kernel(*refs),
        grid_spec=pltpu.PrefetchScalarGridSpec(
            num_scalar_prefetch=1,
            grid=(steps,),
            in_specs=[
                cot,
                cot,
                pl.BlockSpec((chunk, feat), lambda i, r: (r[0] * steps + i, 0)),
                pl.BlockSpec((None, chunk, feat), lambda i, r: (2, i, 0)),
                hid,
                hid,
            ],
            out_specs=[hid, hid],
        ),
        out_shape=[jax.ShapeDtypeStruct((part, tokens), BF16)] * 2,
        compiler_params=params(GRANT),
        cost_estimate=cost(LITTLE, LITTLE),
        name="hidden_grads",
    )(r, ca, cb, kept[2], got, to_gate, to_up)


def wgrad_kernel(pairs, act_own, act_other, *refs):
    own, other, out = refs[:pairs], refs[pairs : 2 * pairs], refs[2 * pairs]
    for k in range(pairs):
        total = dot_nn(own[k][...], act_own[...]) + dot_nn(other[k][...], act_other[...])
        out[k] = total.astype(BF16)


def wgrad_call(act_own, act_other, other_block, hidden_own, hidden_other, chunk):
    pairs = len(hidden_own)
    part, tokens = hidden_own[0].shape
    feat = act_own.shape[1]
    hid = pl.BlockSpec((chunk, tokens), lambda i: (i, 0))
    return pl.pallas_call(
        functools.partial(wgrad_kernel, pairs),
        grid=(part // chunk,),
        in_specs=[
            pl.BlockSpec((tokens, feat), lambda i: (0, 0)),
            pl.BlockSpec((tokens, feat), lambda i: (other_block, 0)),
        ]
        + [hid] * (2 * pairs),
        out_specs=pl.BlockSpec((pairs, chunk, feat), lambda i: (0, i, 0)),
        out_shape=jax.ShapeDtypeStruct((pairs, part, feat), BF16),
        compiler_params=params(GRANT),
        cost_estimate=cost(LITTLE, LITTLE),
        name="weight_grads",
    )(act_own, act_other, *hidden_own, *hidden_other)


def back_kernel(pairs, *refs):
    hidden, refs = (refs[:pairs], refs[pairs : 2 * pairs]), refs[2 * pairs :]
    wa, refs = refs[:pairs], refs[pairs:]
    wb, outs = refs[:pairs], refs[pairs:]
    for half in (1, 0):
        for w, out in ((wa, outs[2 * half]), (wb, outs[2 * half + 1])):
            total = dot_tn(hidden[half][0][...], w[0][...])
            for i in range(1, pairs):
                total = total + dot_tn(hidden[half][i][...], w[i][...])
            out[...] = total.astype(out.dtype)


def back_call(r, own, other, kept, got, first):
    pairs = len(own)
    part, tokens = own[0].shape
    feat = got.shape[2]
    out = jax.ShapeDtypeStruct((tokens, feat), BF16)
    of_other = lambda k: pl.BlockSpec((None, part, feat), lambda i, r: (first + k, 0, 0))
    return pl.pallas_call(
        lambda r, *refs: back_kernel(pairs, *refs),
        grid_spec=pltpu.PrefetchScalarGridSpec(
            num_scalar_prefetch=1,
            grid=(1,),
            in_specs=[pl.BlockSpec((part, tokens), lambda i, r: (0, 0))] * (2 * pairs)
            + [pl.BlockSpec((part, feat), lambda i, r: (r[0], 0))] * pairs
            + [of_other(k) for k in range(pairs)],
            out_specs=[pl.BlockSpec((tokens, feat), lambda i, r: (0, 0))] * 4,
        ),
        out_shape=[out] * 4,
        compiler_params=params(GRANT),
        cost_estimate=cost(LITTLE, LITTLE),
        name="back_in",
    )(r, *own, *other, *kept, *([got] * pairs))


def attend_back_kernel(
    scaling, own, prefix, *refs
):
    (gr, wa, wb, q, kv_a, kv_b, qpos, kpos, cosine, sine,
     low_out, sum_out, gkv_own, gkv_send, gk, gv, ga_s) = refs
    step, steps = pl.program_id(0), pl.num_programs(0)
    feat = wa.shape[1]
    visible = visibility(qpos[...], kpos[...], prefix)
    keys = jnp.concatenate([kv_a[:, :HD], kv_b[:, :HD]], axis=0)
    values = jnp.concatenate([kv_a[:, HD:], kv_b[:, HD:]], axis=0)
    ga_s[...] = (dot_nt(gr[:, :feat], wa[...]) + dot_nt(gr[:, feat:], wb[...])).astype(BF16)

    @pl.when(step == 0)
    def _():
        gk[...] = jnp.zeros_like(gk)
        gv[...] = jnp.zeros_like(gv)
        sum_out[...] = jnp.zeros_like(sum_out)

    for h in range(q.shape[1] // HD):
        at = slice(h * HD, (h + 1) * HD)
        weights = softmax(q[:, at], keys, visible, scaling)
        grad_att = ga_s[:, at]
        gw = dot_nt(grad_att, values)
        inner = jnp.sum(weights * gw, axis=1, keepdims=True)
        gs = (weights * (gw - inner)).astype(BF16)
        gk[...] += dot_tn(gs, q[:, at])
        gv[...] += dot_tn(weights.astype(BF16), grad_att)
        grad_q = dot_nn(gs, keys) * scaling
        grad_q = rope(grad_q, cosine[...], sine[...])
        low_out[:, at] = grad_q.astype(BF16)
        sum_out[:, at] += jnp.sum(grad_q, axis=0, keepdims=True)

    @pl.when(step == steps - 1)
    def _():
        half = gk.shape[0] // 2
        gkv_own[:, :HD] = gk[:half, :] * scaling
        gkv_own[:, HD:] = gv[:half, :]
        gkv_send[:, :HD] = (gk[half:, :] * scaling).astype(BF16)
        gkv_send[:, HD:] = gv[half:, :].astype(BF16)


def attend_back_call(prefix, gr, wa, wb, q, kv_a, kv_b, qpos, kpos, cosine, sine, block):
    tokens, qw = q.shape
    whole = lambda v: pl.BlockSpec(v.shape, lambda i, p: (0,) * v.ndim)
    part = lambda v: pl.BlockSpec((block, v.shape[1]), lambda i, p: (i, 0))
    outs = [
        jax.ShapeDtypeStruct((tokens, qw), BF16),
        jax.ShapeDtypeStruct((1, qw), F32),
        jax.ShapeDtypeStruct((tokens, 2 * HD), F32),
        jax.ShapeDtypeStruct((tokens, 2 * HD), BF16),
    ]
    keys = 2 * tokens
    return pl.pallas_call(
        functools.partial(attend_back_kernel, HD**-0.5, block),
        grid_spec=pltpu.PrefetchScalarGridSpec(
            num_scalar_prefetch=1,
            grid=(tokens // block,),
            in_specs=[
                part(gr), whole(wa), whole(wb), part(q), whole(kv_a), whole(kv_b),
                part(qpos), whole(kpos), part(cosine), part(sine),
            ],
            out_specs=[part(outs[0]), whole(outs[1]), whole(outs[2]), whole(outs[3])],
            scratch_shapes=[
                pltpu.VMEM((keys, HD), F32),
                pltpu.VMEM((keys, HD), F32),
                pltpu.VMEM((block, qw), BF16),
            ],
        ),
        out_shape=outs,
        compiler_params=params(40),
        cost_estimate=cost(LITTLE, LITTLE),
        name="attend_back",
    )(prefix, gr, wa, wb, q, kv_a, kv_b, qpos, kpos, cosine, sine)


def qkv_back_kernel(own, got, query_low, cosine, sine, wa, wb, low, sums, back):
    qw = query_low.shape[1]
    total = own[...] + got[...].astype(F32)
    key = rope(total[:, :HD], cosine[...], sine[...])
    value = total[:, HD:]
    sums[:, :HD] = jnp.sum(key, axis=0, keepdims=True)
    sums[:, HD:] = jnp.sum(value, axis=0, keepdims=True)
    low[:, :qw] = query_low[...]
    low[:, qw : qw + HD] = key.astype(BF16)
    low[:, qw + HD :] = value.astype(BF16)
    feat = wa.shape[0]
    back[:, :feat] = dot_nt(low[...], wa[...]).astype(BF16)
    back[:, feat:] = dot_nt(low[...], wb[...]).astype(BF16)


def qkv_back_call(own, got, query_low, cosine, sine, wa, wb):
    tokens = own.shape[0]
    feat, columns = wa.shape
    return pl.pallas_call(
        qkv_back_kernel,
        out_shape=[
            jax.ShapeDtypeStruct((tokens, columns), BF16),
            jax.ShapeDtypeStruct((1, 2 * HD), F32),
            jax.ShapeDtypeStruct((tokens, 2 * feat), BF16),
        ],
        compiler_params=params(32),
        cost_estimate=cost(LITTLE, LITTLE),
        name="qkv_back",
    )(own, got, query_low, cosine, sine, wa, wb)


def rest_kernel(n1, low, attended, grad, in_a, in_b, out_a, out_b):
    feat = n1.shape[1] // 2
    in_b[...] = dot_tn(n1[:, feat:], low[...]).astype(BF16)
    out_b[...] = dot_tn(attended[...], grad[:, feat:]).astype(BF16)
    in_a[...] = dot_tn(n1[:, :feat], low[...]).astype(BF16)
    out_a[...] = dot_tn(attended[...], grad[:, :feat]).astype(BF16)


def rest_call(n1, low, attended, grad):
    feat = n1.shape[1] // 2
    into = jax.ShapeDtypeStruct((feat, low.shape[1]), BF16)
    out = jax.ShapeDtypeStruct((attended.shape[1], feat), BF16)
    return pl.pallas_call(
        rest_kernel,
        out_shape=[into, into, out, out],
        compiler_params=params(32),
        cost_estimate=cost(LITTLE, LITTLE),
        name="rest",
    )(n1, low, attended, grad)


def join_kernel(r_ref, kept, got, out):
    part = kept.shape[0]

    @pl.when(r_ref[0] == 0)
    def _():
        out[:part, :] = kept[...].astype(F32)
        out[part:, :] = got[...].astype(F32)

    @pl.when(r_ref[0] != 0)
    def _():
        out[:part, :] = got[...].astype(F32)
        out[part:, :] = kept[...].astype(F32)


def join_call(r, kept, got, which, chunk):
    part, feat = kept.shape[1:]
    half = pl.BlockSpec((None, part, chunk), lambda i, r: (which, 0, i))
    return pl.pallas_call(
        join_kernel,
        grid_spec=pltpu.PrefetchScalarGridSpec(
            num_scalar_prefetch=1,
            grid=(feat // chunk,),
            in_specs=[half, half],
            out_specs=pl.BlockSpec((2 * part, chunk), lambda i, r: (0, i)),
        ),
        out_shape=jax.ShapeDtypeStruct((2 * part, feat), F32),
        compiler_params=params(32),
        cost_estimate=cost(LITTLE, LITTLE),
        name="join",
    )(r, kept, got)


def pack_kernel(one, two, bias_kv, bias_query, mine, sent):
    feat = one.shape[1] // 2
    for out, first in ((mine, 0), (sent, feat)):
        out[...] = jnp.zeros_like(out)
        at = 0
        for vector, start, size in (
            (one, first, feat),
            (two, first, feat),
            (bias_kv, 0, bias_kv.shape[1]),
            (bias_query, 0, bias_query.shape[1]),
        ):
            for k in range(size // HD):
                out[at : at + 1, :] = vector[:, start + k * HD : start + (k + 1) * HD]
                at += 1


def pack_call(one, two, bias_kv, bias_query):
    out = jax.ShapeDtypeStruct((SMALL_ROWS, HD), F32)
    return pl.pallas_call(
        pack_kernel,
        out_shape=[out, out],
        cost_estimate=cost(LITTLE, LITTLE),
        name="pack",
    )(one, two, bias_kv, bias_query)


def message_kernel(mine, got, rest, out, small):
    rows = rest.shape[0]
    total = mine[...] + got[...]
    small[...] = total
    out[:rows, :] = rest[:, rest.shape[1] - 2 * HD :]
    out[rows:, :HD] = total.astype(BF16)
    out[rows:, HD:] = jnp.zeros((SMALL_ROWS, HD), BF16)


def message_call(mine, got, rest):
    rows = rest.shape[0]
    return pl.pallas_call(
        message_kernel,
        out_shape=[
            jax.ShapeDtypeStruct((rows + SMALL_ROWS, 2 * HD), BF16),
            jax.ShapeDtypeStruct((SMALL_ROWS, HD), F32),
        ],
        cost_estimate=cost(LITTLE, LITTLE),
        name="message",
    )(mine, got, rest)


def head_sum_kernel(cols, heads, gain_rows, chip, *refs):
    messages, (small, rest, out_a, out_b, total) = refs[:cols], refs[cols:]
    rows, columns = rest.shape
    half = out_a.shape[1]
    share = cols // heads
    total[...] = jnp.zeros_like(total)
    total[:gain_rows, :] = sum(m[rows : rows + gain_rows, :HD].astype(F32) for m in messages)
    for head in range(heads):
        both = jnp.zeros((rows, 2 * HD), F32)
        bias = jnp.zeros((SMALL_ROWS, HD), F32)
        for j in range(cols):
            same = jnp.where(lax.rem(chip[0] + j, cols) // share == head, 1.0, 0.0)
            both = both + same * messages[j][:rows, :].astype(F32)
            bias = bias + same * messages[j][rows:, :HD].astype(F32)
        own_columns = columns - 2 * HD - half
        at = own_columns + head * HD
        out_b[:, at : at + HD] = both[:, :HD].astype(BF16)
        at += heads * HD
        out_b[:, at : at + HD] = both[:, HD:].astype(BF16)
        for k in range(2):
            row = gain_rows + k * heads + head
            total[row : row + 1, :] = bias[gain_rows + k : gain_rows + k + 1, :]
    queries = small[gain_rows + 2 :, :]
    first = gain_rows + 2 * heads
    total[first:, :] = queries[: SMALL_ROWS - first, :]
    out_a[:rows, :] = rest[:, :half]
    out_b[:, : columns - 2 * HD - half] = rest[:, half : columns - 2 * HD]
    out_a[rows:, :HD] = total[...].astype(BF16)
    out_a[rows:, HD:] = jnp.zeros((SMALL_ROWS, half - HD), BF16)


def head_sum_call(chip, messages, small, rest, heads, gain_rows):
    rows, columns = rest.shape
    half = (columns + 2 * HD * (heads - 1)) // 2
    vmem = pl.BlockSpec(memory_space=pltpu.VMEM)
    return pl.pallas_call(
        functools.partial(head_sum_kernel, len(messages), heads, gain_rows),
        in_specs=[pl.BlockSpec(memory_space=pltpu.SMEM)] + [vmem] * (len(messages) + 2),
        out_specs=[vmem, vmem],
        out_shape=[
            jax.ShapeDtypeStruct((rows + SMALL_ROWS, half), BF16),
            jax.ShapeDtypeStruct((rows, half), BF16),
        ],
        scratch_shapes=[pltpu.VMEM((SMALL_ROWS, HD), F32)],
        cost_estimate=cost(LITTLE, LITTLE),
        name="head_sums",
    )(chip, *messages, small, rest)


def order_kernel(side, places, *refs):
    first, second, (out_a, out_b) = refs[:side], refs[side : 2 * side], refs[2 * side :]
    rows = second[0].shape[0]
    for i in range(side):
        at = lax.rem(places[1] + i, side) * rows
        out_a[pl.ds(pl.multiple_of(at, 16), rows), :] = first[i][:rows, :]
        at = lax.rem(places[0] + i, side) * rows
        out_b[pl.ds(pl.multiple_of(at, 16), rows), :] = second[i][...]
    total = sum(v[rows:, :].astype(F32) for v in first)
    out_a[side * rows :, :] = total.astype(BF16)


def order_call(places, first, second):
    side = len(first)
    rows, half = second[0].shape
    vmem = pl.BlockSpec(memory_space=pltpu.VMEM)
    return pl.pallas_call(
        functools.partial(order_kernel, side),
        in_specs=[pl.BlockSpec(memory_space=pltpu.SMEM)] + [vmem] * (2 * side),
        out_specs=[vmem, vmem],
        out_shape=[
            jax.ShapeDtypeStruct((side * rows + SMALL_ROWS, half), BF16),
            jax.ShapeDtypeStruct((side * rows, half), BF16),
        ],
        cost_estimate=cost(LITTLE, LITTLE),
        name="order",
    )(places, *first, *second)


def finish_kernel(side, heads, places, *refs):
    first, second, outs = refs[:side], refs[side : 2 * side], refs[2 * side :]
    w_out, w_query, w_keyval, one, two, bias_kv, bias_query, total = outs
    qw = w_query.shape[1]
    block, half = second[0].shape
    rows = block // side
    count = qw // block
    for i in range(side):
        at = lax.rem(places[0] + i, side)
        place = pl.ds(pl.multiple_of(at * block, 16), block)
        w_query[place, : half - qw] = first[i][:block, qw:].astype(F32)
        values = first[i][:block, :qw].astype(F32)

        @pl.when(at < count)
        def _():
            w_out[pl.ds(pl.multiple_of(at * block, 16), block), :qw] = values

        @pl.when(at >= count)
        def _():
            w_out[pl.ds(pl.multiple_of((at - count) * block, 16), block), qw:] = values

        at = lax.rem(places[1] + i, side)
        for k in range(side):
            place = pl.ds(pl.multiple_of(k * block + at * rows, 16), rows)
            piece = second[i][k * rows : (k + 1) * rows, :].astype(F32)
            w_query[place, half - qw :] = piece[:, : 2 * qw - half]
            w_keyval[place, :] = piece[:, 2 * qw - half :]
    total[...] = sum(v[block:, :HD].astype(F32) for v in first)
    at = 0
    for out in (one, two, bias_kv, bias_query):
        out[...] = total[at : at + out.shape[0], :]
        at += out.shape[0]


def finish_call(places, first, second, qw, feat, heads):
    side = len(first)
    vmem = pl.BlockSpec(memory_space=pltpu.VMEM)
    shapes = [(qw, feat), (feat, qw), (feat, 2 * heads * HD)]
    shapes += [(feat // HD, HD), (feat // HD, HD), (2 * heads, HD), (qw // HD, HD)]
    return pl.pallas_call(
        functools.partial(finish_kernel, side, heads),
        in_specs=[pl.BlockSpec(memory_space=pltpu.SMEM)] + [vmem] * (2 * side),
        out_specs=[vmem] * len(shapes),
        out_shape=[jax.ShapeDtypeStruct(s, F32) for s in shapes],
        scratch_shapes=[pltpu.VMEM((SMALL_ROWS, HD), F32)],
        compiler_params=params(32),
        cost_estimate=cost(LITTLE, LITTLE),
        name="finish",
    )(places, *first, *second)
def after(value, *others):
    return lax.optimization_barrier((value,) + others)[0]


def swap_rows(value):
    return lax.ppermute(value, "row", [(0, 1), (1, 0)])


def from_col(value, offset):
    count = lax.axis_size("col")
    return lax.ppermute(value, "col", [((i + offset) % count, i) for i in range(count)])


def gather_col(value):
    third, first = from_col(value, -1), from_col(value, 1)
    return [value, first, from_col(value, 2), third]


def gather_col_ring(value, behind=()):
    third, first = from_col(value, -1), from_col(value, 1)
    middle = value.shape[0] // 2
    upper = from_col(after(first, *behind)[:middle], 1)
    lower = from_col(after(third, *behind)[middle:], -1)
    return [value, first, jnp.concatenate([upper, lower], axis=0), third]


def scatter_col(blocks, behind=()):
    third, first, second = (
        from_col(blocks[3], 1),
        from_col(blocks[1], -1),
        from_col(blocks[2], -2),
    )
    total = blocks[0].astype(F32)
    for part in (first, second, third):
        total = total + after(part, *behind).astype(F32)
    return total


def halves(value):
    middle = value.shape[-1] // 2
    return value[..., :middle], value[..., middle:]


def roll_blocks(value, shift, axis):
    size = value.shape[axis]
    twice = jnp.concatenate([value, value], axis=axis)
    return lax.dynamic_slice_in_dim(twice, shift, size, axis)


def shift_dp(value, along, offset, side):
    pairs = []
    for z in range(side):
        for x in range(side):
            if along == "z":
                source = ((z + offset) % side) * side + x
            else:
                source = z * side + (x + offset) % side
            pairs.append((source, z * side + x))
    return lax.ppermute(value, "dp", pairs)


def scatter_dp(value, along, at, side):
    value = jnp.pad(value, ((0, -value.shape[0] % (8 * side)), (0, 0)))
    rows = value.shape[0] // side
    block = lambda j: lax.dynamic_slice_in_dim(value, ((at + j) % side) * rows, rows, 0)
    got = [shift_dp(block(j), along, -j, side) for j in (1, side - 1, 2)]
    total = block(0).astype(F32)
    for part in got:
        total = total + part.astype(F32)
    return total.astype(BF16)


def gather_dp_ring(value, along, side):
    third, first = shift_dp(value, along, -1, side), shift_dp(value, along, 1, side)
    middle = value.shape[0] // 2
    upper = shift_dp(first[:middle], along, 1, side)
    lower = shift_dp(third[middle:], along, -1, side)
    return [value, first, jnp.concatenate([upper, lower], axis=0), third]


def gather_dp(value, along, side):
    got = {j: shift_dp(value, along, j, side) for j in (1, side - 1, 2)}
    return [value] + [got[j] for j in range(1, side)]


def body(
    layer_input,
    prefix,
    gain_one,
    w_query,
    b_query,
    w_keyval,
    b_keyval,
    w_out,
    gain_two,
    w_gate,
    w_up,
    w_down,
    cotangent,
):
    cols = lax.axis_size("col")
    groups = lax.axis_size("dp")
    side = int(round(groups**0.5))
    r = lax.axis_index("row")
    c = lax.axis_index("col")
    dp = lax.axis_index("dp")
    z_at, x_at = dp // side, dp % side
    core = r.astype(jnp.int32).reshape(1)
    rows_in, feat = layer_input.shape
    own = rows_in // 2
    tokens = own * cols
    width = 2 * feat
    qw = w_query.shape[1]
    kvw = w_keyval.shape[1] // 2
    share = cols // (kvw // HD)
    kv_head = c // share
    ff = w_gate.shape[1]
    part = ff // 2

    x_a = gather_col(layer_input)

    key_start = kv_head * HD
    w_qkv_a = jnp.concatenate(
        [
            w_query,
            lax.dynamic_slice_in_dim(w_keyval, key_start, HD, 1),
            lax.dynamic_slice_in_dim(w_keyval, kvw + key_start, HD, 1),
        ],
        axis=1,
    )
    bias = jnp.concatenate(
        [
            b_query,
            lax.dynamic_slice_in_dim(b_keyval, key_start, HD, 0),
            lax.dynamic_slice_in_dim(b_keyval, kvw + key_start, HD, 0),
        ]
    ).astype(F32)[None]
    w_qkv_b = swap_rows(w_qkv_a)
    gains_a = jnp.stack([gain_one, gain_two])
    gains = jnp.concatenate([gains_a, swap_rows(gains_a)], axis=1).astype(F32)
    gain_one_f, gain_two_f = gains[:1], gains[1:]

    kept = [w_gate.T, w_up.T, w_down]
    sent = [
        lax.dynamic_slice_in_dim(w, (1 - r) * part, part, 0)
        for w in kept
    ]
    sent = jnp.stack(sent)

    block_first = rows_in * ((c + jnp.arange(cols, dtype=jnp.int32)) % cols)
    inside = jnp.arange(own, dtype=jnp.int32)
    pos_own = ((block_first[:, None] + own * r + inside[None]) % SEQ_LEN).reshape(-1)
    pos_other = ((block_first[:, None] + own * (1 - r) + inside[None]) % SEQ_LEN).reshape(-1)
    query_pos = pos_own[:, None]
    key_pos = jnp.concatenate([pos_own, pos_other])[None, :]
    frequency = THETA ** (-jnp.arange(0, HD // 2, dtype=F32) * 2.0 / HD)
    angle = pos_own.astype(F32)[:, None] * frequency[None, :]
    cosine, sine = jnp.cos(angle), jnp.sin(angle)
    cosine = jnp.concatenate([cosine, cosine], axis=1)
    sine_to = jnp.concatenate([-sine, sine], axis=1)
    sine_back = jnp.concatenate([sine, -sine], axis=1)

    x_b = [swap_rows(v) for v in x_a]
    wo_a = gather_col_ring(after(w_out, *x_b, w_qkv_b))
    x_full, normed_one, query, kv_own = qkv_call(
        core, x_a, x_b, gain_one_f, w_qkv_a, w_qkv_b, bias, cosine, sine_to, qw, own
    )
    kv_other = swap_rows(kv_own)
    c_a = lax.all_gather(after(cotangent, *x_a[1:]), "col", axis=0, tiled=True)
    query = after(query, wo_a[1], wo_a[3])
    attended = attend_call(prefix, query, kv_own, kv_other, query_pos, key_pos, tokens)
    got = swap_rows(after(sent, attended))
    att = gather_col_ring(attended, (got,))
    wo_b = [swap_rows(v) for v in wo_a]
    resid, n2_a, n2_b = out_call(att, wo_a, wo_b, x_full, gain_two_f, own)
    n2_other_b, n2_other_a = swap_rows(n2_a), swap_rows(n2_b)


    gated_own = gated_call(core, n2_a, n2_b, kept, got, part // 2)
    gated_other = gated_call(core, n2_other_a, n2_other_b, kept, got, part // 2)

    c_b = swap_rows(after(c_a, gated_own[0]))
    place = after(jnp.stack([r, c]).astype(jnp.int32), gated_other[0])
    cot_a, cot_b = assemble_call(place, c_a, c_b, cols)

    def hidden_grads(half, gated):
        grads = hidden_grad_call(
            core, cot_a, cot_b, half, kept, got, gated[1], gated[2], part // 2
        )
        return [gated[0], *grads]

    hid_own = hidden_grads(0, gated_own)
    hid_other = hidden_grads(1, gated_other)

    def weight_grads(n_own, n_other, cot, own, other):
        return [
            wgrad_call(n_own, n_other, 0, own[1:], other[1:], part // 2),
            wgrad_call(cot, cot, 1, own[:1], other[:1], part // 2),
        ]

    big_b = weight_grads(n2_b, n2_other_b, cot_b, hid_own, hid_other)
    big_a = weight_grads(n2_a, n2_other_a, cot_a, hid_own, hid_other)
    own_grads = (*big_a, *big_b)
    big = lax.psum(own_grads, "dp")

    def sum_cores(own_pair, other_pair):
        from_b, from_a = swap_rows(other_pair[0]), swap_rows(other_pair[1])
        a = own_pair[0].astype(F32) + from_a.astype(F32)
        b = own_pair[1].astype(F32) + from_b.astype(F32)
        return jnp.concatenate([a, b], axis=1).astype(BF16)

    def token_blocks(value):
        return [value[j * own : (j + 1) * own] for j in range(cols)]

    back_own = [after(v, *own_grads) for v in hid_own[1:]]
    terms = back_call(core, back_own, hid_other[1:], kept[:2], got, 0)
    grad_normed_two = scatter_col(token_blocks(sum_cores(terms[:2], terms[2:])))


    def norm_backward(grad, value, gain):
        inverse = lax.rsqrt(jnp.mean(value * value, axis=1, keepdims=True) + EPS)
        unit = value * inverse
        scaled = grad * gain
        mean_term = jnp.mean(scaled * unit, axis=1, keepdims=True)
        return inverse * (scaled - unit * mean_term), jnp.sum(grad * unit, axis=0, keepdims=True)

    grad_norm_two, grad_gain_two = norm_backward(grad_normed_two, resid, gain_two_f)
    cot_full = jnp.concatenate([cot_a[:own], cot_b[:own]], axis=1).astype(F32)
    grad_resid = cot_full + grad_norm_two
    resid_blocks = gather_col(grad_resid.astype(BF16))
    resid_low = jnp.concatenate(resid_blocks, axis=0)

    query_low, grad_b_query, gkv_own, gkv_sent = attend_back_call(
        prefix, resid_low, wo_a[0], wo_b[0], query, kv_own, kv_other,
        query_pos, key_pos, cosine, sine_back, tokens,
    )
    qkv_low, grad_b_kv, back_one = qkv_back_call(
        gkv_own, swap_rows(gkv_sent), query_low, cosine, sine_back, w_qkv_a, w_qkv_b
    )
    grad_normed_one = scatter_col(token_blocks(back_one))

    def exchange_out(value):
        mine, other = halves(value)
        other = swap_rows(other)
        return jnp.where(
            r == 0,
            jnp.concatenate([mine, other], axis=0),
            jnp.concatenate([other, mine], axis=0),
        )

    grad_norm_one, grad_gain_one = norm_backward(
        grad_normed_one, x_full[:own].astype(F32), gain_one_f
    )
    grad_input = exchange_out(grad_resid + grad_norm_one)

    mixed_other = after(hid_other[0], grad_resid)
    terms = back_call(core, hid_own[:1], [mixed_other], kept[2:], got, 2)
    down = token_blocks(sum_cores(terms[:2], terms[2:]))
    down = scatter_col([after(v, grad_normed_one) for v in down])
    output = exchange_out((resid + down).astype(BF16))

    in_a, in_b, out_a, out_b = rest_call(normed_one, qkv_low, attended, resid_low)
    rest = in_a.astype(F32) + swap_rows(in_b).astype(F32)
    grad_wout = out_a.astype(F32) + swap_rows(out_b).astype(F32)
    grad_wout = jnp.concatenate(halves(grad_wout), axis=0)
    rest = jnp.concatenate([grad_wout, rest], axis=1).astype(BF16)
    rest = scatter_dp(scatter_dp(rest, "x", x_at, side), "z", z_at, side)
    piece_rows = rest.shape[0]

    heads = kvw // HD
    mine, sent = pack_call(grad_gain_one, grad_gain_two, grad_b_kv, grad_b_query)
    message, small = message_call(mine, swap_rows(sent), rest)
    big_got = [swap_rows(after(v, message, output)) for v in big[2:]]
    message = after(message, big[0], output)
    chip = c.astype(jnp.int32).reshape(1)
    first, second = head_sum_call(chip, gather_col(message), small, rest, heads, width // HD)
    places = jnp.stack([x_at, z_at]).astype(jnp.int32)
    grad_w_gate = join_call(core, big[0], big_got[0], 0, 256)
    grad_w_up = join_call(core, big[0], big_got[0], 1, 256)
    grad_w_down = join_call(core, big[1], big_got[1], 0, 256)
    first, second = gather_dp(first, "z", side), gather_dp(second, "x", side)
    first, second = order_call(places, first, second)
    first, second = gather_dp(first, "x", side), gather_dp(second, "z", side)
    places = after(places, grad_w_gate, grad_w_up, grad_w_down)
    grad_wout, grad_wq, grad_wkv, one, two, bias_kv, bias_query = finish_call(
        places, first, second, qw, feat, heads
    )

    return (
        output,
        grad_input,
        one.reshape(-1),
        grad_wq,
        bias_query.reshape(-1),
        grad_wkv,
        bias_kv.reshape(-1),
        grad_wout,
        two.reshape(-1),
        grad_w_gate.T,
        grad_w_up.T,
        grad_w_down,
    )


def solution(mesh):
    return jax.shard_map(
        body,
        mesh=mesh,
        in_specs=(
            P(("dp", "col"), "row"),
            P("dp"),
            P("row"),
            P("row", "col"),
            P("col"),
            P("row", None),
            P(),
            P("col", "row"),
            P("row"),
            P("row", "col"),
            P("row", "col"),
            P("col", "row"),
            P(("dp", "col"), "row"),
        ),
        out_specs=(
            P(("dp", "col"), "row"),
            P(("dp", "col"), "row"),
            P("row"),
            P("row", "col"),
            P("col"),
            P("row", None),
            P(),
            P("col", "row"),
            P("row"),
            P("row", "col"),
            P("row", "col"),
            P("col", "row"),
        ),
        check_vma=False,
    )
```

```python
import functools

import jax
import jax.numpy as jnp
from jax import lax
from jax.experimental import pallas as pl
from jax.experimental.pallas import tpu as pltpu
from jax.sharding import PartitionSpec as P

HD = 128
SEQ_LEN = 1024
EPS = 1e-06
THETA = 1000000.0
NEG = -1e30
BF16 = jnp.bfloat16
F32 = jnp.float32
MIB = 1 << 20
SMALL_ROWS = 32
LITTLE = 1000
GRANT = 40


def dot_nn(left, right):
    return lax.dot_general(left, right, (((1,), (0,)), ((), ())), preferred_element_type=F32)


def dot_nt(left, right):
    return lax.dot_general(left, right, (((1,), (1,)), ((), ())), preferred_element_type=F32)


def dot_tn(left, right):
    return lax.dot_general(left, right, (((0,), (0,)), ((), ())), preferred_element_type=F32)


def params(mib):
    return pltpu.CompilerParams(vmem_limit_bytes=mib * MIB)


def cost(flops, nbytes):
    return pl.CostEstimate(flops=int(flops), bytes_accessed=int(nbytes), transcendentals=0)


def rope(value, cosine, sine):
    return value * cosine + pltpu.roll(value, HD // 2, 1) * sine


def qkv_kernel(cols, own, *refs):
    r_ref, refs = refs[0], refs[1:]
    xa, refs = refs[:cols], refs[cols:]
    xb, refs = refs[:cols], refs[cols:]
    gain, wa, wb, bias, cosine, sine, x_out, n_out, q_out, kv_out = refs
    feat = xa[0].shape[1]
    for j in range(cols):
        rows = pl.ds(j * own, own)
        a = xa[j][...].astype(F32)
        b = xb[j][...].astype(F32)
        total = jnp.sum(a * a, axis=1, keepdims=True) + jnp.sum(b * b, axis=1, keepdims=True)
        inverse = lax.rsqrt(total / (2 * feat) + EPS)
        x_out[rows, :feat] = xa[j][...]
        x_out[rows, feat:] = xb[j][...]
        n_out[rows, :feat] = (a * inverse * gain[:, :feat]).astype(BF16)
        n_out[rows, feat:] = (b * inverse * gain[:, feat:]).astype(BF16)
    qkv = dot_nn(n_out[:, :feat], wa[...]) + dot_nn(n_out[:, feat:], wb[...]) + bias[...]
    qw = q_out.shape[1]
    for h in range(qw // HD):
        at = slice(h * HD, (h + 1) * HD)
        q_out[:, at] = rope(qkv[:, at], cosine[...], sine[...]).astype(BF16)
    kv_out[:, :HD] = rope(qkv[:, qw : qw + HD], cosine[...], sine[...]).astype(BF16)
    kv_out[:, HD:] = qkv[:, qw + HD :].astype(BF16)


def qkv_call(r, xa, xb, gain, wa, wb, bias, cosine, sine, qw, own):
    cols = len(xa)
    feat = xa[0].shape[1]
    tokens = own * cols
    whole = lambda v: pl.BlockSpec(v.shape, lambda i, r: (0,) * v.ndim)
    rest = [gain, wa, wb, bias, cosine, sine]
    outs = [
        jax.ShapeDtypeStruct((tokens, 2 * feat), BF16),
        jax.ShapeDtypeStruct((tokens, 2 * feat), BF16),
        jax.ShapeDtypeStruct((tokens, qw), BF16),
        jax.ShapeDtypeStruct((tokens, 2 * HD), BF16),
    ]
    return pl.pallas_call(
        functools.partial(qkv_kernel, cols, own),
        grid_spec=pltpu.PrefetchScalarGridSpec(
            num_scalar_prefetch=1,
            grid=(1,),
            in_specs=[pl.BlockSpec((own, feat), lambda i, r: (r[0], 0))] * (2 * cols)
            + [whole(v) for v in rest],
            out_specs=[whole(o) for o in outs],
        ),
        out_shape=outs,
        compiler_params=params(40),
        cost_estimate=cost(LITTLE, LITTLE),
        name="qkv",
    )(r, *xa, *xb, *rest)


def softmax(q, k, visible, scaling):
    scores = jnp.where(visible, dot_nt(q, k) * scaling, NEG)
    e = jnp.exp(scores - jnp.max(scores, axis=1, keepdims=True))
    return e * (1.0 / jnp.sum(e, axis=1, keepdims=True))


def visibility(qpos, kpos, prefix_ref):
    return (kpos <= qpos) | (kpos < prefix_ref[0])


def attend_kernel(scaling, prefix, q, kv_a, kv_b, qpos, kpos, out):
    visible = visibility(qpos[...], kpos[...], prefix)
    keys = jnp.concatenate([kv_a[:, :HD], kv_b[:, :HD]], axis=0)
    values = jnp.concatenate([kv_a[:, HD:], kv_b[:, HD:]], axis=0)
    for h in range(q.shape[1] // HD):
        at = slice(h * HD, (h + 1) * HD)
        weights = softmax(q[:, at], keys, visible, scaling)
        out[:, at] = dot_nn(weights.astype(BF16), values).astype(BF16)


def attend_call(prefix, q, kv_a, kv_b, qpos, kpos, block):
    tokens, qw = q.shape
    whole = lambda v: pl.BlockSpec(v.shape, lambda i, p: (0,) * v.ndim)
    part = lambda v: pl.BlockSpec((block, v.shape[1]), lambda i, p: (i, 0))
    return pl.pallas_call(
        functools.partial(attend_kernel, HD**-0.5),
        grid_spec=pltpu.PrefetchScalarGridSpec(
            num_scalar_prefetch=1,
            grid=(tokens // block,),
            in_specs=[part(q), whole(kv_a), whole(kv_b), part(qpos), whole(kpos)],
            out_specs=part(q),
        ),
        out_shape=jax.ShapeDtypeStruct(q.shape, BF16),
        compiler_params=params(32),
        cost_estimate=cost(LITTLE, LITTLE),
        name="attend",
    )(prefix, q, kv_a, kv_b, qpos, kpos)


def out_kernel(cols, own, *refs):
    att, refs = refs[:cols], refs[cols:]
    wa, refs = refs[:cols], refs[cols:]
    wb, refs = refs[:cols], refs[cols:]
    xa, xb, gain, resid_out, na, nb, acc_a, acc_b = refs
    step, steps = pl.program_id(0), pl.num_programs(0)
    chunk = xa.shape[1]
    feat = chunk * steps

    rolled = []
    for j in range(cols):
        tiles = [att[j][((i - j) % cols) * own : ((i - j) % cols + 1) * own, :] for i in range(cols)]
        rolled.append(jnp.concatenate(tiles, axis=0))
    at = pl.ds(pl.multiple_of(step * chunk, 128), chunk)
    for x, w, acc in ((xa, wa, acc_a), (xb, wb, acc_b)):
        total = x[...].astype(F32)
        for j in range(cols):
            total = total + dot_nn(rolled[j], w[j][...])
        acc[:, at] = total

    @pl.when(step == steps - 1)
    def _():
        a, b = acc_a[...], acc_b[...]
        total = jnp.sum(a * a, axis=1, keepdims=True) + jnp.sum(b * b, axis=1, keepdims=True)
        inverse = lax.rsqrt(total / (2 * feat) + EPS)
        na[...] = (a * inverse * gain[:, :feat]).astype(BF16)
        nb[...] = (b * inverse * gain[:, feat:]).astype(BF16)
        resid_out[:, :feat] = acc_a[:own, :]
        resid_out[:, feat:] = acc_b[:own, :]


def out_call(att, wa, wb, x, gain, own):
    cols = len(att)
    tokens, qw = att[0].shape
    feat = wa[0].shape[1]
    steps = 3
    chunk = feat // steps
    whole = lambda v: pl.BlockSpec(v.shape, lambda i: (0,) * v.ndim)
    outs = [
        jax.ShapeDtypeStruct((own, 2 * feat), F32),
        jax.ShapeDtypeStruct((tokens, feat), BF16),
        jax.ShapeDtypeStruct((tokens, feat), BF16),
    ]
    return pl.pallas_call(
        functools.partial(out_kernel, cols, own),
        grid=(steps,),
        in_specs=[whole(a) for a in att]
        + [pl.BlockSpec((qw, chunk), lambda i: (0, i))] * (2 * cols)
        + [
            pl.BlockSpec((tokens, chunk), lambda i: (0, i)),
            pl.BlockSpec((tokens, chunk), lambda i: (0, steps + i)),
            whole(gain),
        ],
        out_specs=[whole(o) for o in outs],
        out_shape=outs,
        scratch_shapes=[pltpu.VMEM((tokens, feat), F32)] * 2,
        compiler_params=params(40),
        cost_estimate=cost(LITTLE, LITTLE),
        name="out_norm",
    )(*att, *wa, *wb, x, x, gain)


def assemble_kernel(cols, meta, ca, cb, out_a, out_b):
    rows = ca.shape[0] // cols
    own = rows // 2
    tokens = cols * own
    r, c = meta[0], meta[1]
    for j in range(cols):
        at = lax.rem(c + j, cols) * rows
        for src, out in ((ca, out_a), (cb, out_b)):
            out[j * own : (j + 1) * own, :] = src[pl.ds(at + r * own, own), :]
            out[tokens + j * own : tokens + (j + 1) * own, :] = src[
                pl.ds(at + (1 - r) * own, own), :
            ]


def assemble_call(meta, ca, cb, cols):
    out = jax.ShapeDtypeStruct(ca.shape, BF16)
    return pl.pallas_call(
        functools.partial(assemble_kernel, cols),
        in_specs=[pl.BlockSpec(memory_space=pltpu.SMEM)]
        + [pl.BlockSpec(memory_space=pltpu.VMEM)] * 2,
        out_specs=[pl.BlockSpec(memory_space=pltpu.VMEM)] * 2,
        out_shape=[out, out],
        compiler_params=params(24),
        cost_estimate=cost(LITTLE, LITTLE),
        name="assemble",
    )(meta, ca, cb)


def gated_kernel(na, nb, ga, gb, ua, ub, mixed, to_gate, to_up):
    gate = dot_nt(ga[...], na[...]) + dot_nt(gb[...], nb[...])
    up = dot_nt(ua[...], na[...]) + dot_nt(ub[...], nb[...])
    s = 0.5 * jnp.tanh(0.5 * gate) + 0.5
    silu = gate * s
    mixed[...] = (silu * up).astype(BF16)
    to_gate[...] = (up * (s + silu * (1.0 - s))).astype(BF16)
    to_up[...] = silu.astype(BF16)


def hidden_grad_kernel(ca, cb, da, db, to_gate, to_up, grad_gate, grad_up):
    grad_mixed = dot_nt(da[...], ca[...]) + dot_nt(db[...], cb[...])
    grad_gate[...] = (grad_mixed * to_gate[...].astype(F32)).astype(BF16)
    grad_up[...] = (grad_mixed * to_up[...].astype(F32)).astype(BF16)


def gated_call(r, na, nb, kept, got, chunk):
    tokens, feat = na.shape
    part = got.shape[1]
    steps = part // chunk
    act = pl.BlockSpec((tokens, feat), lambda i, r: (0, 0))
    mine = pl.BlockSpec((chunk, feat), lambda i, r: (r[0] * steps + i, 0))
    other = lambda k: pl.BlockSpec((None, chunk, feat), lambda i, r: (k, i, 0))
    return pl.pallas_call(
        lambda r, *refs: gated_kernel(*refs),
        grid_spec=pltpu.PrefetchScalarGridSpec(
            num_scalar_prefetch=1,
            grid=(steps,),
            in_specs=[act, act, mine, other(0), mine, other(1)],
            out_specs=[pl.BlockSpec((chunk, tokens), lambda i, r: (i, 0))] * 3,
        ),
        out_shape=[jax.ShapeDtypeStruct((part, tokens), BF16)] * 3,
        compiler_params=params(GRANT),
        cost_estimate=cost(LITTLE, LITTLE),
        name="gated",
    )(r, na, nb, kept[0], got, kept[1], got)


def hidden_grad_call(r, ca, cb, half, kept, got, to_gate, to_up, chunk):
    part, tokens = to_gate.shape
    feat = ca.shape[1]
    steps = part // chunk
    cot = pl.BlockSpec((tokens, feat), lambda i, r: (half, 0))
    hid = pl.BlockSpec((chunk, tokens), lambda i, r: (i, 0))
    return pl.pallas_call(
        lambda r, *refs: hidden_grad_kernel(*refs),
        grid_spec=pltpu.PrefetchScalarGridSpec(
            num_scalar_prefetch=1,
            grid=(steps,),
            in_specs=[
                cot,
                cot,
                pl.BlockSpec((chunk, feat), lambda i, r: (r[0] * steps + i, 0)),
                pl.BlockSpec((None, chunk, feat), lambda i, r: (2, i, 0)),
                hid,
                hid,
            ],
            out_specs=[hid, hid],
        ),
        out_shape=[jax.ShapeDtypeStruct((part, tokens), BF16)] * 2,
        compiler_params=params(GRANT),
        cost_estimate=cost(LITTLE, LITTLE),
        name="hidden_grads",
    )(r, ca, cb, kept[2], got, to_gate, to_up)


def wgrad_kernel(pairs, act_own, act_other, *refs):
    own, other, out = refs[:pairs], refs[pairs : 2 * pairs], refs[2 * pairs]
    for k in range(pairs):
        total = dot_nn(own[k][...], act_own[...]) + dot_nn(other[k][...], act_other[...])
        out[k] = total.astype(BF16)


def wgrad_call(act_own, act_other, other_block, hidden_own, hidden_other, chunk):
    pairs = len(hidden_own)
    part, tokens = hidden_own[0].shape
    feat = act_own.shape[1]
    hid = pl.BlockSpec((chunk, tokens), lambda i: (i, 0))
    return pl.pallas_call(
        functools.partial(wgrad_kernel, pairs),
        grid=(part // chunk,),
        in_specs=[
            pl.BlockSpec((tokens, feat), lambda i: (0, 0)),
            pl.BlockSpec((tokens, feat), lambda i: (other_block, 0)),
        ]
        + [hid] * (2 * pairs),
        out_specs=pl.BlockSpec((pairs, chunk, feat), lambda i: (0, i, 0)),
        out_shape=jax.ShapeDtypeStruct((pairs, part, feat), BF16),
        compiler_params=params(GRANT),
        cost_estimate=cost(LITTLE, LITTLE),
        name="weight_grads",
    )(act_own, act_other, *hidden_own, *hidden_other)


def back_kernel(pairs, *refs):
    hidden, refs = (refs[:pairs], refs[pairs : 2 * pairs]), refs[2 * pairs :]
    wa, refs = refs[:pairs], refs[pairs:]
    wb, outs = refs[:pairs], refs[pairs:]
    for half in (1, 0):
        for w, out in ((wa, outs[2 * half]), (wb, outs[2 * half + 1])):
            total = dot_tn(hidden[half][0][...], w[0][...])
            for i in range(1, pairs):
                total = total + dot_tn(hidden[half][i][...], w[i][...])
            out[...] = total.astype(out.dtype)


def back_call(r, own, other, kept, got, first):
    pairs = len(own)
    part, tokens = own[0].shape
    feat = got.shape[2]
    out = jax.ShapeDtypeStruct((tokens, feat), BF16)
    of_other = lambda k: pl.BlockSpec((None, part, feat), lambda i, r: (first + k, 0, 0))
    return pl.pallas_call(
        lambda r, *refs: back_kernel(pairs, *refs),
        grid_spec=pltpu.PrefetchScalarGridSpec(
            num_scalar_prefetch=1,
            grid=(1,),
            in_specs=[pl.BlockSpec((part, tokens), lambda i, r: (0, 0))] * (2 * pairs)
            + [pl.BlockSpec((part, feat), lambda i, r: (r[0], 0))] * pairs
            + [of_other(k) for k in range(pairs)],
            out_specs=[pl.BlockSpec((tokens, feat), lambda i, r: (0, 0))] * 4,
        ),
        out_shape=[out] * 4,
        compiler_params=params(GRANT),
        cost_estimate=cost(LITTLE, LITTLE),
        name="back_in",
    )(r, *own, *other, *kept, *([got] * pairs))


def attend_back_kernel(
    scaling, own, prefix, *refs
):
    (gr, wa, wb, q, kv_a, kv_b, qpos, kpos, cosine, sine,
     low_out, sum_out, gkv_own, gkv_send, gk, gv, ga_s) = refs
    step, steps = pl.program_id(0), pl.num_programs(0)
    feat = wa.shape[1]
    visible = visibility(qpos[...], kpos[...], prefix)
    keys = jnp.concatenate([kv_a[:, :HD], kv_b[:, :HD]], axis=0)
    values = jnp.concatenate([kv_a[:, HD:], kv_b[:, HD:]], axis=0)
    ga_s[...] = (dot_nt(gr[:, :feat], wa[...]) + dot_nt(gr[:, feat:], wb[...])).astype(BF16)

    @pl.when(step == 0)
    def _():
        gk[...] = jnp.zeros_like(gk)
        gv[...] = jnp.zeros_like(gv)
        sum_out[...] = jnp.zeros_like(sum_out)

    for h in range(q.shape[1] // HD):
        at = slice(h * HD, (h + 1) * HD)
        weights = softmax(q[:, at], keys, visible, scaling)
        grad_att = ga_s[:, at]
        gw = dot_nt(grad_att, values)
        inner = jnp.sum(weights * gw, axis=1, keepdims=True)
        gs = (weights * (gw - inner)).astype(BF16)
        gk[...] += dot_tn(gs, q[:, at])
        gv[...] += dot_tn(weights.astype(BF16), grad_att)
        grad_q = dot_nn(gs, keys) * scaling
        grad_q = rope(grad_q, cosine[...], sine[...])
        low_out[:, at] = grad_q.astype(BF16)
        sum_out[:, at] += jnp.sum(grad_q, axis=0, keepdims=True)

    @pl.when(step == steps - 1)
    def _():
        half = gk.shape[0] // 2
        gkv_own[:, :HD] = gk[:half, :] * scaling
        gkv_own[:, HD:] = gv[:half, :]
        gkv_send[:, :HD] = (gk[half:, :] * scaling).astype(BF16)
        gkv_send[:, HD:] = gv[half:, :].astype(BF16)


def attend_back_call(prefix, gr, wa, wb, q, kv_a, kv_b, qpos, kpos, cosine, sine, block):
    tokens, qw = q.shape
    whole = lambda v: pl.BlockSpec(v.shape, lambda i, p: (0,) * v.ndim)
    part = lambda v: pl.BlockSpec((block, v.shape[1]), lambda i, p: (i, 0))
    outs = [
        jax.ShapeDtypeStruct((tokens, qw), BF16),
        jax.ShapeDtypeStruct((1, qw), F32),
        jax.ShapeDtypeStruct((tokens, 2 * HD), F32),
        jax.ShapeDtypeStruct((tokens, 2 * HD), BF16),
    ]
    keys = 2 * tokens
    return pl.pallas_call(
        functools.partial(attend_back_kernel, HD**-0.5, block),
        grid_spec=pltpu.PrefetchScalarGridSpec(
            num_scalar_prefetch=1,
            grid=(tokens // block,),
            in_specs=[
                part(gr), whole(wa), whole(wb), part(q), whole(kv_a), whole(kv_b),
                part(qpos), whole(kpos), part(cosine), part(sine),
            ],
            out_specs=[part(outs[0]), whole(outs[1]), whole(outs[2]), whole(outs[3])],
            scratch_shapes=[
                pltpu.VMEM((keys, HD), F32),
                pltpu.VMEM((keys, HD), F32),
                pltpu.VMEM((block, qw), BF16),
            ],
        ),
        out_shape=outs,
        compiler_params=params(40),
        cost_estimate=cost(LITTLE, LITTLE),
        name="attend_back",
    )(prefix, gr, wa, wb, q, kv_a, kv_b, qpos, kpos, cosine, sine)


def qkv_back_kernel(own, got, query_low, cosine, sine, wa, wb, low, sums, back):
    qw = query_low.shape[1]
    total = own[...] + got[...].astype(F32)
    key = rope(total[:, :HD], cosine[...], sine[...])
    value = total[:, HD:]
    sums[:, :HD] = jnp.sum(key, axis=0, keepdims=True)
    sums[:, HD:] = jnp.sum(value, axis=0, keepdims=True)
    low[:, :qw] = query_low[...]
    low[:, qw : qw + HD] = key.astype(BF16)
    low[:, qw + HD :] = value.astype(BF16)
    feat = wa.shape[0]
    back[:, :feat] = dot_nt(low[...], wa[...]).astype(BF16)
    back[:, feat:] = dot_nt(low[...], wb[...]).astype(BF16)


def qkv_back_call(own, got, query_low, cosine, sine, wa, wb):
    tokens = own.shape[0]
    feat, columns = wa.shape
    return pl.pallas_call(
        qkv_back_kernel,
        out_shape=[
            jax.ShapeDtypeStruct((tokens, columns), BF16),
            jax.ShapeDtypeStruct((1, 2 * HD), F32),
            jax.ShapeDtypeStruct((tokens, 2 * feat), BF16),
        ],
        compiler_params=params(32),
        cost_estimate=cost(LITTLE, LITTLE),
        name="qkv_back",
    )(own, got, query_low, cosine, sine, wa, wb)


def rest_kernel(n1, low, attended, grad, in_a, in_b, out_a, out_b):
    feat = n1.shape[1] // 2
    in_b[...] = dot_tn(n1[:, feat:], low[...]).astype(BF16)
    out_b[...] = dot_tn(attended[...], grad[:, feat:]).astype(BF16)
    in_a[...] = dot_tn(n1[:, :feat], low[...]).astype(BF16)
    out_a[...] = dot_tn(attended[...], grad[:, :feat]).astype(BF16)


def rest_call(n1, low, attended, grad):
    feat = n1.shape[1] // 2
    into = jax.ShapeDtypeStruct((feat, low.shape[1]), BF16)
    out = jax.ShapeDtypeStruct((attended.shape[1], feat), BF16)
    return pl.pallas_call(
        rest_kernel,
        out_shape=[into, into, out, out],
        compiler_params=params(32),
        cost_estimate=cost(LITTLE, LITTLE),
        name="rest",
    )(n1, low, attended, grad)


def join_kernel(r_ref, kept, got, out):
    part = kept.shape[0]

    @pl.when(r_ref[0] == 0)
    def _():
        out[:part, :] = kept[...].astype(F32)
        out[part:, :] = got[...].astype(F32)

    @pl.when(r_ref[0] != 0)
    def _():
        out[:part, :] = got[...].astype(F32)
        out[part:, :] = kept[...].astype(F32)


def join_call(r, kept, got, which, chunk):
    part, feat = kept.shape[1:]
    half = pl.BlockSpec((None, part, chunk), lambda i, r: (which, 0, i))
    return pl.pallas_call(
        join_kernel,
        grid_spec=pltpu.PrefetchScalarGridSpec(
            num_scalar_prefetch=1,
            grid=(feat // chunk,),
            in_specs=[half, half],
            out_specs=pl.BlockSpec((2 * part, chunk), lambda i, r: (0, i)),
        ),
        out_shape=jax.ShapeDtypeStruct((2 * part, feat), F32),
        compiler_params=params(32),
        cost_estimate=cost(LITTLE, LITTLE),
        name="join",
    )(r, kept, got)


def pack_kernel(one, two, bias_kv, bias_query, mine, sent):
    feat = one.shape[1] // 2
    for out, first in ((mine, 0), (sent, feat)):
        out[...] = jnp.zeros_like(out)
        at = 0
        for vector, start, size in (
            (one, first, feat),
            (two, first, feat),
            (bias_kv, 0, bias_kv.shape[1]),
            (bias_query, 0, bias_query.shape[1]),
        ):
            for k in range(size // HD):
                out[at : at + 1, :] = vector[:, start + k * HD : start + (k + 1) * HD]
                at += 1


def pack_call(one, two, bias_kv, bias_query):
    out = jax.ShapeDtypeStruct((SMALL_ROWS, HD), F32)
    return pl.pallas_call(
        pack_kernel,
        out_shape=[out, out],
        cost_estimate=cost(LITTLE, LITTLE),
        name="pack",
    )(one, two, bias_kv, bias_query)


def message_kernel(mine, got, rest, out, small):
    rows = rest.shape[0]
    total = mine[...] + got[...]
    small[...] = total
    out[:rows, :] = rest[:, rest.shape[1] - 2 * HD :]
    out[rows:, :HD] = total.astype(BF16)
    out[rows:, HD:] = jnp.zeros((SMALL_ROWS, HD), BF16)


def message_call(mine, got, rest):
    rows = rest.shape[0]
    return pl.pallas_call(
        message_kernel,
        out_shape=[
            jax.ShapeDtypeStruct((rows + SMALL_ROWS, 2 * HD), BF16),
            jax.ShapeDtypeStruct((SMALL_ROWS, HD), F32),
        ],
        cost_estimate=cost(LITTLE, LITTLE),
        name="message",
    )(mine, got, rest)


def head_sum_kernel(cols, heads, gain_rows, chip, *refs):
    messages, (small, rest, out_a, out_b, total) = refs[:cols], refs[cols:]
    rows, columns = rest.shape
    half = out_a.shape[1]
    share = cols // heads
    total[...] = jnp.zeros_like(total)
    total[:gain_rows, :] = sum(m[rows : rows + gain_rows, :HD].astype(F32) for m in messages)
    for head in range(heads):
        both = jnp.zeros((rows, 2 * HD), F32)
        bias = jnp.zeros((SMALL_ROWS, HD), F32)
        for j in range(cols):
            same = jnp.where(lax.rem(chip[0] + j, cols) // share == head, 1.0, 0.0)
            both = both + same * messages[j][:rows, :].astype(F32)
            bias = bias + same * messages[j][rows:, :HD].astype(F32)
        own_columns = columns - 2 * HD - half
        at = own_columns + head * HD
        out_b[:, at : at + HD] = both[:, :HD].astype(BF16)
        at += heads * HD
        out_b[:, at : at + HD] = both[:, HD:].astype(BF16)
        for k in range(2):
            row = gain_rows + k * heads + head
            total[row : row + 1, :] = bias[gain_rows + k : gain_rows + k + 1, :]
    queries = small[gain_rows + 2 :, :]
    first = gain_rows + 2 * heads
    total[first:, :] = queries[: SMALL_ROWS - first, :]
    out_a[:rows, :] = rest[:, :half]
    out_b[:, : columns - 2 * HD - half] = rest[:, half : columns - 2 * HD]
    out_a[rows:, :HD] = total[...].astype(BF16)
    out_a[rows:, HD:] = jnp.zeros((SMALL_ROWS, half - HD), BF16)


def head_sum_call(chip, messages, small, rest, heads, gain_rows):
    rows, columns = rest.shape
    half = (columns + 2 * HD * (heads - 1)) // 2
    vmem = pl.BlockSpec(memory_space=pltpu.VMEM)
    return pl.pallas_call(
        functools.partial(head_sum_kernel, len(messages), heads, gain_rows),
        in_specs=[pl.BlockSpec(memory_space=pltpu.SMEM)] + [vmem] * (len(messages) + 2),
        out_specs=[vmem, vmem],
        out_shape=[
            jax.ShapeDtypeStruct((rows + SMALL_ROWS, half), BF16),
            jax.ShapeDtypeStruct((rows, half), BF16),
        ],
        scratch_shapes=[pltpu.VMEM((SMALL_ROWS, HD), F32)],
        cost_estimate=cost(LITTLE, LITTLE),
        name="head_sums",
    )(chip, *messages, small, rest)


def order_kernel(side, places, *refs):
    first, second, (out_a, out_b) = refs[:side], refs[side : 2 * side], refs[2 * side :]
    rows = second[0].shape[0]
    for i in range(side):
        at = lax.rem(places[1] + i, side) * rows
        out_a[pl.ds(pl.multiple_of(at, 16), rows), :] = first[i][:rows, :]
        at = lax.rem(places[0] + i, side) * rows
        out_b[pl.ds(pl.multiple_of(at, 16), rows), :] = second[i][...]
    total = sum(v[rows:, :].astype(F32) for v in first)
    out_a[side * rows :, :] = total.astype(BF16)


def order_call(places, first, second):
    side = len(first)
    rows, half = second[0].shape
    vmem = pl.BlockSpec(memory_space=pltpu.VMEM)
    return pl.pallas_call(
        functools.partial(order_kernel, side),
        in_specs=[pl.BlockSpec(memory_space=pltpu.SMEM)] + [vmem] * (2 * side),
        out_specs=[vmem, vmem],
        out_shape=[
            jax.ShapeDtypeStruct((side * rows + SMALL_ROWS, half), BF16),
            jax.ShapeDtypeStruct((side * rows, half), BF16),
        ],
        cost_estimate=cost(LITTLE, LITTLE),
        name="order",
    )(places, *first, *second)


def finish_kernel(side, heads, places, *refs):
    first, second, outs = refs[:side], refs[side : 2 * side], refs[2 * side :]
    w_out, w_query, w_keyval, one, two, bias_kv, bias_query, total = outs
    qw = w_query.shape[1]
    block, half = second[0].shape
    rows = block // side
    count = qw // block
    for i in range(side):
        at = lax.rem(places[0] + i, side)
        place = pl.ds(pl.multiple_of(at * block, 16), block)
        w_query[place, : half - qw] = first[i][:block, qw:].astype(F32)
        values = first[i][:block, :qw].astype(F32)

        @pl.when(at < count)
        def _():
            w_out[pl.ds(pl.multiple_of(at * block, 16), block), :qw] = values

        @pl.when(at >= count)
        def _():
            w_out[pl.ds(pl.multiple_of((at - count) * block, 16), block), qw:] = values

        at = lax.rem(places[1] + i, side)
        for k in range(side):
            place = pl.ds(pl.multiple_of(k * block + at * rows, 16), rows)
            piece = second[i][k * rows : (k + 1) * rows, :].astype(F32)
            w_query[place, half - qw :] = piece[:, : 2 * qw - half]
            w_keyval[place, :] = piece[:, 2 * qw - half :]
    total[...] = sum(v[block:, :HD].astype(F32) for v in first)
    at = 0
    for out in (one, two, bias_kv, bias_query):
        out[...] = total[at : at + out.shape[0], :]
        at += out.shape[0]


def finish_call(places, first, second, qw, feat, heads):
    side = len(first)
    vmem = pl.BlockSpec(memory_space=pltpu.VMEM)
    shapes = [(qw, feat), (feat, qw), (feat, 2 * heads * HD)]
    shapes += [(feat // HD, HD), (feat // HD, HD), (2 * heads, HD), (qw // HD, HD)]
    return pl.pallas_call(
        functools.partial(finish_kernel, side, heads),
        in_specs=[pl.BlockSpec(memory_space=pltpu.SMEM)] + [vmem] * (2 * side),
        out_specs=[vmem] * len(shapes),
        out_shape=[jax.ShapeDtypeStruct(s, F32) for s in shapes],
        scratch_shapes=[pltpu.VMEM((SMALL_ROWS, HD), F32)],
        compiler_params=params(32),
        cost_estimate=cost(LITTLE, LITTLE),
        name="finish",
    )(places, *first, *second)
def after(value, *others):
    return lax.optimization_barrier((value,) + others)[0]


def swap_rows(value):
    return lax.ppermute(value, "row", [(0, 1), (1, 0)])


def from_col(value, offset):
    count = lax.axis_size("col")
    return lax.ppermute(value, "col", [((i + offset) % count, i) for i in range(count)])


def gather_col(value):
    third, first = from_col(value, -1), from_col(value, 1)
    return [value, first, from_col(value, 2), third]


def gather_col_ring(value, behind=()):
    third, first = from_col(value, -1), from_col(value, 1)
    middle = value.shape[0] // 2
    upper = from_col(after(first, *behind)[:middle], 1)
    lower = from_col(after(third, *behind)[middle:], -1)
    return [value, first, jnp.concatenate([upper, lower], axis=0), third]


def scatter_col(blocks, behind=()):
    third, first, second = (
        from_col(blocks[3], 1),
        from_col(blocks[1], -1),
        from_col(blocks[2], -2),
    )
    total = blocks[0].astype(F32)
    for part in (first, second, third):
        total = total + after(part, *behind).astype(F32)
    return total


def halves(value):
    middle = value.shape[-1] // 2
    return value[..., :middle], value[..., middle:]


def roll_blocks(value, shift, axis):
    size = value.shape[axis]
    twice = jnp.concatenate([value, value], axis=axis)
    return lax.dynamic_slice_in_dim(twice, shift, size, axis)


def shift_dp(value, along, offset, side):
    pairs = []
    for z in range(side):
        for x in range(side):
            if along == "z":
                source = ((z + offset) % side) * side + x
            else:
                source = z * side + (x + offset) % side
            pairs.append((source, z * side + x))
    return lax.ppermute(value, "dp", pairs)


def scatter_dp(value, along, at, side):
    value = jnp.pad(value, ((0, -value.shape[0] % (8 * side)), (0, 0)))
    rows = value.shape[0] // side
    block = lambda j: lax.dynamic_slice_in_dim(value, ((at + j) % side) * rows, rows, 0)
    got = [shift_dp(block(j), along, -j, side) for j in (1, side - 1, 2)]
    total = block(0).astype(F32)
    for part in got:
        total = total + part.astype(F32)
    return total.astype(BF16)


def gather_dp_ring(value, along, side):
    third, first = shift_dp(value, along, -1, side), shift_dp(value, along, 1, side)
    middle = value.shape[0] // 2
    upper = shift_dp(first[:middle], along, 1, side)
    lower = shift_dp(third[middle:], along, -1, side)
    return [value, first, jnp.concatenate([upper, lower], axis=0), third]


def gather_dp(value, along, side):
    got = {j: shift_dp(value, along, j, side) for j in (1, side - 1, 2)}
    return [value] + [got[j] for j in range(1, side)]


def body(
    layer_input,
    prefix,
    gain_one,
    w_query,
    b_query,
    w_keyval,
    b_keyval,
    w_out,
    gain_two,
    w_gate,
    w_up,
    w_down,
    cotangent,
):
    cols = lax.axis_size("col")
    groups = lax.axis_size("dp")
    side = int(round(groups**0.5))
    r = lax.axis_index("row")
    c = lax.axis_index("col")
    dp = lax.axis_index("dp")
    z_at, x_at = dp // side, dp % side
    core = r.astype(jnp.int32).reshape(1)
    rows_in, feat = layer_input.shape
    own = rows_in // 2
    tokens = own * cols
    width = 2 * feat
    qw = w_query.shape[1]
    kvw = w_keyval.shape[1] // 2
    share = cols // (kvw // HD)
    kv_head = c // share
    ff = w_gate.shape[1]
    part = ff // 2

    x_a = gather_col(layer_input)

    key_start = kv_head * HD
    w_qkv_a = jnp.concatenate(
        [
            w_query,
            lax.dynamic_slice_in_dim(w_keyval, key_start, HD, 1),
            lax.dynamic_slice_in_dim(w_keyval, kvw + key_start, HD, 1),
        ],
        axis=1,
    )
    bias = jnp.concatenate(
        [
            b_query,
            lax.dynamic_slice_in_dim(b_keyval, key_start, HD, 0),
            lax.dynamic_slice_in_dim(b_keyval, kvw + key_start, HD, 0),
        ]
    ).astype(F32)[None]
    w_qkv_b = swap_rows(w_qkv_a)
    gains_a = jnp.stack([gain_one, gain_two])
    gains = jnp.concatenate([gains_a, swap_rows(gains_a)], axis=1).astype(F32)
    gain_one_f, gain_two_f = gains[:1], gains[1:]

    kept = [w_gate.T, w_up.T, w_down]
    sent = [
        lax.dynamic_slice_in_dim(w, (1 - r) * part, part, 0)
        for w in kept
    ]
    sent = jnp.stack(sent)

    block_first = rows_in * ((c + jnp.arange(cols, dtype=jnp.int32)) % cols)
    inside = jnp.arange(own, dtype=jnp.int32)
    pos_own = ((block_first[:, None] + own * r + inside[None]) % SEQ_LEN).reshape(-1)
    pos_other = ((block_first[:, None] + own * (1 - r) + inside[None]) % SEQ_LEN).reshape(-1)
    query_pos = pos_own[:, None]
    key_pos = jnp.concatenate([pos_own, pos_other])[None, :]
    frequency = THETA ** (-jnp.arange(0, HD // 2, dtype=F32) * 2.0 / HD)
    angle = pos_own.astype(F32)[:, None] * frequency[None, :]
    cosine, sine = jnp.cos(angle), jnp.sin(angle)
    cosine = jnp.concatenate([cosine, cosine], axis=1)
    sine_to = jnp.concatenate([-sine, sine], axis=1)
    sine_back = jnp.concatenate([sine, -sine], axis=1)

    x_b = [swap_rows(v) for v in x_a]
    wo_a = gather_col_ring(after(w_out, *x_b, w_qkv_b))
    x_full, normed_one, query, kv_own = qkv_call(
        core, x_a, x_b, gain_one_f, w_qkv_a, w_qkv_b, bias, cosine, sine_to, qw, own
    )
    kv_other = swap_rows(kv_own)
    query = after(query, wo_a[1], wo_a[3])
    attended = attend_call(prefix, query, kv_own, kv_other, query_pos, key_pos, tokens)
    got = swap_rows(after(sent, attended))
    att = gather_col_ring(attended, (got,))
    wo_b = [swap_rows(v) for v in wo_a]
    c_a = lax.all_gather(after(cotangent, *att[1:]), "col", axis=0, tiled=True)
    resid, n2_a, n2_b = out_call(att, wo_a, wo_b, x_full, gain_two_f, own)
    n2_other_b, n2_other_a = swap_rows(n2_a), swap_rows(n2_b)


    gated_own = gated_call(
        core, after(n2_a, n2_other_a, n2_other_b), n2_b, kept, got, part // 2
    )
    gated_other = gated_call(core, n2_other_a, n2_other_b, kept, got, part // 2)

    c_b = swap_rows(after(c_a, gated_own[0]))
    place = after(jnp.stack([r, c]).astype(jnp.int32), gated_other[0])
    cot_a, cot_b = assemble_call(place, c_a, c_b, cols)

    def hidden_grads(half, gated):
        grads = hidden_grad_call(
            core, cot_a, cot_b, half, kept, got, gated[1], gated[2], part // 2
        )
        return [gated[0], *grads]

    hid_own = hidden_grads(0, gated_own)
    hid_other = hidden_grads(1, gated_other)

    def weight_grads(n_own, n_other, cot, own, other):
        return [
            wgrad_call(n_own, n_other, 0, own[1:], other[1:], part // 2),
            wgrad_call(cot, cot, 1, own[:1], other[:1], part // 2),
        ]

    big_b = weight_grads(n2_b, n2_other_b, cot_b, hid_own, hid_other)
    big_a = weight_grads(n2_a, n2_other_a, cot_a, hid_own, hid_other)
    own_grads = (*big_a, *big_b)
    big = lax.psum(own_grads, "dp")

    def sum_cores(own_pair, other_pair):
        from_b, from_a = swap_rows(other_pair[0]), swap_rows(other_pair[1])
        a = own_pair[0].astype(F32) + from_a.astype(F32)
        b = own_pair[1].astype(F32) + from_b.astype(F32)
        return jnp.concatenate([a, b], axis=1).astype(BF16)

    def token_blocks(value):
        return [value[j * own : (j + 1) * own] for j in range(cols)]

    back_own = [after(v, *own_grads) for v in hid_own[1:]]
    terms = back_call(core, back_own, hid_other[1:], kept[:2], got, 0)
    grad_normed_two = scatter_col(token_blocks(sum_cores(terms[:2], terms[2:])))


    def norm_backward(grad, value, gain):
        inverse = lax.rsqrt(jnp.mean(value * value, axis=1, keepdims=True) + EPS)
        unit = value * inverse
        scaled = grad * gain
        mean_term = jnp.mean(scaled * unit, axis=1, keepdims=True)
        return inverse * (scaled - unit * mean_term), jnp.sum(grad * unit, axis=0, keepdims=True)

    grad_norm_two, grad_gain_two = norm_backward(grad_normed_two, resid, gain_two_f)
    cot_full = jnp.concatenate([cot_a[:own], cot_b[:own]], axis=1).astype(F32)
    grad_resid = cot_full + grad_norm_two
    resid_blocks = gather_col(grad_resid.astype(BF16))
    resid_low = jnp.concatenate(resid_blocks, axis=0)

    query_low, grad_b_query, gkv_own, gkv_sent = attend_back_call(
        prefix, resid_low, wo_a[0], wo_b[0], query, kv_own, kv_other,
        query_pos, key_pos, cosine, sine_back, tokens,
    )
    qkv_low, grad_b_kv, back_one = qkv_back_call(
        gkv_own, swap_rows(gkv_sent), query_low, cosine, sine_back, w_qkv_a, w_qkv_b
    )
    grad_normed_one = scatter_col(token_blocks(back_one))

    def exchange_out(value):
        mine, other = halves(value)
        other = swap_rows(other)
        return jnp.where(
            r == 0,
            jnp.concatenate([mine, other], axis=0),
            jnp.concatenate([other, mine], axis=0),
        )

    grad_norm_one, grad_gain_one = norm_backward(
        grad_normed_one, x_full[:own].astype(F32), gain_one_f
    )
    grad_input = exchange_out(grad_resid + grad_norm_one)

    in_a, in_b, out_a, out_b = rest_call(normed_one, qkv_low, attended, resid_low)
    rest = in_a.astype(F32) + swap_rows(in_b).astype(F32)
    grad_wout = out_a.astype(F32) + swap_rows(out_b).astype(F32)
    grad_wout = jnp.concatenate(halves(grad_wout), axis=0)
    rest = jnp.concatenate([grad_wout, rest], axis=1).astype(BF16)
    rest = scatter_dp(rest, "x", x_at, side)
    mixed_other = after(hid_other[0], grad_resid)
    terms = back_call(core, hid_own[:1], [mixed_other], kept[2:], got, 2)
    down = token_blocks(sum_cores(terms[:2], terms[2:]))
    down = scatter_col([after(v, grad_normed_one, rest) for v in down])
    output = exchange_out((resid + down).astype(BF16))

    rest = scatter_dp(rest, "z", z_at, side)
    piece_rows = rest.shape[0]

    heads = kvw // HD
    mine, sent = pack_call(grad_gain_one, grad_gain_two, grad_b_kv, grad_b_query)
    message, small = message_call(mine, swap_rows(sent), rest)
    chip = c.astype(jnp.int32).reshape(1)
    first, second = head_sum_call(chip, gather_col(message), small, rest, heads, width // HD)
    places = jnp.stack([x_at, z_at]).astype(jnp.int32)
    first, second = gather_dp(first, "z", side), gather_dp(second, "x", side)
    first, second = order_call(places, first, second)
    big_got = [swap_rows(after(v, first, output)) for v in big[2:]]
    grad_w_gate = join_call(core, big[0], big_got[0], 0, 256)
    grad_w_up = join_call(core, big[0], big_got[0], 1, 256)
    grad_w_down = join_call(core, big[1], big_got[1], 0, 256)
    first, second = after(first, big[0]), after(second, big[0])
    first, second = gather_dp(first, "x", side), gather_dp(second, "z", side)
    places = after(places, grad_w_gate, grad_w_up, grad_w_down)
    grad_wout, grad_wq, grad_wkv, one, two, bias_kv, bias_query = finish_call(
        places, first, second, qw, feat, heads
    )

    return (
        output,
        grad_input,
        one.reshape(-1),
        grad_wq,
        bias_query.reshape(-1),
        grad_wkv,
        bias_kv.reshape(-1),
        grad_wout,
        two.reshape(-1),
        grad_w_gate.T,
        grad_w_up.T,
        grad_w_down,
    )


def solution(mesh):
    return jax.shard_map(
        body,
        mesh=mesh,
        in_specs=(
            P(("dp", "col"), "row"),
            P("dp"),
            P("row"),
            P("row", "col"),
            P("col"),
            P("row", None),
            P(),
            P("col", "row"),
            P("row"),
            P("row", "col"),
            P("row", "col"),
            P("col", "row"),
            P(("dp", "col"), "row"),
        ),
        out_specs=(
            P(("dp", "col"), "row"),
            P(("dp", "col"), "row"),
            P("row"),
            P("row", "col"),
            P("col"),
            P("row", None),
            P(),
            P("col", "row"),
            P("row"),
            P("row", "col"),
            P("row", "col"),
            P("col", "row"),
        ),
        check_vma=False,
    )
```

```python
import functools

import jax
import jax.numpy as jnp
from jax import lax
from jax.experimental import pallas as pl
from jax.experimental.pallas import tpu as pltpu
from jax.sharding import PartitionSpec as P

HD = 128
SEQ_LEN = 1024
EPS = 1e-06
THETA = 1000000.0
NEG = -1e30
BF16 = jnp.bfloat16
F32 = jnp.float32
MIB = 1 << 20
SMALL_ROWS = 32
LITTLE = 1000
GRANT = 40


def dot_nn(left, right):
    return lax.dot_general(left, right, (((1,), (0,)), ((), ())), preferred_element_type=F32)


def dot_nt(left, right):
    return lax.dot_general(left, right, (((1,), (1,)), ((), ())), preferred_element_type=F32)


def dot_tn(left, right):
    return lax.dot_general(left, right, (((0,), (0,)), ((), ())), preferred_element_type=F32)


def params(mib):
    return pltpu.CompilerParams(vmem_limit_bytes=mib * MIB)


def cost(flops, nbytes):
    return pl.CostEstimate(flops=int(flops), bytes_accessed=int(nbytes), transcendentals=0)


def rope(value, cosine, sine):
    return value * cosine + pltpu.roll(value, HD // 2, 1) * sine


def qkv_kernel(cols, own, *refs):
    r_ref, refs = refs[0], refs[1:]
    xa, refs = refs[:cols], refs[cols:]
    xb, refs = refs[:cols], refs[cols:]
    gain, wa, wb, bias, cosine, sine, x_out, n_out, q_out, kv_out = refs
    feat = xa[0].shape[1]
    for j in range(cols):
        rows = pl.ds(j * own, own)
        a = xa[j][...].astype(F32)
        b = xb[j][...].astype(F32)
        total = jnp.sum(a * a, axis=1, keepdims=True) + jnp.sum(b * b, axis=1, keepdims=True)
        inverse = lax.rsqrt(total / (2 * feat) + EPS)
        x_out[rows, :feat] = xa[j][...]
        x_out[rows, feat:] = xb[j][...]
        n_out[rows, :feat] = (a * inverse * gain[:, :feat]).astype(BF16)
        n_out[rows, feat:] = (b * inverse * gain[:, feat:]).astype(BF16)
    qkv = dot_nn(n_out[:, :feat], wa[...]) + dot_nn(n_out[:, feat:], wb[...]) + bias[...]
    qw = q_out.shape[1]
    for h in range(qw // HD):
        at = slice(h * HD, (h + 1) * HD)
        q_out[:, at] = rope(qkv[:, at], cosine[...], sine[...]).astype(BF16)
    kv_out[:, :HD] = rope(qkv[:, qw : qw + HD], cosine[...], sine[...]).astype(BF16)
    kv_out[:, HD:] = qkv[:, qw + HD :].astype(BF16)


def qkv_call(r, xa, xb, gain, wa, wb, bias, cosine, sine, qw, own):
    cols = len(xa)
    feat = xa[0].shape[1]
    tokens = own * cols
    whole = lambda v: pl.BlockSpec(v.shape, lambda i, r: (0,) * v.ndim)
    rest = [gain, wa, wb, bias, cosine, sine]
    outs = [
        jax.ShapeDtypeStruct((tokens, 2 * feat), BF16),
        jax.ShapeDtypeStruct((tokens, 2 * feat), BF16),
        jax.ShapeDtypeStruct((tokens, qw), BF16),
        jax.ShapeDtypeStruct((tokens, 2 * HD), BF16),
    ]
    return pl.pallas_call(
        functools.partial(qkv_kernel, cols, own),
        grid_spec=pltpu.PrefetchScalarGridSpec(
            num_scalar_prefetch=1,
            grid=(1,),
            in_specs=[pl.BlockSpec((own, feat), lambda i, r: (r[0], 0))] * (2 * cols)
            + [whole(v) for v in rest],
            out_specs=[whole(o) for o in outs],
        ),
        out_shape=outs,
        compiler_params=params(40),
        cost_estimate=cost(LITTLE, LITTLE),
        name="qkv",
    )(r, *xa, *xb, *rest)


def softmax(q, k, visible, scaling):
    scores = jnp.where(visible, dot_nt(q, k) * scaling, NEG)
    e = jnp.exp(scores - jnp.max(scores, axis=1, keepdims=True))
    return e * (1.0 / jnp.sum(e, axis=1, keepdims=True))


def visibility(qpos, kpos, prefix_ref):
    return (kpos <= qpos) | (kpos < prefix_ref[0])


def attend_kernel(scaling, prefix, q, kv_a, kv_b, qpos, kpos, out):
    visible = visibility(qpos[...], kpos[...], prefix)
    keys = jnp.concatenate([kv_a[:, :HD], kv_b[:, :HD]], axis=0)
    values = jnp.concatenate([kv_a[:, HD:], kv_b[:, HD:]], axis=0)
    for h in range(q.shape[1] // HD):
        at = slice(h * HD, (h + 1) * HD)
        weights = softmax(q[:, at], keys, visible, scaling)
        out[:, at] = dot_nn(weights.astype(BF16), values).astype(BF16)


def attend_call(prefix, q, kv_a, kv_b, qpos, kpos, block):
    tokens, qw = q.shape
    whole = lambda v: pl.BlockSpec(v.shape, lambda i, p: (0,) * v.ndim)
    part = lambda v: pl.BlockSpec((block, v.shape[1]), lambda i, p: (i, 0))
    return pl.pallas_call(
        functools.partial(attend_kernel, HD**-0.5),
        grid_spec=pltpu.PrefetchScalarGridSpec(
            num_scalar_prefetch=1,
            grid=(tokens // block,),
            in_specs=[part(q), whole(kv_a), whole(kv_b), part(qpos), whole(kpos)],
            out_specs=part(q),
        ),
        out_shape=jax.ShapeDtypeStruct(q.shape, BF16),
        compiler_params=params(32),
        cost_estimate=cost(LITTLE, LITTLE),
        name="attend",
    )(prefix, q, kv_a, kv_b, qpos, kpos)


def out_kernel(cols, own, *refs):
    att, refs = refs[:cols], refs[cols:]
    wa, refs = refs[:cols], refs[cols:]
    wb, refs = refs[:cols], refs[cols:]
    xa, xb, gain, resid_out, na, nb, acc_a, acc_b = refs
    step, steps = pl.program_id(0), pl.num_programs(0)
    chunk = xa.shape[1]
    feat = chunk * steps

    rolled = []
    for j in range(cols):
        tiles = [att[j][((i - j) % cols) * own : ((i - j) % cols + 1) * own, :] for i in range(cols)]
        rolled.append(jnp.concatenate(tiles, axis=0))
    at = pl.ds(pl.multiple_of(step * chunk, 128), chunk)
    for x, w, acc in ((xa, wa, acc_a), (xb, wb, acc_b)):
        total = x[...].astype(F32)
        for j in range(cols):
            total = total + dot_nn(rolled[j], w[j][...])
        acc[:, at] = total

    @pl.when(step == steps - 1)
    def _():
        a, b = acc_a[...], acc_b[...]
        total = jnp.sum(a * a, axis=1, keepdims=True) + jnp.sum(b * b, axis=1, keepdims=True)
        inverse = lax.rsqrt(total / (2 * feat) + EPS)
        na[...] = (a * inverse * gain[:, :feat]).astype(BF16)
        nb[...] = (b * inverse * gain[:, feat:]).astype(BF16)
        resid_out[:, :feat] = acc_a[:own, :]
        resid_out[:, feat:] = acc_b[:own, :]


def out_call(att, wa, wb, x, gain, own):
    cols = len(att)
    tokens, qw = att[0].shape
    feat = wa[0].shape[1]
    steps = 3
    chunk = feat // steps
    whole = lambda v: pl.BlockSpec(v.shape, lambda i: (0,) * v.ndim)
    outs = [
        jax.ShapeDtypeStruct((own, 2 * feat), F32),
        jax.ShapeDtypeStruct((tokens, feat), BF16),
        jax.ShapeDtypeStruct((tokens, feat), BF16),
    ]
    return pl.pallas_call(
        functools.partial(out_kernel, cols, own),
        grid=(steps,),
        in_specs=[whole(a) for a in att]
        + [pl.BlockSpec((qw, chunk), lambda i: (0, i))] * (2 * cols)
        + [
            pl.BlockSpec((tokens, chunk), lambda i: (0, i)),
            pl.BlockSpec((tokens, chunk), lambda i: (0, steps + i)),
            whole(gain),
        ],
        out_specs=[whole(o) for o in outs],
        out_shape=outs,
        scratch_shapes=[pltpu.VMEM((tokens, feat), F32)] * 2,
        compiler_params=params(40),
        cost_estimate=cost(LITTLE, LITTLE),
        name="out_norm",
    )(*att, *wa, *wb, x, x, gain)


def assemble_kernel(cols, meta, ca, cb, out_a, out_b):
    rows = ca.shape[0] // cols
    own = rows // 2
    tokens = cols * own
    r, c = meta[0], meta[1]
    for j in range(cols):
        at = lax.rem(c + j, cols) * rows
        for src, out in ((ca, out_a), (cb, out_b)):
            out[j * own : (j + 1) * own, :] = src[pl.ds(at + r * own, own), :]
            out[tokens + j * own : tokens + (j + 1) * own, :] = src[
                pl.ds(at + (1 - r) * own, own), :
            ]


def assemble_call(meta, ca, cb, cols):
    out = jax.ShapeDtypeStruct(ca.shape, BF16)
    return pl.pallas_call(
        functools.partial(assemble_kernel, cols),
        in_specs=[pl.BlockSpec(memory_space=pltpu.SMEM)]
        + [pl.BlockSpec(memory_space=pltpu.VMEM)] * 2,
        out_specs=[pl.BlockSpec(memory_space=pltpu.VMEM)] * 2,
        out_shape=[out, out],
        compiler_params=params(24),
        cost_estimate=cost(LITTLE, LITTLE),
        name="assemble",
    )(meta, ca, cb)


def gated_kernel(*refs):
    acts, (ga, gb, ua, ub), outs = refs[:4], refs[4:8], refs[8:]
    for half in range(2):
        na, nb = acts[2 * half : 2 * half + 2]
        mixed, to_gate, to_up = outs[3 * half : 3 * half + 3]
        gate = dot_nt(ga[...], na[...]) + dot_nt(gb[...], nb[...])
        up = dot_nt(ua[...], na[...]) + dot_nt(ub[...], nb[...])
        s = 0.5 * jnp.tanh(0.5 * gate) + 0.5
        silu = gate * s
        mixed[...] = (silu * up).astype(BF16)
        to_gate[...] = (up * (s + silu * (1.0 - s))).astype(BF16)
        to_up[...] = silu.astype(BF16)


def hidden_grad_kernel(ca, cb, da, db, *refs):
    factors, outs = refs[:4], refs[4:]
    tokens = factors[0].shape[1]
    for half in range(2):
        rows = slice(half * tokens, (half + 1) * tokens)
        to_gate, to_up = factors[2 * half : 2 * half + 2]
        grad_gate, grad_up = outs[2 * half : 2 * half + 2]
        grad_mixed = dot_nt(da[...], ca[rows, :]) + dot_nt(db[...], cb[rows, :])
        grad_gate[...] = (grad_mixed * to_gate[...].astype(F32)).astype(BF16)
        grad_up[...] = (grad_mixed * to_up[...].astype(F32)).astype(BF16)


def gated_call(r, acts, kept, got, chunk):
    tokens, feat = acts[0].shape
    part = got.shape[1]
    steps = part // chunk
    act = pl.BlockSpec((tokens, feat), lambda i, r: (0, 0))
    mine = pl.BlockSpec((chunk, feat), lambda i, r: (r[0] * steps + i, 0))
    other = lambda k: pl.BlockSpec((None, chunk, feat), lambda i, r: (k, i, 0))
    return pl.pallas_call(
        lambda r, *refs: gated_kernel(*refs),
        grid_spec=pltpu.PrefetchScalarGridSpec(
            num_scalar_prefetch=1,
            grid=(steps,),
            in_specs=[act] * 4 + [mine, other(0), mine, other(1)],
            out_specs=[pl.BlockSpec((chunk, tokens), lambda i, r: (i, 0))] * 6,
        ),
        out_shape=[jax.ShapeDtypeStruct((part, tokens), BF16)] * 6,
        compiler_params=params(GRANT),
        cost_estimate=cost(LITTLE, LITTLE),
        name="gated",
    )(r, *acts, kept[0], got, kept[1], got)


def hidden_grad_call(r, ca, cb, kept, got, factors, chunk):
    part, tokens = factors[0].shape
    feat = ca.shape[1]
    steps = part // chunk
    cot = pl.BlockSpec(ca.shape, lambda i, r: (0, 0))
    hid = pl.BlockSpec((chunk, tokens), lambda i, r: (i, 0))
    return pl.pallas_call(
        lambda r, *refs: hidden_grad_kernel(*refs),
        grid_spec=pltpu.PrefetchScalarGridSpec(
            num_scalar_prefetch=1,
            grid=(steps,),
            in_specs=[
                cot,
                cot,
                pl.BlockSpec((chunk, feat), lambda i, r: (r[0] * steps + i, 0)),
                pl.BlockSpec((None, chunk, feat), lambda i, r: (2, i, 0)),
            ]
            + [hid] * 4,
            out_specs=[hid] * 4,
        ),
        out_shape=[jax.ShapeDtypeStruct((part, tokens), BF16)] * 4,
        compiler_params=params(GRANT),
        cost_estimate=cost(LITTLE, LITTLE),
        name="hidden_grads",
    )(r, ca, cb, kept[2], got, *factors)


def wgrad_kernel(pairs, act_own, act_other, *refs):
    own, other, out = refs[:pairs], refs[pairs : 2 * pairs], refs[2 * pairs]
    for k in range(pairs):
        total = dot_nn(own[k][...], act_own[...]) + dot_nn(other[k][...], act_other[...])
        out[k] = total.astype(BF16)


def wgrad_call(act_own, act_other, other_block, hidden_own, hidden_other, chunk):
    pairs = len(hidden_own)
    part, tokens = hidden_own[0].shape
    feat = act_own.shape[1]
    hid = pl.BlockSpec((chunk, tokens), lambda i: (i, 0))
    return pl.pallas_call(
        functools.partial(wgrad_kernel, pairs),
        grid=(part // chunk,),
        in_specs=[
            pl.BlockSpec((tokens, feat), lambda i: (0, 0)),
            pl.BlockSpec((tokens, feat), lambda i: (other_block, 0)),
        ]
        + [hid] * (2 * pairs),
        out_specs=pl.BlockSpec((pairs, chunk, feat), lambda i: (0, i, 0)),
        out_shape=jax.ShapeDtypeStruct((pairs, part, feat), BF16),
        compiler_params=params(GRANT),
        cost_estimate=cost(LITTLE, LITTLE),
        name="weight_grads",
    )(act_own, act_other, *hidden_own, *hidden_other)


def back_kernel(pairs, *refs):
    hidden, refs = (refs[:pairs], refs[pairs : 2 * pairs]), refs[2 * pairs :]
    wa, refs = refs[:pairs], refs[pairs:]
    wb, outs = refs[:pairs], refs[pairs:]
    for half in (1, 0):
        for w, out in ((wa, outs[2 * half]), (wb, outs[2 * half + 1])):
            total = dot_tn(hidden[half][0][...], w[0][...])
            for i in range(1, pairs):
                total = total + dot_tn(hidden[half][i][...], w[i][...])
            out[...] = total.astype(out.dtype)


def back_call(r, own, other, kept, got, first):
    pairs = len(own)
    part, tokens = own[0].shape
    feat = got.shape[2]
    out = jax.ShapeDtypeStruct((tokens, feat), BF16)
    of_other = lambda k: pl.BlockSpec((None, part, feat), lambda i, r: (first + k, 0, 0))
    return pl.pallas_call(
        lambda r, *refs: back_kernel(pairs, *refs),
        grid_spec=pltpu.PrefetchScalarGridSpec(
            num_scalar_prefetch=1,
            grid=(1,),
            in_specs=[pl.BlockSpec((part, tokens), lambda i, r: (0, 0))] * (2 * pairs)
            + [pl.BlockSpec((part, feat), lambda i, r: (r[0], 0))] * pairs
            + [of_other(k) for k in range(pairs)],
            out_specs=[pl.BlockSpec((tokens, feat), lambda i, r: (0, 0))] * 4,
        ),
        out_shape=[out] * 4,
        compiler_params=params(GRANT),
        cost_estimate=cost(LITTLE, LITTLE),
        name="back_in",
    )(r, *own, *other, *kept, *([got] * pairs))


def attend_back_kernel(
    scaling, own, prefix, *refs
):
    (gr, wa, wb, q, kv_a, kv_b, qpos, kpos, cosine, sine,
     low_out, sum_out, gkv_own, gkv_send, gk, gv, ga_s) = refs
    step, steps = pl.program_id(0), pl.num_programs(0)
    feat = wa.shape[1]
    visible = visibility(qpos[...], kpos[...], prefix)
    keys = jnp.concatenate([kv_a[:, :HD], kv_b[:, :HD]], axis=0)
    values = jnp.concatenate([kv_a[:, HD:], kv_b[:, HD:]], axis=0)
    ga_s[...] = (dot_nt(gr[:, :feat], wa[...]) + dot_nt(gr[:, feat:], wb[...])).astype(BF16)

    @pl.when(step == 0)
    def _():
        gk[...] = jnp.zeros_like(gk)
        gv[...] = jnp.zeros_like(gv)
        sum_out[...] = jnp.zeros_like(sum_out)

    for h in range(q.shape[1] // HD):
        at = slice(h * HD, (h + 1) * HD)
        weights = softmax(q[:, at], keys, visible, scaling)
        grad_att = ga_s[:, at]
        gw = dot_nt(grad_att, values)
        inner = jnp.sum(weights * gw, axis=1, keepdims=True)
        gs = (weights * (gw - inner)).astype(BF16)
        gk[...] += dot_tn(gs, q[:, at])
        gv[...] += dot_tn(weights.astype(BF16), grad_att)
        grad_q = dot_nn(gs, keys) * scaling
        grad_q = rope(grad_q, cosine[...], sine[...])
        low_out[:, at] = grad_q.astype(BF16)
        sum_out[:, at] += jnp.sum(grad_q, axis=0, keepdims=True)

    @pl.when(step == steps - 1)
    def _():
        half = gk.shape[0] // 2
        gkv_own[:, :HD] = gk[:half, :] * scaling
        gkv_own[:, HD:] = gv[:half, :]
        gkv_send[:, :HD] = (gk[half:, :] * scaling).astype(BF16)
        gkv_send[:, HD:] = gv[half:, :].astype(BF16)


def attend_back_call(prefix, gr, wa, wb, q, kv_a, kv_b, qpos, kpos, cosine, sine, block):
    tokens, qw = q.shape
    whole = lambda v: pl.BlockSpec(v.shape, lambda i, p: (0,) * v.ndim)
    part = lambda v: pl.BlockSpec((block, v.shape[1]), lambda i, p: (i, 0))
    outs = [
        jax.ShapeDtypeStruct((tokens, qw), BF16),
        jax.ShapeDtypeStruct((1, qw), F32),
        jax.ShapeDtypeStruct((tokens, 2 * HD), F32),
        jax.ShapeDtypeStruct((tokens, 2 * HD), BF16),
    ]
    keys = 2 * tokens
    return pl.pallas_call(
        functools.partial(attend_back_kernel, HD**-0.5, block),
        grid_spec=pltpu.PrefetchScalarGridSpec(
            num_scalar_prefetch=1,
            grid=(tokens // block,),
            in_specs=[
                part(gr), whole(wa), whole(wb), part(q), whole(kv_a), whole(kv_b),
                part(qpos), whole(kpos), part(cosine), part(sine),
            ],
            out_specs=[part(outs[0]), whole(outs[1]), whole(outs[2]), whole(outs[3])],
            scratch_shapes=[
                pltpu.VMEM((keys, HD), F32),
                pltpu.VMEM((keys, HD), F32),
                pltpu.VMEM((block, qw), BF16),
            ],
        ),
        out_shape=outs,
        compiler_params=params(40),
        cost_estimate=cost(LITTLE, LITTLE),
        name="attend_back",
    )(prefix, gr, wa, wb, q, kv_a, kv_b, qpos, kpos, cosine, sine)


def qkv_back_kernel(own, got, query_low, cosine, sine, wa, wb, low, sums, back):
    qw = query_low.shape[1]
    total = own[...] + got[...].astype(F32)
    key = rope(total[:, :HD], cosine[...], sine[...])
    value = total[:, HD:]
    sums[:, :HD] = jnp.sum(key, axis=0, keepdims=True)
    sums[:, HD:] = jnp.sum(value, axis=0, keepdims=True)
    low[:, :qw] = query_low[...]
    low[:, qw : qw + HD] = key.astype(BF16)
    low[:, qw + HD :] = value.astype(BF16)
    feat = wa.shape[0]
    back[:, :feat] = dot_nt(low[...], wa[...]).astype(BF16)
    back[:, feat:] = dot_nt(low[...], wb[...]).astype(BF16)


def qkv_back_call(own, got, query_low, cosine, sine, wa, wb):
    tokens = own.shape[0]
    feat, columns = wa.shape
    return pl.pallas_call(
        qkv_back_kernel,
        out_shape=[
            jax.ShapeDtypeStruct((tokens, columns), BF16),
            jax.ShapeDtypeStruct((1, 2 * HD), F32),
            jax.ShapeDtypeStruct((tokens, 2 * feat), BF16),
        ],
        compiler_params=params(32),
        cost_estimate=cost(LITTLE, LITTLE),
        name="qkv_back",
    )(own, got, query_low, cosine, sine, wa, wb)


def rest_kernel(n1, low, attended, grad, in_a, in_b, out_a, out_b):
    feat = n1.shape[1] // 2
    in_b[...] = dot_tn(n1[:, feat:], low[...]).astype(BF16)
    out_b[...] = dot_tn(attended[...], grad[:, feat:]).astype(BF16)
    in_a[...] = dot_tn(n1[:, :feat], low[...]).astype(BF16)
    out_a[...] = dot_tn(attended[...], grad[:, :feat]).astype(BF16)


def rest_call(n1, low, attended, grad):
    feat = n1.shape[1] // 2
    into = jax.ShapeDtypeStruct((feat, low.shape[1]), BF16)
    out = jax.ShapeDtypeStruct((attended.shape[1], feat), BF16)
    return pl.pallas_call(
        rest_kernel,
        out_shape=[into, into, out, out],
        compiler_params=params(32),
        cost_estimate=cost(LITTLE, LITTLE),
        name="rest",
    )(n1, low, attended, grad)


def join_kernel(r_ref, kept, got, out):
    part = kept.shape[0]

    @pl.when(r_ref[0] == 0)
    def _():
        out[:part, :] = kept[...].astype(F32)
        out[part:, :] = got[...].astype(F32)

    @pl.when(r_ref[0] != 0)
    def _():
        out[:part, :] = got[...].astype(F32)
        out[part:, :] = kept[...].astype(F32)


def join_call(r, kept, got, which, chunk):
    part, feat = kept.shape[1:]
    half = pl.BlockSpec((None, part, chunk), lambda i, r: (which, 0, i))
    return pl.pallas_call(
        join_kernel,
        grid_spec=pltpu.PrefetchScalarGridSpec(
            num_scalar_prefetch=1,
            grid=(feat // chunk,),
            in_specs=[half, half],
            out_specs=pl.BlockSpec((2 * part, chunk), lambda i, r: (0, i)),
        ),
        out_shape=jax.ShapeDtypeStruct((2 * part, feat), F32),
        compiler_params=params(32),
        cost_estimate=cost(LITTLE, LITTLE),
        name="join",
    )(r, kept, got)


def pack_kernel(one, two, bias_kv, bias_query, mine, sent):
    feat = one.shape[1] // 2
    for out, first in ((mine, 0), (sent, feat)):
        out[...] = jnp.zeros_like(out)
        at = 0
        for vector, start, size in (
            (one, first, feat),
            (two, first, feat),
            (bias_kv, 0, bias_kv.shape[1]),
            (bias_query, 0, bias_query.shape[1]),
        ):
            for k in range(size // HD):
                out[at : at + 1, :] = vector[:, start + k * HD : start + (k + 1) * HD]
                at += 1


def pack_call(one, two, bias_kv, bias_query):
    out = jax.ShapeDtypeStruct((SMALL_ROWS, HD), F32)
    return pl.pallas_call(
        pack_kernel,
        out_shape=[out, out],
        cost_estimate=cost(LITTLE, LITTLE),
        name="pack",
    )(one, two, bias_kv, bias_query)


def message_kernel(mine, got, rest, out, small):
    rows = rest.shape[0]
    total = mine[...] + got[...]
    small[...] = total
    out[:rows, :] = rest[:, rest.shape[1] - 2 * HD :]
    out[rows:, :HD] = total.astype(BF16)
    out[rows:, HD:] = jnp.zeros((SMALL_ROWS, HD), BF16)


def message_call(mine, got, rest):
    rows = rest.shape[0]
    return pl.pallas_call(
        message_kernel,
        out_shape=[
            jax.ShapeDtypeStruct((rows + SMALL_ROWS, 2 * HD), BF16),
            jax.ShapeDtypeStruct((SMALL_ROWS, HD), F32),
        ],
        cost_estimate=cost(LITTLE, LITTLE),
        name="message",
    )(mine, got, rest)


def head_sum_kernel(cols, heads, gain_rows, chip, *refs):
    messages, (small, rest, out_a, out_b, total) = refs[:cols], refs[cols:]
    rows, columns = rest.shape
    half = out_a.shape[1]
    share = cols // heads
    total[...] = jnp.zeros_like(total)
    total[:gain_rows, :] = sum(m[rows : rows + gain_rows, :HD].astype(F32) for m in messages)
    for head in range(heads):
        both = jnp.zeros((rows, 2 * HD), F32)
        bias = jnp.zeros((SMALL_ROWS, HD), F32)
        for j in range(cols):
            same = jnp.where(lax.rem(chip[0] + j, cols) // share == head, 1.0, 0.0)
            both = both + same * messages[j][:rows, :].astype(F32)
            bias = bias + same * messages[j][rows:, :HD].astype(F32)
        own_columns = columns - 2 * HD - half
        at = own_columns + head * HD
        out_b[:, at : at + HD] = both[:, :HD].astype(BF16)
        at += heads * HD
        out_b[:, at : at + HD] = both[:, HD:].astype(BF16)
        for k in range(2):
            row = gain_rows + k * heads + head
            total[row : row + 1, :] = bias[gain_rows + k : gain_rows + k + 1, :]
    queries = small[gain_rows + 2 :, :]
    first = gain_rows + 2 * heads
    total[first:, :] = queries[: SMALL_ROWS - first, :]
    out_a[:rows, :] = rest[:, :half]
    out_b[:, : columns - 2 * HD - half] = rest[:, half : columns - 2 * HD]
    out_a[rows:, :HD] = total[...].astype(BF16)
    out_a[rows:, HD:] = jnp.zeros((SMALL_ROWS, half - HD), BF16)


def head_sum_call(chip, messages, small, rest, heads, gain_rows):
    rows, columns = rest.shape
    half = (columns + 2 * HD * (heads - 1)) // 2
    vmem = pl.BlockSpec(memory_space=pltpu.VMEM)
    return pl.pallas_call(
        functools.partial(head_sum_kernel, len(messages), heads, gain_rows),
        in_specs=[pl.BlockSpec(memory_space=pltpu.SMEM)] + [vmem] * (len(messages) + 2),
        out_specs=[vmem, vmem],
        out_shape=[
            jax.ShapeDtypeStruct((rows + SMALL_ROWS, half), BF16),
            jax.ShapeDtypeStruct((rows, half), BF16),
        ],
        scratch_shapes=[pltpu.VMEM((SMALL_ROWS, HD), F32)],
        cost_estimate=cost(LITTLE, LITTLE),
        name="head_sums",
    )(chip, *messages, small, rest)


def order_kernel(side, places, *refs):
    first, second, (out_a, out_b) = refs[:side], refs[side : 2 * side], refs[2 * side :]
    rows = second[0].shape[0]
    for i in range(side):
        at = lax.rem(places[1] + i, side) * rows
        out_a[pl.ds(pl.multiple_of(at, 16), rows), :] = first[i][:rows, :]
        at = lax.rem(places[0] + i, side) * rows
        out_b[pl.ds(pl.multiple_of(at, 16), rows), :] = second[i][...]
    total = sum(v[rows:, :].astype(F32) for v in first)
    out_a[side * rows :, :] = total.astype(BF16)


def order_call(places, first, second):
    side = len(first)
    rows, half = second[0].shape
    vmem = pl.BlockSpec(memory_space=pltpu.VMEM)
    return pl.pallas_call(
        functools.partial(order_kernel, side),
        in_specs=[pl.BlockSpec(memory_space=pltpu.SMEM)] + [vmem] * (2 * side),
        out_specs=[vmem, vmem],
        out_shape=[
            jax.ShapeDtypeStruct((side * rows + SMALL_ROWS, half), BF16),
            jax.ShapeDtypeStruct((side * rows, half), BF16),
        ],
        cost_estimate=cost(LITTLE, LITTLE),
        name="order",
    )(places, *first, *second)


def finish_kernel(side, heads, places, *refs):
    first, second, outs = refs[:side], refs[side : 2 * side], refs[2 * side :]
    w_out, w_query, w_keyval, one, two, bias_kv, bias_query, total = outs
    qw = w_query.shape[1]
    block, half = second[0].shape
    rows = block // side
    count = qw // block
    for i in range(side):
        at = lax.rem(places[0] + i, side)
        place = pl.ds(pl.multiple_of(at * block, 16), block)
        w_query[place, : half - qw] = first[i][:block, qw:].astype(F32)
        values = first[i][:block, :qw].astype(F32)

        @pl.when(at < count)
        def _():
            w_out[pl.ds(pl.multiple_of(at * block, 16), block), :qw] = values

        @pl.when(at >= count)
        def _():
            w_out[pl.ds(pl.multiple_of((at - count) * block, 16), block), qw:] = values

        at = lax.rem(places[1] + i, side)
        for k in range(side):
            place = pl.ds(pl.multiple_of(k * block + at * rows, 16), rows)
            piece = second[i][k * rows : (k + 1) * rows, :].astype(F32)
            w_query[place, half - qw :] = piece[:, : 2 * qw - half]
            w_keyval[place, :] = piece[:, 2 * qw - half :]
    total[...] = sum(v[block:, :HD].astype(F32) for v in first)
    at = 0
    for out in (one, two, bias_kv, bias_query):
        out[...] = total[at : at + out.shape[0], :]
        at += out.shape[0]


def finish_call(places, first, second, qw, feat, heads):
    side = len(first)
    vmem = pl.BlockSpec(memory_space=pltpu.VMEM)
    shapes = [(qw, feat), (feat, qw), (feat, 2 * heads * HD)]
    shapes += [(feat // HD, HD), (feat // HD, HD), (2 * heads, HD), (qw // HD, HD)]
    return pl.pallas_call(
        functools.partial(finish_kernel, side, heads),
        in_specs=[pl.BlockSpec(memory_space=pltpu.SMEM)] + [vmem] * (2 * side),
        out_specs=[vmem] * len(shapes),
        out_shape=[jax.ShapeDtypeStruct(s, F32) for s in shapes],
        scratch_shapes=[pltpu.VMEM((SMALL_ROWS, HD), F32)],
        compiler_params=params(32),
        cost_estimate=cost(LITTLE, LITTLE),
        name="finish",
    )(places, *first, *second)
def after(value, *others):
    return lax.optimization_barrier((value,) + others)[0]


def swap_rows(value):
    return lax.ppermute(value, "row", [(0, 1), (1, 0)])


def from_col(value, offset):
    count = lax.axis_size("col")
    return lax.ppermute(value, "col", [((i + offset) % count, i) for i in range(count)])


def gather_col(value):
    third, first = from_col(value, -1), from_col(value, 1)
    return [value, first, from_col(value, 2), third]


def gather_col_ring(value, behind=()):
    third, first = from_col(value, -1), from_col(value, 1)
    middle = value.shape[0] // 2
    upper = from_col(after(first, *behind)[:middle], 1)
    lower = from_col(after(third, *behind)[middle:], -1)
    return [value, first, jnp.concatenate([upper, lower], axis=0), third]


def scatter_col(blocks, behind=()):
    third, first, second = (
        from_col(blocks[3], 1),
        from_col(blocks[1], -1),
        from_col(blocks[2], -2),
    )
    total = blocks[0].astype(F32)
    for part in (first, second, third):
        total = total + after(part, *behind).astype(F32)
    return total


def halves(value):
    middle = value.shape[-1] // 2
    return value[..., :middle], value[..., middle:]


def roll_blocks(value, shift, axis):
    size = value.shape[axis]
    twice = jnp.concatenate([value, value], axis=axis)
    return lax.dynamic_slice_in_dim(twice, shift, size, axis)


def shift_dp(value, along, offset, side):
    pairs = []
    for z in range(side):
        for x in range(side):
            if along == "z":
                source = ((z + offset) % side) * side + x
            else:
                source = z * side + (x + offset) % side
            pairs.append((source, z * side + x))
    return lax.ppermute(value, "dp", pairs)


def scatter_dp(value, along, at, side):
    value = jnp.pad(value, ((0, -value.shape[0] % (8 * side)), (0, 0)))
    rows = value.shape[0] // side
    block = lambda j: lax.dynamic_slice_in_dim(value, ((at + j) % side) * rows, rows, 0)
    got = [shift_dp(block(j), along, -j, side) for j in (1, side - 1, 2)]
    total = block(0).astype(F32)
    for part in got:
        total = total + part.astype(F32)
    return total.astype(BF16)


def gather_dp_ring(value, along, side):
    third, first = shift_dp(value, along, -1, side), shift_dp(value, along, 1, side)
    middle = value.shape[0] // 2
    upper = shift_dp(first[:middle], along, 1, side)
    lower = shift_dp(third[middle:], along, -1, side)
    return [value, first, jnp.concatenate([upper, lower], axis=0), third]


def gather_dp(value, along, side):
    got = {j: shift_dp(value, along, j, side) for j in (1, side - 1, 2)}
    return [value] + [got[j] for j in range(1, side)]


def body(
    layer_input,
    prefix,
    gain_one,
    w_query,
    b_query,
    w_keyval,
    b_keyval,
    w_out,
    gain_two,
    w_gate,
    w_up,
    w_down,
    cotangent,
):
    cols = lax.axis_size("col")
    groups = lax.axis_size("dp")
    side = int(round(groups**0.5))
    r = lax.axis_index("row")
    c = lax.axis_index("col")
    dp = lax.axis_index("dp")
    z_at, x_at = dp // side, dp % side
    core = r.astype(jnp.int32).reshape(1)
    rows_in, feat = layer_input.shape
    own = rows_in // 2
    tokens = own * cols
    width = 2 * feat
    qw = w_query.shape[1]
    kvw = w_keyval.shape[1] // 2
    share = cols // (kvw // HD)
    kv_head = c // share
    ff = w_gate.shape[1]
    part = ff // 2

    x_a = gather_col(layer_input)

    key_start = kv_head * HD
    w_qkv_a = jnp.concatenate(
        [
            w_query,
            lax.dynamic_slice_in_dim(w_keyval, key_start, HD, 1),
            lax.dynamic_slice_in_dim(w_keyval, kvw + key_start, HD, 1),
        ],
        axis=1,
    )
    bias = jnp.concatenate(
        [
            b_query,
            lax.dynamic_slice_in_dim(b_keyval, key_start, HD, 0),
            lax.dynamic_slice_in_dim(b_keyval, kvw + key_start, HD, 0),
        ]
    ).astype(F32)[None]
    w_qkv_b = swap_rows(w_qkv_a)
    gains_a = jnp.stack([gain_one, gain_two])
    gains = jnp.concatenate([gains_a, swap_rows(gains_a)], axis=1).astype(F32)
    gain_one_f, gain_two_f = gains[:1], gains[1:]

    kept = [w_gate.T, w_up.T, w_down]
    sent = [
        lax.dynamic_slice_in_dim(w, (1 - r) * part, part, 0)
        for w in kept
    ]
    sent = jnp.stack(sent)

    block_first = rows_in * ((c + jnp.arange(cols, dtype=jnp.int32)) % cols)
    inside = jnp.arange(own, dtype=jnp.int32)
    pos_own = ((block_first[:, None] + own * r + inside[None]) % SEQ_LEN).reshape(-1)
    pos_other = ((block_first[:, None] + own * (1 - r) + inside[None]) % SEQ_LEN).reshape(-1)
    query_pos = pos_own[:, None]
    key_pos = jnp.concatenate([pos_own, pos_other])[None, :]
    frequency = THETA ** (-jnp.arange(0, HD // 2, dtype=F32) * 2.0 / HD)
    angle = pos_own.astype(F32)[:, None] * frequency[None, :]
    cosine, sine = jnp.cos(angle), jnp.sin(angle)
    cosine = jnp.concatenate([cosine, cosine], axis=1)
    sine_to = jnp.concatenate([-sine, sine], axis=1)
    sine_back = jnp.concatenate([sine, -sine], axis=1)

    x_b = [swap_rows(v) for v in x_a]
    wo_a = gather_col_ring(after(w_out, *x_b, w_qkv_b))
    x_full, normed_one, query, kv_own = qkv_call(
        core, x_a, x_b, gain_one_f, w_qkv_a, w_qkv_b, bias, cosine, sine_to, qw, own
    )
    kv_other = swap_rows(kv_own)
    query = after(query, wo_a[1], wo_a[3])
    attended = attend_call(prefix, query, kv_own, kv_other, query_pos, key_pos, tokens)
    got = swap_rows(after(sent, attended))
    att = gather_col_ring(attended, (got,))
    wo_b = [swap_rows(v) for v in wo_a]
    c_a = lax.all_gather(after(cotangent, *att[1:]), "col", axis=0, tiled=True)
    resid, n2_a, n2_b = out_call(att, wo_a, wo_b, x_full, gain_two_f, own)
    n2_other_b, n2_other_a = swap_rows(n2_a), swap_rows(n2_b)


    acts = (after(n2_a, n2_other_a, n2_other_b), n2_b, n2_other_a, n2_other_b)
    gated = gated_call(core, acts, kept, got, part // 2)
    c_b = swap_rows(after(c_a, n2_other_a, n2_other_b))
    place = after(jnp.stack([r, c]).astype(jnp.int32), gated[0])
    cot_a, cot_b = assemble_call(place, c_a, c_b, cols)
    factors = (*gated[1:3], *gated[4:6])
    grads = hidden_grad_call(core, cot_a, cot_b, kept, got, factors, part // 2)
    hid_own = [gated[0], *grads[:2]]
    hid_other = [gated[3], *grads[2:]]

    def weight_grads(n_own, n_other, cot, own, other):
        return [
            wgrad_call(n_own, n_other, 0, own[1:], other[1:], part // 2),
            wgrad_call(cot, cot, 1, own[:1], other[:1], part // 2),
        ]

    big_b = weight_grads(n2_b, n2_other_b, cot_b, hid_own, hid_other)
    big_a = weight_grads(n2_a, n2_other_a, cot_a, hid_own, hid_other)
    own_grads = (*big_a, *big_b)
    big = lax.psum(own_grads, "dp")

    def sum_cores(own_pair, other_pair):
        from_b, from_a = swap_rows(other_pair[0]), swap_rows(other_pair[1])
        a = own_pair[0].astype(F32) + from_a.astype(F32)
        b = own_pair[1].astype(F32) + from_b.astype(F32)
        return jnp.concatenate([a, b], axis=1).astype(BF16)

    def token_blocks(value):
        return [value[j * own : (j + 1) * own] for j in range(cols)]

    back_own = [after(v, *own_grads) for v in hid_own[1:]]
    terms = back_call(core, back_own, hid_other[1:], kept[:2], got, 0)
    grad_normed_two = scatter_col(token_blocks(sum_cores(terms[:2], terms[2:])))


    def norm_backward(grad, value, gain):
        inverse = lax.rsqrt(jnp.mean(value * value, axis=1, keepdims=True) + EPS)
        unit = value * inverse
        scaled = grad * gain
        mean_term = jnp.mean(scaled * unit, axis=1, keepdims=True)
        return inverse * (scaled - unit * mean_term), jnp.sum(grad * unit, axis=0, keepdims=True)

    grad_norm_two, grad_gain_two = norm_backward(grad_normed_two, resid, gain_two_f)
    cot_full = jnp.concatenate([cot_a[:own], cot_b[:own]], axis=1).astype(F32)
    grad_resid = cot_full + grad_norm_two
    resid_blocks = gather_col(grad_resid.astype(BF16))
    resid_low = jnp.concatenate(resid_blocks, axis=0)

    query_low, grad_b_query, gkv_own, gkv_sent = attend_back_call(
        prefix, resid_low, wo_a[0], wo_b[0], query, kv_own, kv_other,
        query_pos, key_pos, cosine, sine_back, tokens,
    )
    qkv_low, grad_b_kv, back_one = qkv_back_call(
        gkv_own, swap_rows(gkv_sent), query_low, cosine, sine_back, w_qkv_a, w_qkv_b
    )
    grad_normed_one = scatter_col(token_blocks(back_one))

    def exchange_out(value):
        mine, other = halves(value)
        other = swap_rows(other)
        return jnp.where(
            r == 0,
            jnp.concatenate([mine, other], axis=0),
            jnp.concatenate([other, mine], axis=0),
        )

    grad_norm_one, grad_gain_one = norm_backward(
        grad_normed_one, x_full[:own].astype(F32), gain_one_f
    )
    grad_input = exchange_out(grad_resid + grad_norm_one)

    in_a, in_b, out_a, out_b = rest_call(normed_one, qkv_low, attended, resid_low)
    rest = in_a.astype(F32) + swap_rows(in_b).astype(F32)
    grad_wout = out_a.astype(F32) + swap_rows(out_b).astype(F32)
    grad_wout = jnp.concatenate(halves(grad_wout), axis=0)
    rest = jnp.concatenate([grad_wout, rest], axis=1).astype(BF16)
    rest = scatter_dp(rest, "x", x_at, side)
    mixed_other = after(hid_other[0], grad_resid)
    terms = back_call(core, hid_own[:1], [mixed_other], kept[2:], got, 2)
    down = token_blocks(sum_cores(terms[:2], terms[2:]))
    down = scatter_col([after(v, grad_normed_one, rest) for v in down])
    output = exchange_out((resid + down).astype(BF16))

    rest = scatter_dp(rest, "z", z_at, side)
    piece_rows = rest.shape[0]

    heads = kvw // HD
    mine, sent = pack_call(grad_gain_one, grad_gain_two, grad_b_kv, grad_b_query)
    message, small = message_call(mine, swap_rows(sent), rest)
    chip = c.astype(jnp.int32).reshape(1)
    first, second = head_sum_call(chip, gather_col(message), small, rest, heads, width // HD)
    places = jnp.stack([x_at, z_at]).astype(jnp.int32)
    first, second = gather_dp(first, "z", side), gather_dp(second, "x", side)
    first, second = order_call(places, first, second)
    big_got = [swap_rows(after(v, first, output)) for v in big[2:]]
    grad_w_gate = join_call(core, big[0], big_got[0], 0, 256)
    grad_w_up = join_call(core, big[0], big_got[0], 1, 256)
    grad_w_down = join_call(core, big[1], big_got[1], 0, 256)
    first, second = after(first, big[0]), after(second, big[0])
    first, second = gather_dp(first, "x", side), gather_dp(second, "z", side)
    places = after(places, grad_w_gate, grad_w_up, grad_w_down)
    grad_wout, grad_wq, grad_wkv, one, two, bias_kv, bias_query = finish_call(
        places, first, second, qw, feat, heads
    )

    return (
        output,
        grad_input,
        one.reshape(-1),
        grad_wq,
        bias_query.reshape(-1),
        grad_wkv,
        bias_kv.reshape(-1),
        grad_wout,
        two.reshape(-1),
        grad_w_gate.T,
        grad_w_up.T,
        grad_w_down,
    )


def solution(mesh):
    return jax.shard_map(
        body,
        mesh=mesh,
        in_specs=(
            P(("dp", "col"), "row"),
            P("dp"),
            P("row"),
            P("row", "col"),
            P("col"),
            P("row", None),
            P(),
            P("col", "row"),
            P("row"),
            P("row", "col"),
            P("row", "col"),
            P("col", "row"),
            P(("dp", "col"), "row"),
        ),
        out_specs=(
            P(("dp", "col"), "row"),
            P(("dp", "col"), "row"),
            P("row"),
            P("row", "col"),
            P("col"),
            P("row", None),
            P(),
            P("col", "row"),
            P("row"),
            P("row", "col"),
            P("row", "col"),
            P("col", "row"),
        ),
        check_vma=False,
    )
```

```python
import functools

import jax
import jax.numpy as jnp
from jax import lax
from jax.experimental import pallas as pl
from jax.experimental.pallas import tpu as pltpu
from jax.sharding import PartitionSpec as P

HD = 128
SEQ_LEN = 1024
EPS = 1e-06
THETA = 1000000.0
NEG = -1e30
BF16 = jnp.bfloat16
F32 = jnp.float32
MIB = 1 << 20
SMALL_ROWS = 32
LITTLE = 1000
GRANT = 40


def dot_nn(left, right):
    return lax.dot_general(left, right, (((1,), (0,)), ((), ())), preferred_element_type=F32)


def dot_nt(left, right):
    return lax.dot_general(left, right, (((1,), (1,)), ((), ())), preferred_element_type=F32)


def dot_tn(left, right):
    return lax.dot_general(left, right, (((0,), (0,)), ((), ())), preferred_element_type=F32)


def params(mib):
    return pltpu.CompilerParams(vmem_limit_bytes=mib * MIB)


def cost(flops, nbytes):
    return pl.CostEstimate(flops=int(flops), bytes_accessed=int(nbytes), transcendentals=0)


def rope(value, cosine, sine):
    return value * cosine + pltpu.roll(value, HD // 2, 1) * sine


def qkv_kernel(cols, own, *refs):
    r_ref, refs = refs[0], refs[1:]
    xa, refs = refs[:cols], refs[cols:]
    xb, refs = refs[:cols], refs[cols:]
    gain, wa, wb, bias, cosine, sine, x_out, n_out, q_out, kv_out = refs
    feat = xa[0].shape[1]
    for j in range(cols):
        rows = pl.ds(j * own, own)
        a = xa[j][...].astype(F32)
        b = xb[j][...].astype(F32)
        total = jnp.sum(a * a, axis=1, keepdims=True) + jnp.sum(b * b, axis=1, keepdims=True)
        inverse = lax.rsqrt(total / (2 * feat) + EPS)
        x_out[rows, :feat] = xa[j][...]
        x_out[rows, feat:] = xb[j][...]
        n_out[rows, :feat] = (a * inverse * gain[:, :feat]).astype(BF16)
        n_out[rows, feat:] = (b * inverse * gain[:, feat:]).astype(BF16)
    qkv = dot_nn(n_out[:, :feat], wa[...]) + dot_nn(n_out[:, feat:], wb[...]) + bias[...]
    qw = q_out.shape[1]
    for h in range(qw // HD):
        at = slice(h * HD, (h + 1) * HD)
        q_out[:, at] = rope(qkv[:, at], cosine[...], sine[...]).astype(BF16)
    kv_out[:, :HD] = rope(qkv[:, qw : qw + HD], cosine[...], sine[...]).astype(BF16)
    kv_out[:, HD:] = qkv[:, qw + HD :].astype(BF16)


def qkv_call(r, xa, xb, gain, wa, wb, bias, cosine, sine, qw, own):
    cols = len(xa)
    feat = xa[0].shape[1]
    tokens = own * cols
    whole = lambda v: pl.BlockSpec(v.shape, lambda i, r: (0,) * v.ndim)
    rest = [gain, wa, wb, bias, cosine, sine]
    outs = [
        jax.ShapeDtypeStruct((tokens, 2 * feat), BF16),
        jax.ShapeDtypeStruct((tokens, 2 * feat), BF16),
        jax.ShapeDtypeStruct((tokens, qw), BF16),
        jax.ShapeDtypeStruct((tokens, 2 * HD), BF16),
    ]
    return pl.pallas_call(
        functools.partial(qkv_kernel, cols, own),
        grid_spec=pltpu.PrefetchScalarGridSpec(
            num_scalar_prefetch=1,
            grid=(1,),
            in_specs=[pl.BlockSpec((own, feat), lambda i, r: (r[0], 0))] * (2 * cols)
            + [whole(v) for v in rest],
            out_specs=[whole(o) for o in outs],
        ),
        out_shape=outs,
        compiler_params=params(40),
        cost_estimate=cost(LITTLE, LITTLE),
        name="qkv",
    )(r, *xa, *xb, *rest)


def softmax(q, k, visible, scaling):
    scores = jnp.where(visible, dot_nt(q, k) * scaling, NEG)
    e = jnp.exp(scores - jnp.max(scores, axis=1, keepdims=True))
    return e * (1.0 / jnp.sum(e, axis=1, keepdims=True))


def visibility(qpos, kpos, prefix_ref):
    return (kpos <= qpos) | (kpos < prefix_ref[0])


def attend_kernel(scaling, prefix, q, kv_a, kv_b, qpos, kpos, out):
    visible = visibility(qpos[...], kpos[...], prefix)
    keys = jnp.concatenate([kv_a[:, :HD], kv_b[:, :HD]], axis=0)
    values = jnp.concatenate([kv_a[:, HD:], kv_b[:, HD:]], axis=0)
    for h in range(q.shape[1] // HD):
        at = slice(h * HD, (h + 1) * HD)
        weights = softmax(q[:, at], keys, visible, scaling)
        out[:, at] = dot_nn(weights.astype(BF16), values).astype(BF16)


def attend_call(prefix, q, kv_a, kv_b, qpos, kpos, block):
    tokens, qw = q.shape
    whole = lambda v: pl.BlockSpec(v.shape, lambda i, p: (0,) * v.ndim)
    part = lambda v: pl.BlockSpec((block, v.shape[1]), lambda i, p: (i, 0))
    return pl.pallas_call(
        functools.partial(attend_kernel, HD**-0.5),
        grid_spec=pltpu.PrefetchScalarGridSpec(
            num_scalar_prefetch=1,
            grid=(tokens // block,),
            in_specs=[part(q), whole(kv_a), whole(kv_b), part(qpos), whole(kpos)],
            out_specs=part(q),
        ),
        out_shape=jax.ShapeDtypeStruct(q.shape, BF16),
        compiler_params=params(32),
        cost_estimate=cost(LITTLE, LITTLE),
        name="attend",
    )(prefix, q, kv_a, kv_b, qpos, kpos)


def out_kernel(cols, own, *refs):
    att, refs = refs[:cols], refs[cols:]
    wa, refs = refs[:cols], refs[cols:]
    wb, refs = refs[:cols], refs[cols:]
    xa, xb, gain, resid_out, na, nb, acc_a, acc_b = refs
    step, steps = pl.program_id(0), pl.num_programs(0)
    chunk = xa.shape[1]
    feat = chunk * steps

    rolled = []
    for j in range(cols):
        tiles = [att[j][((i - j) % cols) * own : ((i - j) % cols + 1) * own, :] for i in range(cols)]
        rolled.append(jnp.concatenate(tiles, axis=0))
    at = pl.ds(pl.multiple_of(step * chunk, 128), chunk)
    for x, w, acc in ((xa, wa, acc_a), (xb, wb, acc_b)):
        total = x[...].astype(F32)
        for j in range(cols):
            total = total + dot_nn(rolled[j], w[j][...])
        acc[:, at] = total

    @pl.when(step == steps - 1)
    def _():
        a, b = acc_a[...], acc_b[...]
        total = jnp.sum(a * a, axis=1, keepdims=True) + jnp.sum(b * b, axis=1, keepdims=True)
        inverse = lax.rsqrt(total / (2 * feat) + EPS)
        na[...] = (a * inverse * gain[:, :feat]).astype(BF16)
        nb[...] = (b * inverse * gain[:, feat:]).astype(BF16)
        resid_out[:, :feat] = acc_a[:own, :]
        resid_out[:, feat:] = acc_b[:own, :]


def out_call(att, wa, wb, x, gain, own):
    cols = len(att)
    tokens, qw = att[0].shape
    feat = wa[0].shape[1]
    steps = 3
    chunk = feat // steps
    whole = lambda v: pl.BlockSpec(v.shape, lambda i: (0,) * v.ndim)
    outs = [
        jax.ShapeDtypeStruct((own, 2 * feat), F32),
        jax.ShapeDtypeStruct((tokens, feat), BF16),
        jax.ShapeDtypeStruct((tokens, feat), BF16),
    ]
    return pl.pallas_call(
        functools.partial(out_kernel, cols, own),
        grid=(steps,),
        in_specs=[whole(a) for a in att]
        + [pl.BlockSpec((qw, chunk), lambda i: (0, i))] * (2 * cols)
        + [
            pl.BlockSpec((tokens, chunk), lambda i: (0, i)),
            pl.BlockSpec((tokens, chunk), lambda i: (0, steps + i)),
            whole(gain),
        ],
        out_specs=[whole(o) for o in outs],
        out_shape=outs,
        scratch_shapes=[pltpu.VMEM((tokens, feat), F32)] * 2,
        compiler_params=params(40),
        cost_estimate=cost(LITTLE, LITTLE),
        name="out_norm",
    )(*att, *wa, *wb, x, x, gain)


def assemble_kernel(cols, meta, ca, cb, out_a, out_b):
    rows = ca.shape[0] // cols
    own = rows // 2
    tokens = cols * own
    r, c = meta[0], meta[1]
    for j in range(cols):
        at = lax.rem(c + j, cols) * rows
        for src, out in ((ca, out_a), (cb, out_b)):
            out[j * own : (j + 1) * own, :] = src[pl.ds(at + r * own, own), :]
            out[tokens + j * own : tokens + (j + 1) * own, :] = src[
                pl.ds(at + (1 - r) * own, own), :
            ]


def assemble_call(meta, ca, cb, cols):
    out = jax.ShapeDtypeStruct(ca.shape, BF16)
    return pl.pallas_call(
        functools.partial(assemble_kernel, cols),
        in_specs=[pl.BlockSpec(memory_space=pltpu.SMEM)]
        + [pl.BlockSpec(memory_space=pltpu.VMEM)] * 2,
        out_specs=[pl.BlockSpec(memory_space=pltpu.VMEM)] * 2,
        out_shape=[out, out],
        compiler_params=params(24),
        cost_estimate=cost(LITTLE, LITTLE),
        name="assemble",
    )(meta, ca, cb)


def gated_kernel(*refs):
    acts, (ga, gb, ua, ub), outs = refs[:4], refs[4:8], refs[8:]
    for half in range(2):
        na, nb = acts[2 * half : 2 * half + 2]
        mixed, to_gate, to_up = outs[3 * half : 3 * half + 3]
        gate = dot_nt(ga[...], na[...]) + dot_nt(gb[...], nb[...])
        up = dot_nt(ua[...], na[...]) + dot_nt(ub[...], nb[...])
        s = 0.5 * jnp.tanh(0.5 * gate) + 0.5
        silu = gate * s
        mixed[...] = (silu * up).astype(BF16)
        to_gate[...] = (up * (s + silu * (1.0 - s))).astype(BF16)
        to_up[...] = silu.astype(BF16)


def hidden_grad_kernel(ca, cb, da, db, *refs):
    factors, outs = refs[:4], refs[4:]
    tokens = factors[0].shape[1]
    for half in range(2):
        rows = slice(half * tokens, (half + 1) * tokens)
        to_gate, to_up = factors[2 * half : 2 * half + 2]
        grad_gate, grad_up = outs[2 * half : 2 * half + 2]
        grad_mixed = dot_nt(da[...], ca[rows, :]) + dot_nt(db[...], cb[rows, :])
        grad_gate[...] = (grad_mixed * to_gate[...].astype(F32)).astype(BF16)
        grad_up[...] = (grad_mixed * to_up[...].astype(F32)).astype(BF16)


def gated_call(r, acts, kept, got, chunk):
    tokens, feat = acts[0].shape
    part = got.shape[1]
    steps = part // chunk
    act = pl.BlockSpec((tokens, feat), lambda i, r: (0, 0))
    mine = pl.BlockSpec((chunk, feat), lambda i, r: (r[0] * steps + i, 0))
    other = lambda k: pl.BlockSpec((None, chunk, feat), lambda i, r: (k, i, 0))
    return pl.pallas_call(
        lambda r, *refs: gated_kernel(*refs),
        grid_spec=pltpu.PrefetchScalarGridSpec(
            num_scalar_prefetch=1,
            grid=(steps,),
            in_specs=[act] * 4 + [mine, other(0), mine, other(1)],
            out_specs=[pl.BlockSpec((chunk, tokens), lambda i, r: (i, 0))] * 6,
        ),
        out_shape=[jax.ShapeDtypeStruct((part, tokens), BF16)] * 6,
        compiler_params=params(GRANT),
        cost_estimate=cost(LITTLE, LITTLE),
        name="gated",
    )(r, *acts, kept[0], got, kept[1], got)


def hidden_grad_call(r, ca, cb, kept, got, factors, chunk):
    part, tokens = factors[0].shape
    feat = ca.shape[1]
    steps = part // chunk
    cot = pl.BlockSpec(ca.shape, lambda i, r: (0, 0))
    hid = pl.BlockSpec((chunk, tokens), lambda i, r: (i, 0))
    return pl.pallas_call(
        lambda r, *refs: hidden_grad_kernel(*refs),
        grid_spec=pltpu.PrefetchScalarGridSpec(
            num_scalar_prefetch=1,
            grid=(steps,),
            in_specs=[
                cot,
                cot,
                pl.BlockSpec((chunk, feat), lambda i, r: (r[0] * steps + i, 0)),
                pl.BlockSpec((None, chunk, feat), lambda i, r: (2, i, 0)),
            ]
            + [hid] * 4,
            out_specs=[hid] * 4,
        ),
        out_shape=[jax.ShapeDtypeStruct((part, tokens), BF16)] * 4,
        compiler_params=params(GRANT),
        cost_estimate=cost(LITTLE, LITTLE),
        name="hidden_grads",
    )(r, ca, cb, kept[2], got, *factors)


def wgrad_kernel(pairs, *refs):
    acts, refs = refs[:4], refs[4:]
    own, other, outs = refs[:pairs], refs[pairs : 2 * pairs], refs[2 * pairs :]
    for side, out in enumerate(outs):
        for k in range(pairs):
            total = dot_nn(own[k][...], acts[2 * side][...])
            total = total + dot_nn(other[k][...], acts[2 * side + 1][...])
            out[k] = total.astype(BF16)


def wgrad_call(acts, other_block, hidden_own, hidden_other, chunk):
    pairs = len(hidden_own)
    part, tokens = hidden_own[0].shape
    feat = acts[0].shape[1]
    hid = pl.BlockSpec((chunk, tokens), lambda i: (i, 0))
    act = lambda block: pl.BlockSpec((tokens, feat), lambda i: (block, 0))
    return pl.pallas_call(
        functools.partial(wgrad_kernel, pairs),
        grid=(part // chunk,),
        in_specs=[act(0), act(other_block)] * 2 + [hid] * (2 * pairs),
        out_specs=[pl.BlockSpec((pairs, chunk, feat), lambda i: (0, i, 0))] * 2,
        out_shape=[jax.ShapeDtypeStruct((pairs, part, feat), BF16)] * 2,
        compiler_params=params(GRANT),
        cost_estimate=cost(LITTLE, LITTLE),
        name="weight_grads",
    )(*acts, *hidden_own, *hidden_other)


def back_kernel(pairs, *refs):
    hidden, refs = (refs[:pairs], refs[pairs : 2 * pairs]), refs[2 * pairs :]
    wa, refs = refs[:pairs], refs[pairs:]
    wb, outs = refs[:pairs], refs[pairs:]
    for half in (1, 0):
        for w, out in ((wa, outs[2 * half]), (wb, outs[2 * half + 1])):
            total = dot_tn(hidden[half][0][...], w[0][...])
            for i in range(1, pairs):
                total = total + dot_tn(hidden[half][i][...], w[i][...])
            out[...] = total.astype(out.dtype)


def back_call(r, own, other, kept, got, first):
    pairs = len(own)
    part, tokens = own[0].shape
    feat = got.shape[2]
    out = jax.ShapeDtypeStruct((tokens, feat), BF16)
    of_other = lambda k: pl.BlockSpec((None, part, feat), lambda i, r: (first + k, 0, 0))
    return pl.pallas_call(
        lambda r, *refs: back_kernel(pairs, *refs),
        grid_spec=pltpu.PrefetchScalarGridSpec(
            num_scalar_prefetch=1,
            grid=(1,),
            in_specs=[pl.BlockSpec((part, tokens), lambda i, r: (0, 0))] * (2 * pairs)
            + [pl.BlockSpec((part, feat), lambda i, r: (r[0], 0))] * pairs
            + [of_other(k) for k in range(pairs)],
            out_specs=[pl.BlockSpec((tokens, feat), lambda i, r: (0, 0))] * 4,
        ),
        out_shape=[out] * 4,
        compiler_params=params(GRANT),
        cost_estimate=cost(LITTLE, LITTLE),
        name="back_in",
    )(r, *own, *other, *kept, *([got] * pairs))


def attend_back_kernel(
    scaling, own, prefix, *refs
):
    (gr, wa, wb, q, kv_a, kv_b, qpos, kpos, cosine, sine,
     low_out, sum_out, gkv_own, gkv_send, gk, gv, ga_s) = refs
    step, steps = pl.program_id(0), pl.num_programs(0)
    feat = wa.shape[1]
    visible = visibility(qpos[...], kpos[...], prefix)
    keys = jnp.concatenate([kv_a[:, :HD], kv_b[:, :HD]], axis=0)
    values = jnp.concatenate([kv_a[:, HD:], kv_b[:, HD:]], axis=0)
    ga_s[...] = (dot_nt(gr[:, :feat], wa[...]) + dot_nt(gr[:, feat:], wb[...])).astype(BF16)

    @pl.when(step == 0)
    def _():
        gk[...] = jnp.zeros_like(gk)
        gv[...] = jnp.zeros_like(gv)
        sum_out[...] = jnp.zeros_like(sum_out)

    for h in range(q.shape[1] // HD):
        at = slice(h * HD, (h + 1) * HD)
        weights = softmax(q[:, at], keys, visible, scaling)
        grad_att = ga_s[:, at]
        gw = dot_nt(grad_att, values)
        inner = jnp.sum(weights * gw, axis=1, keepdims=True)
        gs = (weights * (gw - inner)).astype(BF16)
        gk[...] += dot_tn(gs, q[:, at])
        gv[...] += dot_tn(weights.astype(BF16), grad_att)
        grad_q = dot_nn(gs, keys) * scaling
        grad_q = rope(grad_q, cosine[...], sine[...])
        low_out[:, at] = grad_q.astype(BF16)
        sum_out[:, at] += jnp.sum(grad_q, axis=0, keepdims=True)

    @pl.when(step == steps - 1)
    def _():
        half = gk.shape[0] // 2
        gkv_own[:, :HD] = gk[:half, :] * scaling
        gkv_own[:, HD:] = gv[:half, :]
        gkv_send[:, :HD] = (gk[half:, :] * scaling).astype(BF16)
        gkv_send[:, HD:] = gv[half:, :].astype(BF16)


def attend_back_call(prefix, gr, wa, wb, q, kv_a, kv_b, qpos, kpos, cosine, sine, block):
    tokens, qw = q.shape
    whole = lambda v: pl.BlockSpec(v.shape, lambda i, p: (0,) * v.ndim)
    part = lambda v: pl.BlockSpec((block, v.shape[1]), lambda i, p: (i, 0))
    outs = [
        jax.ShapeDtypeStruct((tokens, qw), BF16),
        jax.ShapeDtypeStruct((1, qw), F32),
        jax.ShapeDtypeStruct((tokens, 2 * HD), F32),
        jax.ShapeDtypeStruct((tokens, 2 * HD), BF16),
    ]
    keys = 2 * tokens
    return pl.pallas_call(
        functools.partial(attend_back_kernel, HD**-0.5, block),
        grid_spec=pltpu.PrefetchScalarGridSpec(
            num_scalar_prefetch=1,
            grid=(tokens // block,),
            in_specs=[
                part(gr), whole(wa), whole(wb), part(q), whole(kv_a), whole(kv_b),
                part(qpos), whole(kpos), part(cosine), part(sine),
            ],
            out_specs=[part(outs[0]), whole(outs[1]), whole(outs[2]), whole(outs[3])],
            scratch_shapes=[
                pltpu.VMEM((keys, HD), F32),
                pltpu.VMEM((keys, HD), F32),
                pltpu.VMEM((block, qw), BF16),
            ],
        ),
        out_shape=outs,
        compiler_params=params(40),
        cost_estimate=cost(LITTLE, LITTLE),
        name="attend_back",
    )(prefix, gr, wa, wb, q, kv_a, kv_b, qpos, kpos, cosine, sine)


def qkv_back_kernel(own, got, query_low, cosine, sine, wa, wb, low, sums, back):
    qw = query_low.shape[1]
    total = own[...] + got[...].astype(F32)
    key = rope(total[:, :HD], cosine[...], sine[...])
    value = total[:, HD:]
    sums[:, :HD] = jnp.sum(key, axis=0, keepdims=True)
    sums[:, HD:] = jnp.sum(value, axis=0, keepdims=True)
    low[:, :qw] = query_low[...]
    low[:, qw : qw + HD] = key.astype(BF16)
    low[:, qw + HD :] = value.astype(BF16)
    feat = wa.shape[0]
    back[:, :feat] = dot_nt(low[...], wa[...]).astype(BF16)
    back[:, feat:] = dot_nt(low[...], wb[...]).astype(BF16)


def qkv_back_call(own, got, query_low, cosine, sine, wa, wb):
    tokens = own.shape[0]
    feat, columns = wa.shape
    return pl.pallas_call(
        qkv_back_kernel,
        out_shape=[
            jax.ShapeDtypeStruct((tokens, columns), BF16),
            jax.ShapeDtypeStruct((1, 2 * HD), F32),
            jax.ShapeDtypeStruct((tokens, 2 * feat), BF16),
        ],
        compiler_params=params(32),
        cost_estimate=cost(LITTLE, LITTLE),
        name="qkv_back",
    )(own, got, query_low, cosine, sine, wa, wb)


def rest_kernel(n1, low, attended, grad, in_a, in_b, out_a, out_b):
    feat = n1.shape[1] // 2
    in_b[...] = dot_tn(n1[:, feat:], low[...]).astype(BF16)
    out_b[...] = dot_tn(attended[...], grad[:, feat:]).astype(BF16)
    in_a[...] = dot_tn(n1[:, :feat], low[...]).astype(BF16)
    out_a[...] = dot_tn(attended[...], grad[:, :feat]).astype(BF16)


def rest_call(n1, low, attended, grad):
    feat = n1.shape[1] // 2
    into = jax.ShapeDtypeStruct((feat, low.shape[1]), BF16)
    out = jax.ShapeDtypeStruct((attended.shape[1], feat), BF16)
    return pl.pallas_call(
        rest_kernel,
        out_shape=[into, into, out, out],
        compiler_params=params(32),
        cost_estimate=cost(LITTLE, LITTLE),
        name="rest",
    )(n1, low, attended, grad)


def join_kernel(r_ref, kept, got, out):
    part = kept.shape[0]

    @pl.when(r_ref[0] == 0)
    def _():
        out[:part, :] = kept[...].astype(F32)
        out[part:, :] = got[...].astype(F32)

    @pl.when(r_ref[0] != 0)
    def _():
        out[:part, :] = got[...].astype(F32)
        out[part:, :] = kept[...].astype(F32)


def join_call(r, kept, got, which, chunk):
    part, feat = kept.shape[1:]
    half = pl.BlockSpec((None, part, chunk), lambda i, r: (which, 0, i))
    return pl.pallas_call(
        join_kernel,
        grid_spec=pltpu.PrefetchScalarGridSpec(
            num_scalar_prefetch=1,
            grid=(feat // chunk,),
            in_specs=[half, half],
            out_specs=pl.BlockSpec((2 * part, chunk), lambda i, r: (0, i)),
        ),
        out_shape=jax.ShapeDtypeStruct((2 * part, feat), F32),
        compiler_params=params(32),
        cost_estimate=cost(LITTLE, LITTLE),
        name="join",
    )(r, kept, got)


def pack_kernel(one, two, bias_kv, bias_query, mine, sent):
    feat = one.shape[1] // 2
    for out, first in ((mine, 0), (sent, feat)):
        out[...] = jnp.zeros_like(out)
        at = 0
        for vector, start, size in (
            (one, first, feat),
            (two, first, feat),
            (bias_kv, 0, bias_kv.shape[1]),
            (bias_query, 0, bias_query.shape[1]),
        ):
            for k in range(size // HD):
                out[at : at + 1, :] = vector[:, start + k * HD : start + (k + 1) * HD]
                at += 1


def pack_call(one, two, bias_kv, bias_query):
    out = jax.ShapeDtypeStruct((SMALL_ROWS, HD), F32)
    return pl.pallas_call(
        pack_kernel,
        out_shape=[out, out],
        cost_estimate=cost(LITTLE, LITTLE),
        name="pack",
    )(one, two, bias_kv, bias_query)


def message_kernel(mine, got, rest, out, small):
    rows = rest.shape[0]
    total = mine[...] + got[...]
    small[...] = total
    out[:rows, :] = rest[:, rest.shape[1] - 2 * HD :]
    out[rows:, :HD] = total.astype(BF16)
    out[rows:, HD:] = jnp.zeros((SMALL_ROWS, HD), BF16)


def message_call(mine, got, rest):
    rows = rest.shape[0]
    return pl.pallas_call(
        message_kernel,
        out_shape=[
            jax.ShapeDtypeStruct((rows + SMALL_ROWS, 2 * HD), BF16),
            jax.ShapeDtypeStruct((SMALL_ROWS, HD), F32),
        ],
        cost_estimate=cost(LITTLE, LITTLE),
        name="message",
    )(mine, got, rest)


def head_sum_kernel(cols, heads, gain_rows, chip, *refs):
    messages, (small, rest, out_a, out_b, total) = refs[:cols], refs[cols:]
    rows, columns = rest.shape
    half = out_a.shape[1]
    share = cols // heads
    total[...] = jnp.zeros_like(total)
    total[:gain_rows, :] = sum(m[rows : rows + gain_rows, :HD].astype(F32) for m in messages)
    for head in range(heads):
        both = jnp.zeros((rows, 2 * HD), F32)
        bias = jnp.zeros((SMALL_ROWS, HD), F32)
        for j in range(cols):
            same = jnp.where(lax.rem(chip[0] + j, cols) // share == head, 1.0, 0.0)
            both = both + same * messages[j][:rows, :].astype(F32)
            bias = bias + same * messages[j][rows:, :HD].astype(F32)
        own_columns = columns - 2 * HD - half
        at = own_columns + head * HD
        out_b[:, at : at + HD] = both[:, :HD].astype(BF16)
        at += heads * HD
        out_b[:, at : at + HD] = both[:, HD:].astype(BF16)
        for k in range(2):
            row = gain_rows + k * heads + head
            total[row : row + 1, :] = bias[gain_rows + k : gain_rows + k + 1, :]
    queries = small[gain_rows + 2 :, :]
    first = gain_rows + 2 * heads
    total[first:, :] = queries[: SMALL_ROWS - first, :]
    out_a[:rows, :] = rest[:, :half]
    out_b[:, : columns - 2 * HD - half] = rest[:, half : columns - 2 * HD]
    out_a[rows:, :HD] = total[...].astype(BF16)
    out_a[rows:, HD:] = jnp.zeros((SMALL_ROWS, half - HD), BF16)


def head_sum_call(chip, messages, small, rest, heads, gain_rows):
    rows, columns = rest.shape
    half = (columns + 2 * HD * (heads - 1)) // 2
    vmem = pl.BlockSpec(memory_space=pltpu.VMEM)
    return pl.pallas_call(
        functools.partial(head_sum_kernel, len(messages), heads, gain_rows),
        in_specs=[pl.BlockSpec(memory_space=pltpu.SMEM)] + [vmem] * (len(messages) + 2),
        out_specs=[vmem, vmem],
        out_shape=[
            jax.ShapeDtypeStruct((rows + SMALL_ROWS, half), BF16),
            jax.ShapeDtypeStruct((rows, half), BF16),
        ],
        scratch_shapes=[pltpu.VMEM((SMALL_ROWS, HD), F32)],
        cost_estimate=cost(LITTLE, LITTLE),
        name="head_sums",
    )(chip, *messages, small, rest)


def order_kernel(side, places, *refs):
    first, second, (out_a, out_b) = refs[:side], refs[side : 2 * side], refs[2 * side :]
    rows = second[0].shape[0]
    for i in range(side):
        at = lax.rem(places[1] + i, side) * rows
        out_a[pl.ds(pl.multiple_of(at, 16), rows), :] = first[i][:rows, :]
        at = lax.rem(places[0] + i, side) * rows
        out_b[pl.ds(pl.multiple_of(at, 16), rows), :] = second[i][...]
    total = sum(v[rows:, :].astype(F32) for v in first)
    out_a[side * rows :, :] = total.astype(BF16)


def order_call(places, first, second):
    side = len(first)
    rows, half = second[0].shape
    vmem = pl.BlockSpec(memory_space=pltpu.VMEM)
    return pl.pallas_call(
        functools.partial(order_kernel, side),
        in_specs=[pl.BlockSpec(memory_space=pltpu.SMEM)] + [vmem] * (2 * side),
        out_specs=[vmem, vmem],
        out_shape=[
            jax.ShapeDtypeStruct((side * rows + SMALL_ROWS, half), BF16),
            jax.ShapeDtypeStruct((side * rows, half), BF16),
        ],
        cost_estimate=cost(LITTLE, LITTLE),
        name="order",
    )(places, *first, *second)


def finish_kernel(side, heads, places, *refs):
    first, second, outs = refs[:side], refs[side : 2 * side], refs[2 * side :]
    w_out, w_query, w_keyval, one, two, bias_kv, bias_query, total = outs
    qw = w_query.shape[1]
    block, half = second[0].shape
    rows = block // side
    count = qw // block
    for i in range(side):
        at = lax.rem(places[0] + i, side)
        place = pl.ds(pl.multiple_of(at * block, 16), block)
        w_query[place, : half - qw] = first[i][:block, qw:].astype(F32)
        values = first[i][:block, :qw].astype(F32)

        @pl.when(at < count)
        def _():
            w_out[pl.ds(pl.multiple_of(at * block, 16), block), :qw] = values

        @pl.when(at >= count)
        def _():
            w_out[pl.ds(pl.multiple_of((at - count) * block, 16), block), qw:] = values

        at = lax.rem(places[1] + i, side)
        for k in range(side):
            place = pl.ds(pl.multiple_of(k * block + at * rows, 16), rows)
            piece = second[i][k * rows : (k + 1) * rows, :].astype(F32)
            w_query[place, half - qw :] = piece[:, : 2 * qw - half]
            w_keyval[place, :] = piece[:, 2 * qw - half :]
    total[...] = sum(v[block:, :HD].astype(F32) for v in first)
    at = 0
    for out in (one, two, bias_kv, bias_query):
        out[...] = total[at : at + out.shape[0], :]
        at += out.shape[0]


def finish_call(places, first, second, qw, feat, heads):
    side = len(first)
    vmem = pl.BlockSpec(memory_space=pltpu.VMEM)
    shapes = [(qw, feat), (feat, qw), (feat, 2 * heads * HD)]
    shapes += [(feat // HD, HD), (feat // HD, HD), (2 * heads, HD), (qw // HD, HD)]
    return pl.pallas_call(
        functools.partial(finish_kernel, side, heads),
        in_specs=[pl.BlockSpec(memory_space=pltpu.SMEM)] + [vmem] * (2 * side),
        out_specs=[vmem] * len(shapes),
        out_shape=[jax.ShapeDtypeStruct(s, F32) for s in shapes],
        scratch_shapes=[pltpu.VMEM((SMALL_ROWS, HD), F32)],
        compiler_params=params(32),
        cost_estimate=cost(LITTLE, LITTLE),
        name="finish",
    )(places, *first, *second)
def after(value, *others):
    return lax.optimization_barrier((value,) + others)[0]


def swap_rows(value):
    return lax.ppermute(value, "row", [(0, 1), (1, 0)])


def from_col(value, offset):
    count = lax.axis_size("col")
    return lax.ppermute(value, "col", [((i + offset) % count, i) for i in range(count)])


def gather_col(value):
    third, first = from_col(value, -1), from_col(value, 1)
    return [value, first, from_col(value, 2), third]


def gather_col_ring(value, behind=()):
    third, first = from_col(value, -1), from_col(value, 1)
    middle = value.shape[0] // 2
    upper = from_col(after(first, *behind)[:middle], 1)
    lower = from_col(after(third, *behind)[middle:], -1)
    return [value, first, jnp.concatenate([upper, lower], axis=0), third]


def scatter_col(blocks, behind=()):
    third, first, second = (
        from_col(blocks[3], 1),
        from_col(blocks[1], -1),
        from_col(blocks[2], -2),
    )
    total = blocks[0].astype(F32)
    for part in (first, second, third):
        total = total + after(part, *behind).astype(F32)
    return total


def halves(value):
    middle = value.shape[-1] // 2
    return value[..., :middle], value[..., middle:]


def roll_blocks(value, shift, axis):
    size = value.shape[axis]
    twice = jnp.concatenate([value, value], axis=axis)
    return lax.dynamic_slice_in_dim(twice, shift, size, axis)


def shift_dp(value, along, offset, side):
    pairs = []
    for z in range(side):
        for x in range(side):
            if along == "z":
                source = ((z + offset) % side) * side + x
            else:
                source = z * side + (x + offset) % side
            pairs.append((source, z * side + x))
    return lax.ppermute(value, "dp", pairs)


def scatter_dp(value, along, at, side):
    value = jnp.pad(value, ((0, -value.shape[0] % (8 * side)), (0, 0)))
    rows = value.shape[0] // side
    block = lambda j: lax.dynamic_slice_in_dim(value, ((at + j) % side) * rows, rows, 0)
    got = [shift_dp(block(j), along, -j, side) for j in (1, side - 1, 2)]
    total = block(0).astype(F32)
    for part in got:
        total = total + part.astype(F32)
    return total.astype(BF16)


def gather_dp_ring(value, along, side):
    third, first = shift_dp(value, along, -1, side), shift_dp(value, along, 1, side)
    middle = value.shape[0] // 2
    upper = shift_dp(first[:middle], along, 1, side)
    lower = shift_dp(third[middle:], along, -1, side)
    return [value, first, jnp.concatenate([upper, lower], axis=0), third]


def gather_dp(value, along, side):
    got = {j: shift_dp(value, along, j, side) for j in (1, side - 1, 2)}
    return [value] + [got[j] for j in range(1, side)]


def body(
    layer_input,
    prefix,
    gain_one,
    w_query,
    b_query,
    w_keyval,
    b_keyval,
    w_out,
    gain_two,
    w_gate,
    w_up,
    w_down,
    cotangent,
):
    cols = lax.axis_size("col")
    groups = lax.axis_size("dp")
    side = int(round(groups**0.5))
    r = lax.axis_index("row")
    c = lax.axis_index("col")
    dp = lax.axis_index("dp")
    z_at, x_at = dp // side, dp % side
    core = r.astype(jnp.int32).reshape(1)
    rows_in, feat = layer_input.shape
    own = rows_in // 2
    tokens = own * cols
    width = 2 * feat
    qw = w_query.shape[1]
    kvw = w_keyval.shape[1] // 2
    share = cols // (kvw // HD)
    kv_head = c // share
    ff = w_gate.shape[1]
    part = ff // 2

    x_a = gather_col(layer_input)

    key_start = kv_head * HD
    w_qkv_a = jnp.concatenate(
        [
            w_query,
            lax.dynamic_slice_in_dim(w_keyval, key_start, HD, 1),
            lax.dynamic_slice_in_dim(w_keyval, kvw + key_start, HD, 1),
        ],
        axis=1,
    )
    bias = jnp.concatenate(
        [
            b_query,
            lax.dynamic_slice_in_dim(b_keyval, key_start, HD, 0),
            lax.dynamic_slice_in_dim(b_keyval, kvw + key_start, HD, 0),
        ]
    ).astype(F32)[None]
    w_qkv_b = swap_rows(w_qkv_a)
    gains_a = jnp.stack([gain_one, gain_two])
    gains = jnp.concatenate([gains_a, swap_rows(gains_a)], axis=1).astype(F32)
    gain_one_f, gain_two_f = gains[:1], gains[1:]

    kept = [w_gate.T, w_up.T, w_down]
    sent = [
        lax.dynamic_slice_in_dim(w, (1 - r) * part, part, 0)
        for w in kept
    ]
    sent = jnp.stack(sent)

    block_first = rows_in * ((c + jnp.arange(cols, dtype=jnp.int32)) % cols)
    inside = jnp.arange(own, dtype=jnp.int32)
    pos_own = ((block_first[:, None] + own * r + inside[None]) % SEQ_LEN).reshape(-1)
    pos_other = ((block_first[:, None] + own * (1 - r) + inside[None]) % SEQ_LEN).reshape(-1)
    query_pos = pos_own[:, None]
    key_pos = jnp.concatenate([pos_own, pos_other])[None, :]
    frequency = THETA ** (-jnp.arange(0, HD // 2, dtype=F32) * 2.0 / HD)
    angle = pos_own.astype(F32)[:, None] * frequency[None, :]
    cosine, sine = jnp.cos(angle), jnp.sin(angle)
    cosine = jnp.concatenate([cosine, cosine], axis=1)
    sine_to = jnp.concatenate([-sine, sine], axis=1)
    sine_back = jnp.concatenate([sine, -sine], axis=1)

    x_b = [swap_rows(v) for v in x_a]
    wo_a = gather_col_ring(after(w_out, *x_b, w_qkv_b))
    x_full, normed_one, query, kv_own = qkv_call(
        core, x_a, x_b, gain_one_f, w_qkv_a, w_qkv_b, bias, cosine, sine_to, qw, own
    )
    kv_other = swap_rows(kv_own)
    query = after(query, wo_a[1], wo_a[3])
    attended = attend_call(prefix, query, kv_own, kv_other, query_pos, key_pos, tokens)
    got = swap_rows(after(sent, attended))
    att = gather_col_ring(attended, (got,))
    wo_b = [swap_rows(v) for v in wo_a]
    c_a = lax.all_gather(after(cotangent, *att[1:]), "col", axis=0, tiled=True)
    resid, n2_a, n2_b = out_call(att, wo_a, wo_b, x_full, gain_two_f, own)
    n2_other_b, n2_other_a = swap_rows(n2_a), swap_rows(n2_b)


    acts = (after(n2_a, n2_other_a, n2_other_b), n2_b, n2_other_a, n2_other_b)
    gated = gated_call(core, acts, kept, got, part // 2)
    c_b = swap_rows(after(c_a, n2_other_a, n2_other_b))
    place = after(jnp.stack([r, c]).astype(jnp.int32), gated[0])
    cot_a, cot_b = assemble_call(place, c_a, c_b, cols)
    factors = (*gated[1:3], *gated[4:6])
    grads = hidden_grad_call(core, cot_a, cot_b, kept, got, factors, part // 2)
    hid_own = [gated[0], *grads[:2]]
    hid_other = [gated[3], *grads[2:]]

    down_a, down_b = wgrad_call(
        (cot_a, cot_a, cot_b, cot_b), 1, hid_own[:1], hid_other[:1], part // 2
    )
    into_a, into_b = wgrad_call(
        (n2_a, n2_other_a, n2_b, n2_other_b), 0, hid_own[1:], hid_other[1:], part // 2
    )
    own_grads = (into_a, down_a, into_b, down_b)
    big = lax.psum(own_grads, "dp")

    def sum_cores(own_pair, other_pair):
        from_b, from_a = swap_rows(other_pair[0]), swap_rows(other_pair[1])
        a = own_pair[0].astype(F32) + from_a.astype(F32)
        b = own_pair[1].astype(F32) + from_b.astype(F32)
        return jnp.concatenate([a, b], axis=1).astype(BF16)

    def token_blocks(value):
        return [value[j * own : (j + 1) * own] for j in range(cols)]

    back_own = [after(v, *own_grads) for v in hid_own[1:]]
    terms = back_call(core, back_own, hid_other[1:], kept[:2], got, 0)
    grad_normed_two = scatter_col(token_blocks(sum_cores(terms[:2], terms[2:])))


    def norm_backward(grad, value, gain):
        inverse = lax.rsqrt(jnp.mean(value * value, axis=1, keepdims=True) + EPS)
        unit = value * inverse
        scaled = grad * gain
        mean_term = jnp.mean(scaled * unit, axis=1, keepdims=True)
        return inverse * (scaled - unit * mean_term), jnp.sum(grad * unit, axis=0, keepdims=True)

    grad_norm_two, grad_gain_two = norm_backward(grad_normed_two, resid, gain_two_f)
    cot_full = jnp.concatenate([cot_a[:own], cot_b[:own]], axis=1).astype(F32)
    grad_resid = cot_full + grad_norm_two
    resid_blocks = gather_col(grad_resid.astype(BF16))
    resid_low = jnp.concatenate(resid_blocks, axis=0)

    query_low, grad_b_query, gkv_own, gkv_sent = attend_back_call(
        prefix, resid_low, wo_a[0], wo_b[0], query, kv_own, kv_other,
        query_pos, key_pos, cosine, sine_back, tokens,
    )
    qkv_low, grad_b_kv, back_one = qkv_back_call(
        gkv_own, swap_rows(gkv_sent), query_low, cosine, sine_back, w_qkv_a, w_qkv_b
    )
    grad_normed_one = scatter_col(token_blocks(back_one))

    def exchange_out(value):
        mine, other = halves(value)
        other = swap_rows(other)
        return jnp.where(
            r == 0,
            jnp.concatenate([mine, other], axis=0),
            jnp.concatenate([other, mine], axis=0),
        )

    grad_norm_one, grad_gain_one = norm_backward(
        grad_normed_one, x_full[:own].astype(F32), gain_one_f
    )
    grad_input = exchange_out(grad_resid + grad_norm_one)

    in_a, in_b, out_a, out_b = rest_call(normed_one, qkv_low, attended, resid_low)
    rest = in_a.astype(F32) + swap_rows(in_b).astype(F32)
    grad_wout = out_a.astype(F32) + swap_rows(out_b).astype(F32)
    grad_wout = jnp.concatenate(halves(grad_wout), axis=0)
    rest = jnp.concatenate([grad_wout, rest], axis=1).astype(BF16)
    rest = scatter_dp(rest, "x", x_at, side)
    mixed_other = after(hid_other[0], grad_resid)
    terms = back_call(core, hid_own[:1], [mixed_other], kept[2:], got, 2)
    down = token_blocks(sum_cores(terms[:2], terms[2:]))
    down = scatter_col([after(v, grad_normed_one, rest) for v in down])
    output = exchange_out((resid + down).astype(BF16))

    rest = scatter_dp(rest, "z", z_at, side)
    piece_rows = rest.shape[0]

    heads = kvw // HD
    mine, sent = pack_call(grad_gain_one, grad_gain_two, grad_b_kv, grad_b_query)
    message, small = message_call(mine, swap_rows(sent), rest)
    chip = c.astype(jnp.int32).reshape(1)
    first, second = head_sum_call(chip, gather_col(message), small, rest, heads, width // HD)
    places = jnp.stack([x_at, z_at]).astype(jnp.int32)
    first, second = gather_dp(first, "z", side), gather_dp(second, "x", side)
    first, second = order_call(places, first, second)
    big_got = [swap_rows(after(v, first, output)) for v in big[2:]]
    grad_w_gate = join_call(core, big[0], big_got[0], 0, 256)
    grad_w_up = join_call(core, big[0], big_got[0], 1, 256)
    grad_w_down = join_call(core, big[1], big_got[1], 0, 256)
    first, second = after(first, big[0]), after(second, big[0])
    first, second = gather_dp(first, "x", side), gather_dp(second, "z", side)
    places = after(places, grad_w_gate, grad_w_up, grad_w_down)
    grad_wout, grad_wq, grad_wkv, one, two, bias_kv, bias_query = finish_call(
        places, first, second, qw, feat, heads
    )

    return (
        output,
        grad_input,
        one.reshape(-1),
        grad_wq,
        bias_query.reshape(-1),
        grad_wkv,
        bias_kv.reshape(-1),
        grad_wout,
        two.reshape(-1),
        grad_w_gate.T,
        grad_w_up.T,
        grad_w_down,
    )


def solution(mesh):
    return jax.shard_map(
        body,
        mesh=mesh,
        in_specs=(
            P(("dp", "col"), "row"),
            P("dp"),
            P("row"),
            P("row", "col"),
            P("col"),
            P("row", None),
            P(),
            P("col", "row"),
            P("row"),
            P("row", "col"),
            P("row", "col"),
            P("col", "row"),
            P(("dp", "col"), "row"),
        ),
        out_specs=(
            P(("dp", "col"), "row"),
            P(("dp", "col"), "row"),
            P("row"),
            P("row", "col"),
            P("col"),
            P("row", None),
            P(),
            P("col", "row"),
            P("row"),
            P("row", "col"),
            P("row", "col"),
            P("col", "row"),
        ),
        check_vma=False,
    )
```
